32 devices in a mesh: trk: 8 (over z, y), mod: 4 (over x, core).
Axes of the slice: x: 2, y: 2, z: 4, core: 2. Of those that a mesh axis runs over, the one named last changes fastest.
Arguments:
- local_deriv: float32 [5, 12, 16384], P(None, None, ('trk', 'mod')), may hold values from -6 to 6
- global_deriv: float32 [8, 12, 16384], P(None, None, ('trk', 'mod')), may hold values from -6 to 6
- measured: float32 [12, 16384], P(None, ('trk', 'mod')), may hold values from -5 to 5
- hit_weight: float32 [12, 16384], P(None, ('trk', 'mod')), may hold values from 0.25 to 4
- hit_module: int32 [12, 16384], P(None, ('trk', 'mod')), may hold values from 0 to 65535, as said below
- hit_count: int32 [16384], P(('trk', 'mod')), may hold values from 6 to 12
- track_road: int32 [16384], P(('trk', 'mod')), may hold values from 0 to 8191, as said below
- road_start: int32 [8192], P(('trk', 'mod')), may hold values from 0 to 65535, as said below
- prior_weight: float32 [65536, 8], P(('trk', 'mod')), may hold values from 0.5 to 8
Outputs:
- normal_blocks: float32 [8192, 128, 128], P(('trk', 'mod'))
- rhs: float32 [65536, 8], P(('trk', 'mod'))
- corrections: float32 [65536, 8], P(('trk', 'mod'))
The draws below stay inside these ranges and needn't reach their ends.
Inputs may be any that keep to these rules, and one draw needn't show every extreme that they name: `hit_module`: each hit slot of track t, padding too, names one of the 16 modules (road_start[track_road[t]] + k) mod 65536, k = 0 to 15; the slots of one track name different modules. `track_road`: call the device that holds road_start[r] the owner of road r. At most 64 of the 512 tracks of one device belong to roads of one owner; one owner receives exactly 64 tracks from every device. road_start[r] lies between 16 / 2 * r and 16 / 2 * r + 16 / 2 - 1.
All inputs are finite; a program needn't handle non-finite values.
Results may differ from the reference program's by a relative error of at most 0.00016.
Values sent between devices are 32-bit elements; how exact they have to be, the bound alone decides.
No kernel may reach another device: no remote copies, remote signals or barrier semaphores. Data moves between devices by JAX's collectives and lax.ppermute only.
A program may use at most 128 MiB of HBM per device.

```python
import math
import jax
import jax.numpy as jnp
from jax import lax

NPAR = 8
NLOC = 5
NHIT = 12
ROAD = 16
NMOD = 65536
TRK_DEV = 512
CAP = 64
TRACKS = 16384
NROAD = 8192
DEVICES = 32


def road_layout(key):
    spacing = ROAD // 2
    offsets = jax.random.randint(jax.random.fold_in(key, 11), (NROAD,), 0, spacing)
    road_index = jnp.arange(NROAD, dtype=jnp.int32)
    offsets = jnp.where(road_index == 0, 0, offsets)
    offsets = jnp.where(road_index == NROAD - 1, spacing - 1, offsets)
    return (spacing * road_index + offsets).astype(jnp.int32)


def track_owners(key):
    slot_total = DEVICES * CAP
    hot_rank = jax.random.permutation(jax.random.fold_in(key, 21), DEVICES)
    is_hot = hot_rank < DEVICES // 4
    slot_owner = jnp.arange(slot_total, dtype=jnp.int32) // CAP
    slot_rank = jnp.arange(slot_total, dtype=jnp.int32) % CAP
    available = jnp.where(is_hot[slot_owner], CAP, CAP // 4)
    unavailable = (slot_rank >= available).astype(jnp.int32)
    forced = (hot_rank[slot_owner] == 0).astype(jnp.int32)

    def shuffle_slots(one_key):
        return jax.random.permutation(one_key, slot_total)

    def shuffle_tracks(one_key):
        return jax.random.permutation(one_key, TRK_DEV)
    shuffled = jax.vmap(shuffle_slots)(jax.random.split(jax.random.fold_in(key, 23), DEVICES))
    scores = shuffled + slot_total * (1 + unavailable - forced)[None, :]
    chosen = jnp.argsort(scores, axis=1, stable=True)[:, :TRK_DEV]
    track_order = jax.vmap(shuffle_tracks)(jax.random.split(jax.random.fold_in(key, 24), DEVICES))
    chosen = jnp.take_along_axis(chosen, track_order, axis=1)
    owner_dev = chosen // CAP
    road_dev = NROAD // DEVICES
    local_road = jax.random.randint(jax.random.fold_in(key, 25), (DEVICES, TRK_DEV), 0, road_dev)
    return (owner_dev * road_dev + local_road).reshape(-1).astype(jnp.int32)


def hit_layout(key):
    starts = road_layout(key)
    road_ids = track_owners(key)
    scores = jax.random.randint(jax.random.fold_in(key, 31), (TRACKS, ROAD), 0, 1073741824)
    picked = jnp.argsort(scores, axis=1, stable=True)[:, :NHIT].astype(jnp.int32)
    modules = (starts[road_ids][:, None] + picked) % NMOD
    return (road_ids, modules.T.astype(jnp.int32))


def draw_road_start(key, part):
    return road_layout(key)


def draw_track_road(key, part):
    return hit_layout(key)[0]


def draw_hit_module(key, part):
    return hit_layout(key)[1]


def draw_measured(key, part):
    road_ids = track_owners(key)
    road_scale = 0.5 + road_ids.astype(jnp.float32) / NROAD
    values = jax.random.normal(jax.random.fold_in(key, 43), (NHIT, TRACKS), jnp.float32) * road_scale[None, :]
    return jnp.clip(values, -5.0, 5.0).astype(jnp.float32)


def plant(drawn, rng, smallest, largest):
    longest = drawn.shape.index(max(drawn.shape))
    spots = []
    for shift in (0, 1):
        where = [jax.random.randint(jax.random.fold_in(rng, axis), (), 0, length) for axis, length in enumerate(drawn.shape)]
        where[longest] = (where[longest] + shift) % drawn.shape[longest]
        spots.append(tuple(where))
    return drawn.at[spots[0]].set(smallest).at[spots[1]].set(largest)


def shard_levels(own_key, dims, shards, smallest, largest):
    def one(axis_at, parts):
        steps = jax.random.uniform(jax.random.fold_in(jax.random.fold_in(own_key, 6), axis_at), (parts,), jnp.float32, smallest / len(shards), largest / len(shards))
        return jnp.repeat(jnp.exp(steps), dims[axis_at] // parts).reshape((-1,) + (1,) * (len(dims) - axis_at - 1))

    gain = one(*shards[0])
    for cut in shards[1:]:
        gain = gain * one(*cut)
    return gain


def noise(key, shape, scale, most, cuts=(), kind=jnp.bfloat16):
    level = shard_levels(key, shape, cuts, -0.22, 0.18) if cuts else 1.0
    values = jax.random.normal(key, shape, jnp.float32) * scale * level
    return jnp.minimum(jnp.maximum(values, -most), most).astype(kind)


def setup_inputs(seed: int = 0) -> dict:
    seeds = jax.random.split(jax.random.key(seed), 10)
    local_deriv = noise(seeds[0], (NLOC, NHIT, TRACKS), 1.0, 6.0, ((2, 32),), jnp.float32)
    global_deriv = noise(seeds[1], (NPAR, NHIT, TRACKS), 1.0, 6.0, ((2, 32),), jnp.float32)
    measured = draw_measured(jax.random.fold_in(seeds[9], 71), 0)
    hit_weight = jnp.clip(jnp.exp(math.log(4.0) - 2.7725887 * jax.random.uniform(seeds[3], (NHIT, TRACKS), jnp.float32) ** shard_levels(seeds[3], (NHIT, TRACKS), ((1, 32),), -0.2, 0.2)), 0.25, 4.0)
    hit_module = draw_hit_module(jax.random.fold_in(seeds[9], 71), 0)
    hit_count = plant(jax.random.randint(seeds[5], (TRACKS,), 6, NHIT + 1), jax.random.fold_in(seeds[5], 1), 6, NHIT).astype(jnp.int32)
    track_road = draw_track_road(jax.random.fold_in(seeds[9], 71), 0)
    road_start = draw_road_start(jax.random.fold_in(seeds[9], 71), 0)
    prior_weight = jnp.clip(jnp.exp(math.log(8.0) - 2.7725887 * jax.random.uniform(seeds[8], (NMOD, NPAR), jnp.float32) ** shard_levels(seeds[8], (NMOD, NPAR), ((0, 32),), -0.2, 0.2)), 0.5, 8.0)
    return {"local_deriv": local_deriv, "global_deriv": global_deriv, "measured": measured, "hit_weight": hit_weight, "hit_module": hit_module, "hit_count": hit_count, "track_road": track_road, "road_start": road_start, "prior_weight": prior_weight}


EPS = 1e-06
HIGHEST = lax.Precision.HIGHEST

def local_fit(local_deriv, measured, hit_weight, hit_count):
    nlocal = local_deriv.shape[0]
    hit_slots = local_deriv.shape[1]
    position = lax.broadcasted_iota(jnp.int32, hit_weight.shape, 0)
    weight = jnp.where(position < hit_count[None, :], hit_weight, jnp.zeros_like(hit_weight))
    weighted = local_deriv * weight[None]
    local_gram = lax.optimization_barrier(jnp.sum(weighted[:, None] * local_deriv[None, :], axis=2))
    factor = {}
    for row_num in range(nlocal):
        for col_num in range(row_num + 1):
            running = local_gram[row_num, col_num]
            if row_num == col_num:
                running = running + 1.0
            for inner_num in range(col_num):
                running = running - factor[row_num, inner_num] * factor[col_num, inner_num]
            if row_num == col_num:
                factor[row_num, col_num] = jnp.sqrt(running)
            else:
                factor[row_num, col_num] = running / factor[col_num, col_num]
    solved_rows = []
    for row_num in range(nlocal):
        running = weighted[row_num]
        for col_num in range(row_num):
            running = running - factor[row_num, col_num][None] * solved_rows[col_num]
        solved_rows.append(running / factor[row_num, row_num][None])
    projected = jnp.stack(solved_rows)
    diagonal = jnp.eye(hit_slots, dtype=jnp.float32)[:, :, None] * weight[None]
    schur_block = diagonal - lax.optimization_barrier(jnp.sum(projected[:, :, None] * projected[:, None, :], axis=0))
    solved = lax.optimization_barrier(jnp.sum(schur_block * measured[None], axis=1))
    return (schur_block, solved)

def pair_blocks(global_rows, schur_rows):
    scaled_pairs = schur_rows[:, :, :, None] * global_rows[:, None, :, :]
    return global_rows[:, :, None, :, None] * scaled_pairs[:, :, :, None, :]

def minres_finish(beta_one, alpha_one, beta_two, alpha_two, beta_three, lanczos_one, lanczos_two):
    entry_first = alpha_one * alpha_one + beta_two * beta_two
    entry_cross = beta_two * (alpha_one + alpha_two)
    entry_second = beta_two * beta_two + alpha_two * alpha_two + beta_three * beta_three
    determinant = entry_first * entry_second - entry_cross * entry_cross
    coef_one = beta_one * (entry_second * alpha_one - entry_cross * beta_two) / determinant
    coef_two = beta_one * (entry_first * beta_two - entry_cross * alpha_one) / determinant
    return coef_one * lanczos_one + coef_two * lanczos_two

def apply_normal(vector, normal_blocks, gather_index, prior_weight):
    pieces = vector[gather_index].reshape(gather_index.shape[0], -1)
    mapped = jnp.einsum('rab,rb->ra', normal_blocks, pieces, precision=HIGHEST)
    spread = jnp.zeros_like(vector).at[gather_index.reshape(-1)].add(mapped.reshape(-1, vector.shape[1]))
    return prior_weight * vector + spread

def reference(local_deriv, global_deriv, measured, hit_weight, hit_module, hit_count, track_road, road_start, prior_weight):
    schur_block, solved = local_fit(local_deriv, measured, hit_weight, hit_count)
    slot_num = (hit_module - road_start[track_road][None, :]) % NMOD
    global_rows = jnp.transpose(global_deriv, (2, 1, 0))
    schur_rows = jnp.transpose(schur_block, (2, 0, 1))
    slot_rows = slot_num.T
    pair_index = track_road[:, None, None] * (ROAD * ROAD) + slot_rows[:, :, None] * ROAD + slot_rows[:, None, :]
    block_count = 16
    rows_each = TRACKS // block_count

    def accumulate(blocks, pieces):
        part_global, part_schur, part_index = pieces
        contrib = pair_blocks(part_global, part_schur).reshape(-1, NPAR, NPAR)
        return (blocks.at[part_index.reshape(-1)].add(contrib), None)
    start_blocks = jnp.zeros((NROAD * ROAD * ROAD, NPAR, NPAR), jnp.float32)
    blocks, unused = lax.scan(accumulate, start_blocks, (global_rows.reshape(block_count, rows_each, NHIT, NPAR), schur_rows.reshape(block_count, rows_each, NHIT, NHIT), pair_index.reshape(block_count, rows_each, NHIT, NHIT)))
    normal_blocks = blocks.reshape(NROAD, ROAD, ROAD, NPAR, NPAR).transpose(0, 1, 3, 2, 4).reshape(NROAD, ROAD * NPAR, ROAD * NPAR)
    rhs = jnp.zeros((NMOD, NPAR), jnp.float32).at[hit_module.T.reshape(-1)].add((global_rows * solved.T[:, :, None]).reshape(-1, NPAR))
    gather_index = (road_start[:, None] + jnp.arange(ROAD, dtype=jnp.int32)[None, :]) % NMOD

    def apply_here(vector):
        return apply_normal(vector, normal_blocks, gather_index, prior_weight)
    beta_one = jnp.sqrt(jnp.sum(rhs * rhs) + EPS)
    lanczos_one = rhs / beta_one
    mapped = apply_here(lanczos_one)
    alpha_one = jnp.sum(lanczos_one * mapped)
    residue = mapped - alpha_one * lanczos_one
    beta_two = jnp.sqrt(jnp.sum(residue * residue) + EPS)
    lanczos_two = residue / beta_two
    mapped = apply_here(lanczos_two) - beta_two * lanczos_one
    alpha_two = jnp.sum(lanczos_two * mapped)
    residue = mapped - alpha_two * lanczos_two
    beta_three = jnp.sqrt(jnp.sum(residue * residue) + EPS)
    corrections = minres_finish(beta_one, alpha_one, beta_two, alpha_two, beta_three, lanczos_one, lanczos_two)
    return (normal_blocks, rhs, corrections)
```

```python
import functools

import jax
import jax.numpy as jnp
from jax import lax
from jax.experimental import pallas as pl
from jax.experimental.pallas import tpu as pltpu
from jax.sharding import PartitionSpec as P

NPAR = 8
NHIT = 12
NLOC = 5
ROAD = 16
LANES = 128
EPS = 1e-06
AXES = ("trk", "mod")

W_SOLVED = NHIT * NPAR
W_SLOT = W_SOLVED + NHIT
W_ROAD = W_SLOT + NHIT
W_PROJ0 = W_ROAD + 1
W_PROJ1 = W_PROJ0 + 1
W_PROJ = W_PROJ1 + 2
WORDS = W_PROJ + NLOC * (NHIT - 2)

PER_ITEM = 8
UNROLL = 4
GROUPS = 8
F32 = jnp.float32
BF16 = jnp.bfloat16


def iota(shape, dim):
    return lax.broadcasted_iota(jnp.int32, shape, dim)


def dot(lhs, rhs, lhs_dim, rhs_dim):
    return lax.dot_general(
        lhs, rhs, (((lhs_dim,), (rhs_dim,)), ((), ())), preferred_element_type=F32
    )


def split_three(value):
    high = value.astype(BF16)
    rest = value - high.astype(F32)
    middle = rest.astype(BF16)
    low = (rest - middle.astype(F32)).astype(BF16)
    return high, middle, low


def householder(rows, first, column):
    vector = [row[column : column + 1] for row in rows[first:]]
    norm = jnp.sqrt(sum(part * part for part in vector))
    vector[0] = vector[0] + jnp.where(vector[0] >= 0.0, norm, -norm)
    square = sum(part * part for part in vector)
    scale = jnp.where(square > 1e-30, 2.0 / jnp.maximum(square, 1e-30), 0.0)
    along = sum(part * row for part, row in zip(vector, rows[first:])) * scale
    return rows[:first] + [row - part * along for part, row in zip(vector, rows[first:])]


def send_kernel(
    cap, road_dev, rows_each, ld_ref, gd_ref, me_ref, hw_ref, hm_ref, hc_ref, tr_ref, trc_ref,
    out_ref, words_ref, parts_ref,
):
    tracks = hc_ref.shape[1]
    split = LANES // cap
    words_all = rows_each * split
    weight = jnp.where(iota((NHIT, tracks), 0) < hc_ref[...], hw_ref[...], 0.0)
    root = jnp.sqrt(weight)
    scaled = [ld_ref[a] * root for a in range(NLOC)]
    factor = {}
    for a in range(NLOC):
        for b in range(a + 1):
            running = jnp.sum(scaled[a] * scaled[b], axis=0, keepdims=True)
            if a == b:
                running = running + 1.0
            for c in range(b):
                running = running - factor[a, c] * factor[b, c]
            factor[a, b] = jnp.sqrt(running) if a == b else running / factor[b, b]
    proj = []
    for a in range(NLOC):
        running = scaled[a]
        for b in range(a):
            running = running - factor[a, b] * proj[b]
        proj.append(running / factor[a, a])
    residual = me_ref[...] * root
    solved = residual
    for a in range(NLOC):
        solved = solved - proj[a] * jnp.sum(proj[a] * residual, axis=0, keepdims=True)
    proj = householder(proj, 0, 0)
    proj = householder(proj, 1, 1)
    for i in range(NHIT):
        words_ref[i * NPAR : (i + 1) * NPAR, :] = gd_ref[:, i, :] * root[i : i + 1]
    words_ref[W_SOLVED:W_SLOT, :] = solved
    words_ref[W_SLOT:W_ROAD, :] = (hm_ref[...] & (ROAD - 1)).astype(F32)
    owner = tr_ref[...] // road_dev
    words_ref[W_ROAD:W_PROJ0, :] = (tr_ref[...] - owner * road_dev + 1).astype(F32)
    words_ref[W_PROJ0:W_PROJ1, :] = proj[0][0:1]
    words_ref[W_PROJ1 : W_PROJ1 + 1, :] = proj[0][1:2]
    words_ref[W_PROJ1 + 1 : W_PROJ, :] = proj[1][1:2]
    for a in range(NLOC):
        at = W_PROJ + a * (NHIT - 2)
        words_ref[at : at + NHIT - 2, :] = proj[a][2:]
    words_ref[WORDS:, :] = jnp.zeros((words_all - WORDS, tracks), F32)
    for num, part in enumerate(split_three(words_ref[...])):
        parts_ref[num * words_all : (num + 1) * words_all, :] = part
    owner_col = trc_ref[...] // road_dev
    earlier = iota((tracks, tracks), 0) < iota((tracks, tracks), 1)
    same = jnp.where(jnp.logical_and(owner_col == owner, earlier), 1.0, 0.0)
    rank = jnp.sum(same, axis=0, keepdims=True).astype(jnp.int32)
    target = owner * cap + rank
    blocks = out_ref.shape[0] // split
    lane_part = iota((rows_each, LANES), 1) // cap
    per = 2
    for pair in range(blocks // per):
        hot = jnp.where(
            target == iota((per * LANES, tracks), 0) + pair * per * LANES, 1.0, 0.0
        ).astype(BF16)
        moved = dot(parts_ref[...], hot, 1, 1)
        moved = moved[:words_all] + moved[words_all : 2 * words_all] + moved[2 * words_all :]
        for sub in range(per):
            block = moved[:, sub * LANES : (sub + 1) * LANES]
            for k in range(split):
                made = None
                for m in range(split):
                    piece = block[m * rows_each : (m + 1) * rows_each]
                    if m != k:
                        piece = pltpu.roll(piece, (cap * (m - k)) % LANES, 1)
                    made = piece if made is None else jnp.where(lane_part == m, piece, made)
                out_ref[(pair * per + sub) * split + k] = made


def sort_kernel(cap, recv_ref, off_ref, list_ref, item_ref, bound_ref, off_out_ref, road_ref):
    split = LANES // cap
    roads = off_ref.shape[0]
    blocks = road_ref.shape[0]
    lane_part = iota((1, LANES), 1) // cap
    shift_of = road_part(cap)
    for e in range(blocks):
        made = None
        for k in range(split):
            piece = recv_ref[e * split + k, 0:1, :]
            if k != shift_of:
                piece = pltpu.roll(piece, (cap * (k - shift_of)) % LANES, 1)
            made = piece if made is None else jnp.where(lane_part == k, piece, made)
        road_ref[e : e + 1, :] = made
    road_num = (iota((roads, LANES), 0) + 1).astype(F32)
    upper = jnp.where(iota((LANES, LANES), 0) < iota((LANES, LANES), 1), 1.0, 0.0).astype(BF16)
    offset = off_ref[...]
    counts = jnp.zeros((roads, 1), F32)
    ranks = []
    for e in range(blocks):
        hot = jnp.where(road_ref[e : e + 1, :] == road_num, 1.0, 0.0)
        before = dot(hot.astype(BF16), upper, 1, 0) + counts
        ranks.append(jnp.sum(hot * before, axis=0, keepdims=True))
        off_out_ref[e : e + 1, :] = jnp.sum(hot * offset, axis=0, keepdims=True)
        counts = counts + jnp.sum(hot, axis=1, keepdims=True)
    items = jnp.maximum(jnp.floor((counts + (PER_ITEM - 1)) * (1.0 / PER_ITEM)), 1.0)
    items = jnp.broadcast_to(items, (roads, LANES))
    lower = jnp.where(iota((roads, roads), 1) < iota((roads, roads), 0), 1.0, 0.0).astype(BF16)
    begin = dot(lower, items.astype(BF16), 1, 0)
    rows = list_ref.shape[0]
    total = jnp.zeros((rows, 2 * LANES), F32)
    row_num = iota((rows, LANES), 0).astype(F32)
    lane_num = iota((LANES, LANES), 0).astype(F32)
    track_lane = iota((1, LANES), 1).astype(F32)
    for e in range(blocks):
        road = road_ref[e : e + 1, :]
        hot = jnp.where(road == road_num, 1.0, 0.0)
        place = PER_ITEM * jnp.sum(hot * begin, axis=0, keepdims=True) + ranks[e]
        place = jnp.where(road > 0.5, place, -1.0)
        high = jnp.floor(place * (1.0 / LANES))
        low = place - high * LANES
        pick = jnp.where(high == row_num, 1.0, 0.0).astype(BF16)
        match = low == lane_num
        values = jnp.concatenate(
            [jnp.where(match, float(e + 1), 0.0), jnp.where(match, track_lane, 0.0)], axis=0
        )
        total = total + dot(pick, values.astype(BF16), 1, 1)
    found = total[:, :LANES]
    track = jnp.where(found > 0.5, (found - 1.0) * LANES + total[:, LANES:], float(blocks * LANES))
    list_ref[...] = track.astype(jnp.int32)
    item_rows = item_ref.shape[0]
    for row in range(item_rows):
        item = (iota((1, LANES), 1) + row * LANES).astype(F32)
        road = jnp.sum(jnp.where(begin <= item, 1.0, 0.0), axis=0, keepdims=True) - 1.0
        first = jnp.sum(jnp.where(begin == item, 1.0, 0.0), axis=0, keepdims=True)
        item_ref[row : row + 1, :] = (2.0 * road + first).astype(jnp.int32)
    each = roads // GROUPS
    begins = jnp.where(iota((roads, LANES), 0) == iota((roads, LANES), 1) * each, begin, 0.0)
    bound = jnp.sum(begins, axis=0, keepdims=True)
    last = jnp.sum(items, axis=0, keepdims=True)
    bound = jnp.where(iota((1, LANES), 1) < GROUPS, bound, last)
    bound_ref[...] = jnp.broadcast_to(bound, bound_ref.shape).astype(jnp.int32)


def rows_of(cap):
    split = LANES // cap
    least = -(-WORDS // split)
    return -(-least // 8) * 8


def road_part(cap):
    return W_ROAD // rows_of(cap)


def blocks_kernel(
    cap, bound_ref, list_ref, item_ref, recv_ref, off_ref, out_ref, sums_ref, tiles_ref, words_ref,
    held_ref,
):
    group = pl.program_id(0)
    each = out_ref.shape[0]
    split = LANES // cap
    rows_each = recv_ref.shape[1]
    blocks = off_ref.shape[0]
    width = ROAD * NPAR

    @pl.when(group == 0)
    def _():
        lane_part = iota((rows_each, LANES), 1) // cap
        tiles_ref[blocks * LANES] = jnp.zeros((8, width), F32)

        def lay(e, carry):
            for m in range(split):
                made = None
                for k in range(split):
                    piece = recv_ref[e * split + k]
                    if k != m:
                        piece = pltpu.roll(piece, (cap * (k - m)) % LANES, 1)
                    made = piece if made is None else jnp.where(lane_part == k, piece, made)
                words_ref[m * rows_each : (m + 1) * rows_each, :] = made
            offset = off_ref[pl.ds(e, 1), :]
            slots = []
            for i in range(NHIT):
                slot = words_ref[W_SLOT + i : W_SLOT + i + 1, :] - offset
                slots.append(jnp.where(slot < 0.0, slot + ROAD, slot))
            laid = [jnp.zeros((NPAR, LANES), F32) for s in range(ROAD)]
            for i in range(NHIT):
                value = words_ref[i * NPAR : (i + 1) * NPAR, :]
                wide = jnp.broadcast_to(slots[i], (NPAR, LANES))
                for s in range(ROAD):
                    laid[s] = jnp.where(wide == float(s), value, laid[s])
            slot_num = iota((ROAD, LANES), 0).astype(F32)
            placed = [jnp.zeros((ROAD, LANES), F32) for a in range(NLOC + 1)]
            for i in range(NHIT):
                match = slots[i] == slot_num
                for a in range(NLOC + 1):
                    if a == NLOC:
                        at = W_SOLVED + i
                    elif i == 0:
                        at = W_PROJ0 if a == 0 else None
                    elif i == 1:
                        at = W_PROJ1 + a if a < 2 else None
                    else:
                        at = W_PROJ + a * (NHIT - 2) + i - 2
                    if at is not None:
                        placed[a] = jnp.where(match, words_ref[at : at + 1, :], placed[a])
            start = pl.multiple_of(e * LANES, LANES)
            for a in range(NLOC + 1):
                mixed = jnp.concatenate(
                    [laid[s] * placed[a][s : s + 1] for s in range(ROAD)], axis=0
                )
                at = a if a < NLOC else NLOC + 1
                tiles_ref[pl.ds(start, LANES), at, :] = mixed.T
            tiles_ref[pl.ds(start, LANES), NLOC, :] = jnp.concatenate(laid, axis=0).T
            tiles_ref[pl.ds(start, LANES), NLOC + 2, :] = jnp.zeros((LANES, width), F32)
            return carry

        lax.fori_loop(0, blocks, lay, 0)

    row_kind = iota((PER_ITEM * 8, width), 0) % 8
    is_proj = row_kind < NLOC
    is_own = row_kind == NLOC
    same_slot = iota((width, width), 0) // NPAR == iota((width, width), 1) // NPAR
    begin = bound_ref[0, group]
    end = bound_ref[0, group + 1]

    def step(num, carry):
        for u in range(UNROLL):
            item = begin + num * UNROLL + u
            live = item < end
            item = jnp.minimum(item, end - 1)
            info = item_ref[item // LANES, item % LANES]
            road = info // 2
            first = jnp.logical_and(info % 2 == 1, live)
            local = road - group * each
            at = item * PER_ITEM
            parts = []
            for j in range(PER_ITEM):
                track = list_ref[(at + j) // LANES, (at + j) % LANES]
                track = jnp.where(live, track, blocks * LANES)
                parts.append(tiles_ref[track])
            tall = jnp.concatenate(parts, axis=0)
            high = tall.astype(BF16)
            high32 = high.astype(F32)
            low32 = tall - high32
            low = low32.astype(BF16)
            left = jnp.concatenate([high, high, low], axis=0)
            high_p = jnp.where(is_proj, high32, 0.0).astype(BF16)
            high_o = jnp.where(is_own, high32, 0.0).astype(BF16)
            low_p = jnp.where(is_proj, low32, 0.0).astype(BF16)
            low_o = jnp.where(is_own, low32, 0.0).astype(BF16)
            right = jnp.concatenate(
                [
                    jnp.concatenate([high_p, low_p, high_p], axis=0),
                    jnp.concatenate([high_o, low_o, high_o], axis=0),
                ],
                axis=1,
            )
            both = dot(left, right, 0, 0)
            value = jnp.where(same_slot, both[:, width:], 0.0) - both[:, :width]
            out_ref[local] = value + jnp.where(first, 0.0, out_ref[local])
            added = parts[0]
            for part in parts[1:]:
                added = added + part
            held_ref[local] = added + jnp.where(first, 0.0, held_ref[local])
        return carry

    lax.fori_loop(0, (end - begin + UNROLL - 1) // UNROLL, step, 0)
    sums_ref[...] = held_ref[:, NLOC + 1, :]


def lane_bits(offset, bit):
    return (offset // (1 << bit)) % 2 == 1


def gathered(rows, offset, odd):
    lane = iota(rows.shape, 1)
    here = rows
    there = jnp.concatenate([rows[1:], jnp.zeros((1, LANES), F32)], axis=0)
    if odd:
        half = LANES // 2
        turned_here, turned_there = pltpu.roll(here, half, 1), pltpu.roll(there, half, 1)
        here = jnp.where(lane < LANES - half, turned_here, turned_there)
        there = turned_there
    for bit in range(3):
        step = NPAR << bit
        take = lane_bits(offset, bit)
        turned_here, turned_there = (
            pltpu.roll(here, LANES - step, 1),
            pltpu.roll(there, LANES - step, 1),
        )
        moved = jnp.where(lane < LANES - step, turned_here, turned_there)
        here = jnp.where(take, moved, here)
        there = jnp.where(take, turned_there, there)
    return here


def scattered(rows, offset, odd):
    lane = iota(rows.shape, 1)
    here, there = rows, jnp.zeros_like(rows)
    steps = [(NPAR << bit, bit) for bit in range(3)] + ([(LANES // 2, None)] if odd else [])
    for step, bit in steps:
        turned_here, turned_there = pltpu.roll(here, step, 1), pltpu.roll(there, step, 1)
        new_here = jnp.where(lane < step, 0.0, turned_here)
        new_there = jnp.where(lane < step, turned_here, turned_there)
        if bit is None:
            here, there = new_here, new_there
        else:
            take = lane_bits(offset, bit)
            here = jnp.where(take, new_here, here)
            there = jnp.where(take, new_there, there)
    return here, there


EDGE = 8
NEXT_ROADS = 2
PREV_ROADS = 4


def krylov_kernel(
    blocks_hbm, sums_ref, off_ref, prior_ref, from_prev_ref, from_next_ref,
    first_ref, second_ref, third_ref, dots_ref,
    held, sems, even_sum, odd_sum, even_off, odd_off, prior, even_part, odd_part, turned_even,
    turned_odd, even_out, odd_out, rows_scr,
):
    roads, width = sums_ref.shape
    half = roads // 2
    chunks = sems.shape[0]
    each = roads // chunks
    own = slice(EDGE, EDGE + half)
    total = half + 2 * EDGE
    copies = [
        pltpu.make_async_copy(
            blocks_hbm.at[pl.ds(c * each, each)], held.at[pl.ds(c * each, each)], sems.at[c]
        )
        for c in range(chunks)
    ]
    for copy in copies:
        copy.start()

    two = 2 * EDGE
    at_prev = PREV_ROADS * width
    at_next = NEXT_ROADS * width
    for parity, total_sum, total_off in ((0, even_sum, even_off), (1, odd_sum, odd_off)):
        pick = lambda ref, start, count: ref[pl.ds(start + parity, count, stride=2), :]
        total_sum[0:EDGE] = pick(from_prev_ref, at_prev, EDGE)
        total_sum[own] = pick(sums_ref, 0, half)
        total_sum[EDGE + half :] = pick(from_next_ref, at_next, EDGE)
        total_off[0:EDGE] = pick(from_prev_ref, at_prev + two, EDGE).astype(jnp.int32)
        total_off[own] = pick(off_ref, 0, half).astype(jnp.int32)
        total_off[EDGE + half :] = pick(from_next_ref, at_next + two, EDGE).astype(jnp.int32)
    prior[0:EDGE] = from_prev_ref[at_prev + 2 * two : at_prev + 2 * two + EDGE]
    prior[own] = prior_ref[...]
    prior[EDGE + half :] = from_next_ref[at_next + 2 * two : at_next + 2 * two + EDGE]

    def spread(even, odd):
        even_here, even_there = scattered(even, even_off[...], False)
        odd_here, odd_there = scattered(odd, odd_off[...], True)
        over = even_there + odd_there
        return (
            even_here
            + odd_here
            + jnp.concatenate([jnp.zeros((1, LANES), F32), over[:-1]], axis=0)
        )

    def column_product(tile_at, column):
        acc = None
        for s in range(width // 8):
            term = tile_at(s) * column[s * 8 : (s + 1) * 8]
            acc = term if acc is None else acc + term
        return acc

    def apply(vector, wait):
        even = gathered(vector, even_off[...], False)
        odd = gathered(vector, odd_off[...], True)
        even_part[...] = jnp.zeros_like(even_part)
        odd_part[...] = jnp.zeros_like(odd_part)
        edge_even = jnp.concatenate(
            [even[:EDGE], even[EDGE + half :], jnp.zeros((LANES - 2 * EDGE, LANES), F32)], axis=0
        ).T
        edge_odd = jnp.concatenate(
            [odd[:EDGE], odd[EDGE + half :], jnp.zeros((LANES - 2 * EDGE, LANES), F32)], axis=0
        ).T
        for num in range(PREV_ROADS):
            row = EDGE - PREV_ROADS // 2 + num // 2
            column = (edge_even if num % 2 == 0 else edge_odd)[:, row : row + 1]
            part = even_part if num % 2 == 0 else odd_part
            part[row] = column_product(
                lambda s, num=num: from_prev_ref[num * width + s * 8 : num * width + s * 8 + 8],
                column,
            )
        for num in range(NEXT_ROADS):
            column = (edge_even if num % 2 == 0 else edge_odd)[:, EDGE : EDGE + 1]
            part = even_part if num % 2 == 0 else odd_part
            part[EDGE + half] = column_product(
                lambda s, num=num: from_next_ref[num * width + s * 8 : num * width + s * 8 + 8],
                column,
            )
        turned_even[:, :half] = even[own].T
        turned_odd[:, :half] = odd[own].T
        per = each // 2

        def chunk(c, carry):
            if wait:
                pltpu.make_async_copy(
                    blocks_hbm.at[pl.ds(c * each, each)],
                    held.at[pl.ds(c * each, each)],
                    sems.at[c],
                ).wait()
            columns_even = turned_even[...]
            columns_odd = turned_odd[...]
            for j in range(per):
                for parity, columns, part in (
                    (0, columns_even, even_part),
                    (1, columns_odd, odd_part),
                ):
                    road = c * each + 2 * j + parity
                    part[EDGE + c * per + j] = column_product(
                        lambda s, road=road: held[road, s * 8 : s * 8 + 8, :],
                        columns[:, j : j + 1],
                    )
            turned_even[...] = pltpu.roll(columns_even, columns_even.shape[1] - per, 1)
            turned_odd[...] = pltpu.roll(columns_odd, columns_odd.shape[1] - per, 1)
            return carry

        lax.fori_loop(0, chunks, chunk, 0)
        even = even_part[:, 0, :]
        odd = odd_part[:, 0, :]
        for k in range(1, 8):
            even = even + even_part[:, k, :]
            odd = odd + odd_part[:, k, :]
        return prior[...] * vector + spread(even, odd)

    first = spread(even_sum[...], odd_sum[...])
    second = apply(first, True)
    third = apply(second, False)
    first, second, third = first[own], second[own], third[own]
    first_ref[...] = first
    second_ref[...] = second
    third_ref[...] = third
    lane = iota(dots_ref.shape, 1)
    dots = jnp.zeros(dots_ref.shape, F32)
    pairs = ((first, first), (first, second), (second, second), (second, third), (third, third))
    for num, (one, other) in enumerate(pairs):
        dots = dots + jnp.where(lane == num, jnp.sum(one * other), 0.0)
    dots_ref[...] = dots


def finish_kernel(dots_ref, first_ref, second_ref, out_ref):
    sums = jnp.sum(dots_ref[...], axis=0, keepdims=True)
    s00, s01, s11, s12, s22 = (sums[:, num : num + 1] for num in range(5))
    square_one = s00 + EPS
    beta_one = jnp.sqrt(square_one)
    alpha_one = s01 / square_one
    square_two = (s11 - 2.0 * alpha_one * s01 + alpha_one * alpha_one * s00) / square_one + EPS
    beta_two = jnp.sqrt(square_two)
    scale = 1.0 / (beta_one * beta_two)
    s02 = s11
    cross = s12 - alpha_one * s11 - square_two * s01
    cross = cross - alpha_one * (s02 - alpha_one * s01 - square_two * s00)
    alpha_two = cross * scale * scale
    near = alpha_one + alpha_two
    far = alpha_one * alpha_two - square_two
    square_three = s22 - 2.0 * near * s12 + near * near * s11
    square_three = square_three + 2.0 * far * s02 - 2.0 * near * far * s01 + far * far * s00
    square_three = square_three * scale * scale + EPS
    entry_first = alpha_one * alpha_one + square_two
    entry_cross = beta_two * near
    entry_second = square_two + alpha_two * alpha_two + square_three
    determinant = entry_first * entry_second - entry_cross * entry_cross
    coef_one = beta_one * (entry_second * alpha_one - entry_cross * beta_two) / determinant
    coef_two = beta_one * (entry_first * beta_two - entry_cross * alpha_one) / determinant
    on_second = coef_two * scale
    on_first = coef_one / beta_one - alpha_one * on_second
    out_ref[...] = on_first * first_ref[...] + on_second * second_ref[...]


def neighbour(value, steps):
    count = lax.axis_size(AXES)
    return lax.ppermute(value, AXES, [(s, (s + steps) % count) for s in range(count)])


def shape(*dims, dtype=F32):
    return jax.ShapeDtypeStruct(dims, dtype)


def on_device(
    local_deriv, global_deriv, measured, hit_weight, hit_module, hit_count, track_road, road_start,
    prior_weight,
):
    devices = lax.axis_size(AXES)
    roads = road_start.shape[0]
    tracks = hit_count.shape[0]
    modules = prior_weight.shape[0]
    cap = 4 * tracks // devices
    split = LANES // cap
    rows_each = rows_of(cap)
    slots = devices * cap
    width = ROAD * NPAR
    half = modules // ROAD
    vmem = pl.BlockSpec(memory_space=pltpu.VMEM)
    smem = pl.BlockSpec(memory_space=pltpu.SMEM)
    limit = pltpu.CompilerParams(vmem_limit_bytes=50 * 1024 * 1024)

    send = pl.pallas_call(
        functools.partial(send_kernel, cap, roads, rows_each),
        out_shape=shape(devices, rows_each, LANES),
        in_specs=[vmem] * 8,
        out_specs=vmem,
        scratch_shapes=[
            pltpu.VMEM((rows_each * split, tracks), F32),
            pltpu.VMEM((3 * rows_each * split, tracks), BF16),
        ],
        compiler_params=limit,
        name="fit_and_pack",
    )(
        local_deriv, global_deriv, measured, hit_weight, hit_module, hit_count[None, :],
        track_road[None, :], track_road[:, None],
    )
    recv = lax.all_to_all(send, AXES, split_axis=0, concat_axis=0, tiled=True)

    offset = road_start % ROAD
    list_rows = -(-(PER_ITEM * roads + slots) // (8 * LANES)) * 8
    item_rows = -(-(list_rows * LANES // PER_ITEM) // LANES)
    road_row = W_ROAD % rows_each
    track_list, items, bounds, track_off = pl.pallas_call(
        functools.partial(sort_kernel, cap),
        grid=(1,),
        out_shape=(
            shape(list_rows, LANES, dtype=jnp.int32),
            shape(item_rows, LANES, dtype=jnp.int32),
            shape(8, LANES, dtype=jnp.int32),
            shape(slots // LANES, LANES),
        ),
        in_specs=[
            pl.BlockSpec((devices, 8, LANES), lambda i: (0, road_row // 8, 0)),
            pl.BlockSpec((roads, 1), lambda i: (0, 0)),
        ],
        out_specs=(
            pl.BlockSpec((list_rows, LANES), lambda i: (0, 0)),
            pl.BlockSpec((item_rows, LANES), lambda i: (0, 0)),
            pl.BlockSpec((8, LANES), lambda i: (0, 0)),
            pl.BlockSpec((slots // LANES, LANES), lambda i: (0, 0)),
        ),
        scratch_shapes=[pltpu.VMEM((slots // LANES, LANES), F32)],
        compiler_params=limit,
        name="sort_by_road",
    )(recv, offset.astype(F32)[:, None])

    each = roads // GROUPS
    normal_blocks, sums = pl.pallas_call(
        functools.partial(blocks_kernel, cap),
        grid=(GROUPS,),
        out_shape=(shape(roads, width, width), shape(roads, width)),
        in_specs=[
            smem,
            smem,
            smem,
            pl.BlockSpec((devices, rows_each, LANES), lambda g: (0, 0, 0)),
            pl.BlockSpec((slots // LANES, LANES), lambda g: (0, 0)),
        ],
        out_specs=(
            pl.BlockSpec((each, width, width), lambda g: (g, 0, 0)),
            pl.BlockSpec((each, width), lambda g: (g, 0)),
        ),
        scratch_shapes=[
            pltpu.VMEM((slots + 8, 8, width), F32),
            pltpu.VMEM((rows_each * split, LANES), F32),
            pltpu.VMEM((each, 8, width), F32),
        ],
        compiler_params=limit,
        name="assemble_blocks",
    )(bounds, track_list, items, recv, track_off)

    prior = prior_weight.reshape(half, width)
    off_rows = jnp.broadcast_to((offset % (ROAD // 2)).astype(F32)[:, None], (roads, LANES))
    two = 2 * EDGE
    to_next = jnp.concatenate(
        [
            normal_blocks[-PREV_ROADS:].reshape(-1, width),
            sums[-two:],
            off_rows[-two:],
            prior[-EDGE:],
        ]
    )
    to_prev = jnp.concatenate(
        [
            normal_blocks[:NEXT_ROADS].reshape(-1, width),
            sums[:two],
            off_rows[:two],
            prior[:EDGE],
        ]
    )
    from_prev = neighbour(to_next, 1)
    from_next = neighbour(to_prev, -1)
    total = half + 2 * EDGE
    chunks = 16 if roads >= 256 else 4
    rows = pltpu.VMEM((total, LANES), F32)
    int_rows = pltpu.VMEM((total, LANES), jnp.int32)
    tiles = pltpu.VMEM((total, 8, LANES), F32)
    turned = pltpu.VMEM((LANES, LANES), F32)
    first, second, third, dots = pl.pallas_call(
        krylov_kernel,
        out_shape=(shape(half, width), shape(half, width), shape(half, width), shape(1, LANES)),
        in_specs=[pl.BlockSpec(memory_space=pl.ANY)] + [vmem] * 5,
        out_specs=(vmem,) * 4,
        scratch_shapes=[
            pltpu.VMEM((roads, width, width), F32),
            pltpu.SemaphoreType.DMA((chunks,)),
            rows, rows, int_rows, int_rows, rows, tiles, tiles, turned, turned, rows, rows, rows,
        ],
        compiler_params=limit,
        name="two_products",
    )(normal_blocks, sums, off_rows, prior, from_prev, from_next)
    del third
    everyone = lax.all_to_all(
        jnp.broadcast_to(dots[None], (devices, 1, LANES)), AXES, split_axis=0, concat_axis=0,
        tiled=True,
    )
    corrections = pl.pallas_call(
        finish_kernel,
        out_shape=shape(half, width),
        in_specs=[vmem] * 3,
        out_specs=vmem,
        name="combine",
    )(everyone.reshape(devices, LANES), first, second)
    return (
        normal_blocks, first.reshape(modules, NPAR), corrections.reshape(modules, NPAR),
    )


def solution(mesh):
    track = P(None, None, AXES)
    in_specs = (
        track, track, P(None, AXES), P(None, AXES), P(None, AXES), P(AXES), P(AXES), P(AXES),
        P(AXES, None),
    )
    out_specs = (P(AXES, None, None), P(AXES, None), P(AXES, None))
    return jax.shard_map(
        on_device, mesh=mesh, in_specs=in_specs, out_specs=out_specs, check_vma=False
    )
```

```python
import functools

import jax
import jax.numpy as jnp
from jax import lax
from jax.experimental import pallas as pl
from jax.experimental.pallas import tpu as pltpu
from jax.sharding import PartitionSpec as P

NPAR = 8
NHIT = 12
NLOC = 5
ROAD = 16
LANES = 128
EPS = 1e-06
AXES = ("trk", "mod")

W_SOLVED = NHIT * NPAR
W_SLOT = W_SOLVED + NHIT
W_ROAD = W_SLOT + NHIT
W_PROJ0 = W_ROAD + 1
W_PROJ1 = W_PROJ0 + 1
W_PROJ = W_PROJ1 + 2
WORDS = W_PROJ + NLOC * (NHIT - 2)

PER_ITEM = 8
UNROLL = 16
GROUPS = 16
SUM_ROW = NLOC + 1
EDGE = 8
NEXT_ROADS = 2
PREV_ROADS = 4
F32 = jnp.float32
BF16 = jnp.bfloat16


def iota(shape, dim):
    return lax.broadcasted_iota(jnp.int32, shape, dim)


def dot(lhs, rhs, lhs_dim, rhs_dim):
    return lax.dot_general(
        lhs, rhs, (((lhs_dim,), (rhs_dim,)), ((), ())), preferred_element_type=F32
    )


def split_three(value):
    high = value.astype(BF16)
    rest = value - high.astype(F32)
    middle = rest.astype(BF16)
    low = (rest - middle.astype(F32)).astype(BF16)
    return high, middle, low


def householder(rows, first, column):
    vector = [row[column : column + 1] for row in rows[first:]]
    norm = jnp.sqrt(sum(part * part for part in vector))
    vector[0] = vector[0] + jnp.where(vector[0] >= 0.0, norm, -norm)
    square = sum(part * part for part in vector)
    scale = jnp.where(square > 1e-30, 2.0 / jnp.maximum(square, 1e-30), 0.0)
    along = sum(part * row for part, row in zip(vector, rows[first:])) * scale
    return rows[:first] + [row - part * along for part, row in zip(vector, rows[first:])]


def send_kernel(
    cap, road_dev, rows_each, in_ref, out_ref, words_ref, parts_ref,
):
    tracks = in_ref.shape[1]
    ld_at = NPAR * NHIT
    me_at = ld_at + NLOC * NHIT
    hw_at, hm_at, hc_at = me_at + NHIT, me_at + 2 * NHIT, me_at + 3 * NHIT
    owned = in_ref[hc_at + 1 : hc_at + 2, :].astype(jnp.int32)
    split = LANES // cap
    words_all = rows_each * split
    weight = jnp.where(
        iota((NHIT, tracks), 0).astype(F32) < in_ref[hc_at : hc_at + 1, :],
        in_ref[hw_at:hm_at, :], 0.0,
    )
    root = jnp.sqrt(weight)
    scaled = [in_ref[ld_at + a * NHIT : ld_at + (a + 1) * NHIT, :] * root for a in range(NLOC)]
    factor = {}
    for a in range(NLOC):
        for b in range(a + 1):
            running = jnp.sum(scaled[a] * scaled[b], axis=0, keepdims=True)
            if a == b:
                running = running + 1.0
            for c in range(b):
                running = running - factor[a, c] * factor[b, c]
            factor[a, b] = jnp.sqrt(running) if a == b else running / factor[b, b]
    proj = []
    for a in range(NLOC):
        running = scaled[a]
        for b in range(a):
            running = running - factor[a, b] * proj[b]
        proj.append(running / factor[a, a])
    residual = in_ref[me_at:hw_at, :] * root
    solved = residual
    for a in range(NLOC):
        solved = solved - proj[a] * jnp.sum(proj[a] * residual, axis=0, keepdims=True)
    proj = householder(proj, 0, 0)
    proj = householder(proj, 1, 1)
    for i in range(NHIT):
        words_ref[i * NPAR : (i + 1) * NPAR, :] = in_ref[i * NPAR : (i + 1) * NPAR, :] * root[i : i + 1]
    words_ref[W_SOLVED:W_SLOT, :] = solved
    words_ref[W_SLOT:W_ROAD, :] = (in_ref[hm_at:hc_at, :].astype(jnp.int32) & (ROAD - 1)).astype(F32)
    owner = owned // road_dev
    words_ref[W_ROAD:W_PROJ0, :] = (owned - owner * road_dev + 1).astype(F32)
    words_ref[W_PROJ0:W_PROJ1, :] = proj[0][0:1]
    words_ref[W_PROJ1 : W_PROJ1 + 1, :] = proj[0][1:2]
    words_ref[W_PROJ1 + 1 : W_PROJ, :] = proj[1][1:2]
    for a in range(NLOC):
        at = W_PROJ + a * (NHIT - 2)
        words_ref[at : at + NHIT - 2, :] = proj[a][2:]
    words_ref[WORDS:, :] = jnp.zeros((words_all - WORDS, tracks), F32)
    for num, part in enumerate(split_three(words_ref[...])):
        parts_ref[num * words_all : (num + 1) * words_all, :] = part
    owner_col = jnp.concatenate(
        [
            jnp.broadcast_to(owner[:, at : at + LANES], (LANES, LANES)).astype(F32).T[:, :1]
            for at in range(0, tracks, LANES)
        ],
        axis=0,
    ).astype(jnp.int32)
    earlier = iota((tracks, tracks), 0) < iota((tracks, tracks), 1)
    same = jnp.where(jnp.logical_and(owner_col == owner, earlier), 1.0, 0.0)
    rank = jnp.sum(same, axis=0, keepdims=True).astype(jnp.int32)
    target = owner * cap + rank
    blocks = out_ref.shape[0] // split
    lane_part = iota((rows_each, LANES), 1) // cap
    per = 2
    for pair in range(blocks // per):
        hot = jnp.where(
            target == iota((per * LANES, tracks), 0) + pair * per * LANES, 1.0, 0.0
        ).astype(BF16)
        moved = dot(parts_ref[...], hot, 1, 1)
        moved = moved[:words_all] + moved[words_all : 2 * words_all] + moved[2 * words_all :]
        for sub in range(per):
            block = moved[:, sub * LANES : (sub + 1) * LANES]
            for k in range(split):
                made = None
                for m in range(split):
                    piece = block[m * rows_each : (m + 1) * rows_each]
                    if m != k:
                        piece = pltpu.roll(piece, (cap * (m - k)) % LANES, 1)
                    made = piece if made is None else jnp.where(lane_part == m, piece, made)
                out_ref[(pair * per + sub) * split + k] = made


def sort_kernel(cap, recv_ref, off_ref, list_ref, item_ref, bound_ref, off_out_ref, road_ref):
    split = LANES // cap
    roads = off_ref.shape[0]
    blocks = road_ref.shape[0]
    lane_part = iota((1, LANES), 1) // cap
    shift_of = road_part(cap)
    for e in range(blocks):
        made = None
        for k in range(split):
            piece = recv_ref[e * split + k, 0:1, :]
            if k != shift_of:
                piece = pltpu.roll(piece, (cap * (k - shift_of)) % LANES, 1)
            made = piece if made is None else jnp.where(lane_part == k, piece, made)
        road_ref[e : e + 1, :] = made
    road_num = (iota((roads, LANES), 0) + 1).astype(F32)
    upper = jnp.where(iota((LANES, LANES), 0) < iota((LANES, LANES), 1), 1.0, 0.0).astype(BF16)
    offset = off_ref[...]
    counts = jnp.zeros((roads, 1), F32)
    ranks = []
    for e in range(blocks):
        hot = jnp.where(road_ref[e : e + 1, :] == road_num, 1.0, 0.0)
        before = dot(hot.astype(BF16), upper, 1, 0) + counts
        ranks.append(jnp.sum(hot * before, axis=0, keepdims=True))
        off_out_ref[e : e + 1, :] = jnp.sum(hot * offset, axis=0, keepdims=True)
        counts = counts + jnp.sum(hot, axis=1, keepdims=True)
    items = jnp.maximum(jnp.floor((counts + (PER_ITEM - 1)) * (1.0 / PER_ITEM)), 1.0)
    items = jnp.broadcast_to(items, (roads, LANES))
    lower = jnp.where(iota((roads, roads), 1) < iota((roads, roads), 0), 1.0, 0.0).astype(BF16)
    begin = dot(lower, items.astype(BF16), 1, 0)
    rows = list_ref.shape[0]
    total = jnp.zeros((rows, 2 * LANES), F32)
    row_num = iota((rows, LANES), 0).astype(F32)
    lane_num = iota((LANES, LANES), 0).astype(F32)
    track_lane = iota((1, LANES), 1).astype(F32)
    for e in range(blocks):
        road = road_ref[e : e + 1, :]
        hot = jnp.where(road == road_num, 1.0, 0.0)
        place = PER_ITEM * jnp.sum(hot * begin, axis=0, keepdims=True) + ranks[e]
        place = jnp.where(road > 0.5, place, -1.0)
        high = jnp.floor(place * (1.0 / LANES))
        low = place - high * LANES
        pick = jnp.where(high == row_num, 1.0, 0.0).astype(BF16)
        match = low == lane_num
        values = jnp.concatenate(
            [jnp.where(match, float(e + 1), 0.0), jnp.where(match, track_lane, 0.0)], axis=0
        )
        total = total + dot(pick, values.astype(BF16), 1, 1)
    found = total[:, :LANES]
    track = jnp.where(found > 0.5, (found - 1.0) * LANES + total[:, LANES:], float(blocks * LANES))
    list_ref[...] = track.astype(jnp.int32)
    item_rows = item_ref.shape[0]
    for row in range(item_rows):
        item = (iota((1, LANES), 1) + row * LANES).astype(F32)
        road = jnp.sum(jnp.where(begin <= item, 1.0, 0.0), axis=0, keepdims=True) - 1.0
        first = jnp.sum(jnp.where(begin == item, 1.0, 0.0), axis=0, keepdims=True)
        item_ref[row : row + 1, :] = (2.0 * road + first).astype(jnp.int32)
    each = roads // GROUPS
    begins = jnp.where(iota((roads, LANES), 0) == iota((roads, LANES), 1) * each, begin, 0.0)
    bound = jnp.sum(begins, axis=0, keepdims=True)
    last = jnp.sum(items, axis=0, keepdims=True)
    bound = jnp.where(iota((1, LANES), 1) < GROUPS, bound, last)
    bound_ref[...] = jnp.broadcast_to(bound, bound_ref.shape).astype(jnp.int32)


def rows_of(cap):
    split = LANES // cap
    least = -(-WORDS // split)
    return -(-least // 8) * 8


def road_part(cap):
    return W_ROAD // rows_of(cap)


def lay_tiles(cap, recv_ref, off_ref, tiles_ref, words_ref):
    split = LANES // cap
    rows_each = recv_ref.shape[1]
    blocks = off_ref.shape[0]
    width = ROAD * NPAR
    lane_part = iota((rows_each, LANES), 1) // cap
    tiles_ref[blocks * LANES] = jnp.zeros((8, width), F32)

    def lay(e, held):
        words = words_ref.at[held]
        for m in range(split):
            made = None
            for k in range(split):
                piece = recv_ref[e * split + k]
                if k != m:
                    piece = pltpu.roll(piece, (cap * (k - m)) % LANES, 1)
                made = piece if made is None else jnp.where(lane_part == k, piece, made)
            words[m * rows_each : (m + 1) * rows_each, :] = made
        offset = off_ref[pl.ds(e, 1), :]
        slots = []
        for i in range(NHIT):
            slot = words[W_SLOT + i : W_SLOT + i + 1, :] - offset
            slots.append(jnp.where(slot < 0.0, slot + ROAD, slot))
        laid = [jnp.zeros((NPAR, LANES), F32) for s in range(ROAD)]
        for i in range(NHIT):
            value = words[i * NPAR : (i + 1) * NPAR, :]
            wide = jnp.broadcast_to(slots[i], (NPAR, LANES))
            for s in range(ROAD):
                laid[s] = jnp.where(wide == float(s), value, laid[s])
        slot_num = iota((ROAD, LANES), 0).astype(F32)
        placed = [jnp.zeros((ROAD, LANES), F32) for a in range(NLOC + 1)]
        for i in range(NHIT):
            match = slots[i] == slot_num
            for a in range(NLOC + 1):
                if a == NLOC:
                    at = W_SOLVED + i
                elif i == 0:
                    at = W_PROJ0 if a == 0 else None
                elif i == 1:
                    at = W_PROJ1 + a if a < 2 else None
                else:
                    at = W_PROJ + a * (NHIT - 2) + i - 2
                if at is not None:
                    placed[a] = jnp.where(match, words[at : at + 1, :], placed[a])
        start = pl.multiple_of(e * LANES, LANES)
        for a in range(NLOC + 1):
            mixed = jnp.concatenate([laid[s] * placed[a][s : s + 1] for s in range(ROAD)], axis=0)
            tiles_ref[pl.ds(start, LANES), a if a < NLOC else SUM_ROW, :] = mixed.T
        tiles_ref[pl.ds(start, LANES), NLOC, :] = jnp.concatenate(laid, axis=0).T
        tiles_ref[pl.ds(start, LANES), SUM_ROW + 1, :] = jnp.zeros((LANES, width), F32)

    def lay_two(num, carry):
        lay(2 * num, 0)
        lay(2 * num + 1, 1)
        return carry

    lax.fori_loop(0, blocks // 2, lay_two, 0)


def item_steps(list_ref, item_ref, tiles_ref, out_ref, held_ref):
    width = ROAD * NPAR
    row_kind = iota((PER_ITEM * 8, width), 0) % 8
    is_proj = row_kind < NLOC
    is_own = row_kind == NLOC
    same_slot = iota((width, width), 0) // NPAR == iota((width, width), 1) // NPAR
    spare = list_ref.shape[0] // PER_ITEM - 1

    def step(begin, end, num):
        for u in range(UNROLL):
            item = begin + num * UNROLL + u
            live = item < end
            item = jnp.where(live, item, spare)
            info = item_ref[item]
            first = (info & 1) == 1
            road = jnp.where(live, info >> 1, 0)
            at = item * PER_ITEM
            parts = [tiles_ref[list_ref[at + j]] for j in range(PER_ITEM)]
            tall = jnp.concatenate(parts, axis=0)
            high = tall.astype(BF16)
            high32 = high.astype(F32)
            low32 = tall - high32
            low = low32.astype(BF16)
            left = jnp.concatenate([high, high, low], axis=0)
            high_p = jnp.where(is_proj, high32, 0.0).astype(BF16)
            high_o = jnp.where(is_own, high32, 0.0).astype(BF16)
            low_p = jnp.where(is_proj, low32, 0.0).astype(BF16)
            low_o = jnp.where(is_own, low32, 0.0).astype(BF16)
            right = jnp.concatenate(
                [
                    jnp.concatenate([high_p, low_p, high_p], axis=0),
                    jnp.concatenate([high_o, low_o, high_o], axis=0),
                ],
                axis=1,
            )
            both = dot(left, right, 0, 0)
            value = jnp.where(same_slot, both[:, width:], 0.0) - both[:, :width]
            out_ref[road] = value + jnp.where(first, 0.0, out_ref[road])
            added = parts[0]
            for part in parts[1:]:
                added = added + part
            held_ref[road] = added + jnp.where(first, 0.0, held_ref[road])

    return step


def edge_kernel(
    cap, bound_ref, list_ref, item_ref, recv_ref, off_ref, off_rows_ref, prior_ref,
    tiles_ref, out_ref, sums_ref, to_next_ref, to_prev_ref, words_ref, held_ref,
):
    roads, width = sums_ref.shape
    edge = roads // GROUPS
    lay_tiles(cap, recv_ref, off_ref, tiles_ref, words_ref)
    step = item_steps(list_ref, item_ref, tiles_ref, out_ref, held_ref)
    for group in (0, GROUPS - 1):
        begin, end = bound_ref[group], bound_ref[group + 1]

        def body(num, carry, begin=begin, end=end):
            step(begin, end, num)
            return carry

        lax.fori_loop(0, (end - begin + UNROLL - 1) // UNROLL, body, 0)
    sums_ref[:edge] = held_ref[:edge, SUM_ROW, :]
    sums_ref[roads - edge :] = held_ref[roads - edge :, SUM_ROW, :]
    two = 2 * EDGE
    for ref, first_block, count, first_road, first_row in (
        (to_next_ref, roads - PREV_ROADS, PREV_ROADS, roads - two, prior_ref.shape[0] - EDGE),
        (to_prev_ref, 0, NEXT_ROADS, 0, 0),
    ):
        for num in range(count):
            ref[num * width : (num + 1) * width] = out_ref[first_block + num]
        at = count * width
        ref[at : at + two] = sums_ref[first_road : first_road + two]
        ref[at + two : at + 2 * two] = off_rows_ref[first_road : first_road + two]
        ref[at + 2 * two :] = prior_ref[first_row : first_row + EDGE]


def inner_kernel(
    bound_ref, list_ref, item_ref, tiles_ref, edge_ref, edge_sums_ref,
    blocks_hbm, out_ref, sums_ref, held_ref, sems,
):
    roads, width = sums_ref.shape
    edge = roads // GROUPS
    step = item_steps(list_ref, item_ref, tiles_ref, out_ref, held_ref)
    outer = [
        pltpu.make_async_copy(
            out_ref.at[pl.ds(at, edge)], blocks_hbm.at[pl.ds(at, edge)], sems.at[num]
        )
        for num, at in enumerate((0, roads - edge))
    ]
    begin, end = bound_ref[1], bound_ref[GROUPS - 1]
    done = 0
    copies = []
    pieces = (GROUPS - 2) // 2
    for piece in range(pieces):
        group = 1 + 2 * piece
        until = (bound_ref[group + 2] - begin + UNROLL - 1) // UNROLL

        def body(num, carry):
            step(begin, end, num)
            return carry

        lax.fori_loop(done, until, body, 0)
        done = until
        where = pl.ds(group * edge, 2 * edge)
        copies.append(
            pltpu.make_async_copy(out_ref.at[where], blocks_hbm.at[where], sems.at[2 + piece])
        )
        copies[-1].start()
    for copy in outer:
        copy.start()
    sums_ref[edge : roads - edge] = held_ref[edge : roads - edge, SUM_ROW, :]
    for copy in outer + copies:
        copy.wait()
    del edge_ref, edge_sums_ref


def lane_bits(offset, bit):
    return (offset // (1 << bit)) % 2 == 1


def gathered(rows, offset, odd):
    lane = iota(rows.shape, 1)
    here = rows
    there = jnp.concatenate([rows[1:], jnp.zeros((1, LANES), F32)], axis=0)
    if odd:
        half = LANES // 2
        turned_here, turned_there = pltpu.roll(here, half, 1), pltpu.roll(there, half, 1)
        here = jnp.where(lane < LANES - half, turned_here, turned_there)
        there = turned_there
    for bit in range(3):
        step = NPAR << bit
        take = lane_bits(offset, bit)
        turned_here, turned_there = (
            pltpu.roll(here, LANES - step, 1),
            pltpu.roll(there, LANES - step, 1),
        )
        moved = jnp.where(lane < LANES - step, turned_here, turned_there)
        here = jnp.where(take, moved, here)
        there = jnp.where(take, turned_there, there)
    return here


def scattered(rows, offset, odd):
    lane = iota(rows.shape, 1)
    here, there = rows, jnp.zeros_like(rows)
    steps = [(NPAR << bit, bit) for bit in range(3)] + ([(LANES // 2, None)] if odd else [])
    for step, bit in steps:
        turned_here, turned_there = pltpu.roll(here, step, 1), pltpu.roll(there, step, 1)
        new_here = jnp.where(lane < step, 0.0, turned_here)
        new_there = jnp.where(lane < step, turned_here, turned_there)
        if bit is None:
            here, there = new_here, new_there
        else:
            take = lane_bits(offset, bit)
            here = jnp.where(take, new_here, here)
            there = jnp.where(take, new_there, there)
    return here, there


def krylov_kernel(
    held, sums_ref, off_ref, prior_ref, from_prev_ref, from_next_ref,
    first_ref, second_ref, dots_ref,
    even_sum, odd_sum, even_off, odd_off, prior, even_part, odd_part, turned_even,
    turned_odd,
):
    roads, width = sums_ref.shape
    half = roads // 2
    each = min(roads, 64)
    chunks = roads // each
    own = slice(EDGE, EDGE + half)
    two = 2 * EDGE
    at_prev = PREV_ROADS * width
    at_next = NEXT_ROADS * width
    for parity, total_sum, total_off in ((0, even_sum, even_off), (1, odd_sum, odd_off)):
        pick = lambda ref, start, count: ref[pl.ds(start + parity, count, stride=2), :]
        total_sum[0:EDGE] = pick(from_prev_ref, at_prev, EDGE)
        total_sum[own] = pick(sums_ref, 0, half)
        total_sum[EDGE + half :] = pick(from_next_ref, at_next, EDGE)
        total_off[0:EDGE] = pick(from_prev_ref, at_prev + two, EDGE).astype(jnp.int32)
        total_off[own] = pick(off_ref, 0, half).astype(jnp.int32)
        total_off[EDGE + half :] = pick(from_next_ref, at_next + two, EDGE).astype(jnp.int32)
    prior[0:EDGE] = from_prev_ref[at_prev + 2 * two : at_prev + 2 * two + EDGE]
    prior[own] = prior_ref[...]
    prior[EDGE + half :] = from_next_ref[at_next + 2 * two : at_next + 2 * two + EDGE]

    def spread(even, odd):
        even_here, even_there = scattered(even, even_off[...], False)
        odd_here, odd_there = scattered(odd, odd_off[...], True)
        over = even_there + odd_there
        return (
            even_here
            + odd_here
            + jnp.concatenate([jnp.zeros((1, LANES), F32), over[:-1]], axis=0)
        )

    def column_product(tile_at, column):
        acc = None
        for s in range(width // 8):
            term = tile_at(s) * column[s * 8 : (s + 1) * 8]
            acc = term if acc is None else acc + term
        return acc

    def apply(vector):
        even = gathered(vector, even_off[...], False)
        odd = gathered(vector, odd_off[...], True)
        even_part[...] = jnp.zeros_like(even_part)
        odd_part[...] = jnp.zeros_like(odd_part)
        edge_even = jnp.concatenate(
            [even[:EDGE], even[EDGE + half :], jnp.zeros((LANES - 2 * EDGE, LANES), F32)], axis=0
        ).T
        edge_odd = jnp.concatenate(
            [odd[:EDGE], odd[EDGE + half :], jnp.zeros((LANES - 2 * EDGE, LANES), F32)], axis=0
        ).T
        for num in range(PREV_ROADS):
            row = EDGE - PREV_ROADS // 2 + num // 2
            column = (edge_even if num % 2 == 0 else edge_odd)[:, row : row + 1]
            part = even_part if num % 2 == 0 else odd_part
            part[row] = column_product(
                lambda s, num=num: from_prev_ref[num * width + s * 8 : num * width + s * 8 + 8],
                column,
            )
        for num in range(NEXT_ROADS):
            column = (edge_even if num % 2 == 0 else edge_odd)[:, EDGE : EDGE + 1]
            part = even_part if num % 2 == 0 else odd_part
            part[EDGE + half] = column_product(
                lambda s, num=num: from_next_ref[num * width + s * 8 : num * width + s * 8 + 8],
                column,
            )
        turned_even[:, :half] = even[own].T
        turned_odd[:, :half] = odd[own].T
        per = each // 2

        copies_of = iota((3 * per, per * width), 0) % per == iota((3 * per, per * width), 1) // width
        copies_of = jnp.where(copies_of, 1.0, 0.0).astype(BF16)

        def chunk(c, carry):
            columns_even = turned_even[...]
            columns_odd = turned_odd[...]
            spread_odd = dot(
                jnp.concatenate(split_three(columns_odd[:, :per]), axis=1), copies_of, 1, 0
            )
            for j in range(per):
                road = c * each + 2 * j
                even_part[EDGE + c * per + j] = column_product(
                    lambda s, road=road: held[road, s * 8 : s * 8 + 8, :],
                    columns_even[:, j : j + 1],
                )
                odd_part[EDGE + c * per + j] = column_product(
                    lambda s, road=road: held[road + 1, s * 8 : s * 8 + 8, :],
                    spread_odd[:, j * width : (j + 1) * width],
                )
            turned_even[...] = pltpu.roll(columns_even, columns_even.shape[1] - per, 1)
            turned_odd[...] = pltpu.roll(columns_odd, columns_odd.shape[1] - per, 1)
            return carry

        lax.fori_loop(0, chunks, chunk, 0)
        even = even_part[:, 0, :]
        odd = odd_part[:, 0, :]
        for k in range(1, 8):
            even = even + even_part[:, k, :]
            odd = odd + odd_part[:, k, :]
        return prior[...] * vector + spread(even, odd)

    first = spread(even_sum[...], odd_sum[...])
    second = apply(first)
    third = apply(second)
    first, second, third = first[own], second[own], third[own]
    first_ref[...] = first
    second_ref[...] = second
    lane = iota(dots_ref.shape, 2)
    dots = jnp.zeros(dots_ref.shape, F32)
    pairs = ((first, first), (first, second), (second, second), (second, third), (third, third))
    for num, (one, other) in enumerate(pairs):
        dots = dots + jnp.where(lane == num, jnp.sum(one * other), 0.0)
    dots_ref[...] = dots


def finish_kernel(dots_ref, first_ref, second_ref, out_hbm, out_ref, sem):
    sums = jnp.sum(dots_ref[...], axis=0, keepdims=True)
    s00, s01, s11, s12, s22 = (sums[:, num : num + 1] for num in range(5))
    square_one = s00 + EPS
    beta_one = jnp.sqrt(square_one)
    alpha_one = s01 / square_one
    square_two = (s11 - 2.0 * alpha_one * s01 + alpha_one * alpha_one * s00) / square_one + EPS
    beta_two = jnp.sqrt(square_two)
    scale = 1.0 / (beta_one * beta_two)
    s02 = s11
    cross = s12 - alpha_one * s11 - square_two * s01
    cross = cross - alpha_one * (s02 - alpha_one * s01 - square_two * s00)
    alpha_two = cross * scale * scale
    near = alpha_one + alpha_two
    far = alpha_one * alpha_two - square_two
    square_three = s22 - 2.0 * near * s12 + near * near * s11
    square_three = square_three + 2.0 * far * s02 - 2.0 * near * far * s01 + far * far * s00
    square_three = square_three * scale * scale + EPS
    entry_first = alpha_one * alpha_one + square_two
    entry_cross = beta_two * near
    entry_second = square_two + alpha_two * alpha_two + square_three
    determinant = entry_first * entry_second - entry_cross * entry_cross
    coef_one = beta_one * (entry_second * alpha_one - entry_cross * beta_two) / determinant
    coef_two = beta_one * (entry_first * beta_two - entry_cross * alpha_one) / determinant
    on_second = coef_two * scale
    on_first = coef_one / beta_one - alpha_one * on_second
    out_ref[...] = on_first * first_ref[...] + on_second * second_ref[...]
    copy = pltpu.make_async_copy(out_ref, out_hbm, sem)
    copy.start()
    copy.wait()


def neighbour(value, steps):
    count = lax.axis_size(AXES)
    return lax.ppermute(value, AXES, [(s, (s + steps) % count) for s in range(count)])


def shape(*dims, dtype=F32):
    return jax.ShapeDtypeStruct(dims, dtype)


def on_device(
    local_deriv, global_deriv, measured, hit_weight, hit_module, hit_count, track_road, road_start,
    prior_weight,
):
    devices = lax.axis_size(AXES)
    roads = road_start.shape[0]
    tracks = hit_count.shape[0]
    modules = prior_weight.shape[0]
    cap = 4 * tracks // devices
    split = LANES // cap
    rows_each = rows_of(cap)
    slots = devices * cap
    width = ROAD * NPAR
    half = modules // ROAD
    vmem = pl.BlockSpec(memory_space=pltpu.VMEM)
    smem = pl.BlockSpec(memory_space=pltpu.SMEM)
    limit = pltpu.CompilerParams(vmem_limit_bytes=32 * 1024 * 1024)
    small = pltpu.CompilerParams(vmem_limit_bytes=12 * 1024 * 1024)

    sent = [
        jnp.transpose(global_deriv, (1, 0, 2)).reshape(NHIT * NPAR, tracks),
        local_deriv.reshape(NLOC * NHIT, tracks), measured, hit_weight, hit_module.astype(F32),
        hit_count.astype(F32)[None, :], track_road.astype(F32)[None, :],
    ]
    sent = jnp.concatenate(sent)
    send = pl.pallas_call(
        functools.partial(send_kernel, cap, roads, rows_each),
        out_shape=shape(devices, rows_each, LANES),
        in_specs=[vmem],
        out_specs=vmem,
        scratch_shapes=[
            pltpu.VMEM((rows_each * split, tracks), F32),
            pltpu.VMEM((3 * rows_each * split, tracks), BF16),
        ],
        compiler_params=limit,
        name="fit_and_pack",
    )(sent)
    recv = lax.all_to_all(send, AXES, split_axis=0, concat_axis=0, tiled=True)

    offset = road_start % ROAD
    list_rows = ((PER_ITEM * roads + slots) // (8 * LANES) + 1) * 8
    item_rows = -(-(list_rows * LANES // PER_ITEM) // (8 * LANES)) * 8
    road_row = W_ROAD % rows_each
    track_list, items, bounds, track_off = pl.pallas_call(
        functools.partial(sort_kernel, cap),
        grid=(1,),
        out_shape=(
            shape(list_rows, LANES, dtype=jnp.int32),
            shape(item_rows, LANES, dtype=jnp.int32),
            shape(8, LANES, dtype=jnp.int32),
            shape(slots // LANES, LANES),
        ),
        in_specs=[
            pl.BlockSpec((devices, 8, LANES), lambda i: (0, road_row // 8, 0)),
            pl.BlockSpec((roads, 1), lambda i: (0, 0)),
        ],
        out_specs=(
            pl.BlockSpec((list_rows, LANES), lambda i: (0, 0)),
            pl.BlockSpec((item_rows, LANES), lambda i: (0, 0)),
            pl.BlockSpec((8, LANES), lambda i: (0, 0)),
            pl.BlockSpec((slots // LANES, LANES), lambda i: (0, 0)),
        ),
        scratch_shapes=[pltpu.VMEM((slots // LANES, LANES), F32)],
        compiler_params=limit,
        name="sort_by_road",
    )(recv, offset.astype(F32)[:, None])

    edge = roads // GROUPS
    prior = prior_weight.reshape(half, width)
    off_rows = jnp.broadcast_to((offset % (ROAD // 2)).astype(F32)[:, None], (roads, LANES))
    lists = (bounds.reshape(-1), track_list.reshape(-1), items.reshape(-1))
    halo = 4 * EDGE + EDGE
    tiles, edge_blocks, edge_sums, to_next, to_prev = pl.pallas_call(
        functools.partial(edge_kernel, cap),
        out_shape=(
            shape(slots + 8, 8, width), shape(roads, width, width), shape(roads, width),
            shape(PREV_ROADS * width + halo, width), shape(NEXT_ROADS * width + halo, width),
        ),
        in_specs=[smem] * 3 + [vmem] * 4,
        out_specs=(vmem,) * 5,
        scratch_shapes=[
            pltpu.VMEM((2, rows_each * split, LANES), F32),
            pltpu.VMEM((roads, 8, width), F32),
        ],
        compiler_params=small,
        name="lay_and_assemble_edges",
    )(*lists, recv, track_off, off_rows, prior)
    from_prev = neighbour(to_next, 1)
    from_next = neighbour(to_prev, -1)
    normal_blocks, held_blocks, sums = pl.pallas_call(
        inner_kernel,
        out_shape=(
            shape(roads, width, width), shape(roads, width, width), shape(roads, width),
        ),
        in_specs=[smem] * 3 + [vmem] * 3,
        out_specs=(pl.BlockSpec(memory_space=pltpu.HBM), vmem, vmem),
        scratch_shapes=[
            pltpu.VMEM((roads, 8, width), F32),
            pltpu.SemaphoreType.DMA((2 + (GROUPS - 2) // 2,)),
        ],
        input_output_aliases={4: 1, 5: 2},
        compiler_params=small,
        name="assemble_blocks",
    )(*lists, tiles, edge_blocks, edge_sums)

    total = half + 2 * EDGE
    rows = pltpu.VMEM((total, LANES), F32)
    int_rows = pltpu.VMEM((total, LANES), jnp.int32)
    parts = pltpu.VMEM((total, 8, LANES), F32)
    turned = pltpu.VMEM((LANES, LANES), F32)
    first, second, dots = pl.pallas_call(
        krylov_kernel,
        out_shape=(shape(half, width), shape(half, width), shape(devices, 1, LANES)),
        in_specs=[vmem] * 6,
        out_specs=(vmem,) * 3,
        scratch_shapes=[rows, rows, int_rows, int_rows, rows, parts, parts, turned, turned],
        compiler_params=small,
        name="two_products",
    )(held_blocks, sums, off_rows, prior, from_prev, from_next)
    everyone = lax.all_to_all(dots, AXES, split_axis=0, concat_axis=0, tiled=True)
    rhs = first.reshape(modules, NPAR)
    summed = (everyone.reshape(devices, LANES), rhs.T, second.reshape(modules, NPAR).T)
    corrections = pl.pallas_call(
        finish_kernel,
        out_shape=shape(NPAR, modules),
        in_specs=[vmem] * 3,
        out_specs=pl.BlockSpec(memory_space=pltpu.HBM),
        scratch_shapes=[pltpu.VMEM((NPAR, modules), F32), pltpu.SemaphoreType.DMA],
        name="combine",
    )(*summed)
    return (normal_blocks, rhs, corrections.T)


def solution(mesh):
    track = P(None, None, AXES)
    in_specs = (
        track, track, P(None, AXES), P(None, AXES), P(None, AXES), P(AXES), P(AXES), P(AXES),
        P(AXES, None),
    )
    out_specs = (P(AXES, None, None), P(AXES, None), P(AXES, None))
    return jax.shard_map(
        on_device, mesh=mesh, in_specs=in_specs, out_specs=out_specs, check_vma=False
    )
```

```python
import functools

import jax
import jax.numpy as jnp
from jax import lax
from jax.experimental import pallas as pl
from jax.experimental.pallas import tpu as pltpu
from jax.sharding import PartitionSpec as P

NPAR = 8
NHIT = 12
NLOC = 5
ROAD = 16
LANES = 128
EPS = 1e-06
AXES = ("trk", "mod")

PART = 88
USED = 82
R_ROAD = 10 * NPAR
R_FIRST = R_ROAD + 1
R_SOLVED = PART + 2 * NPAR
R_GAP = R_SOLVED + NHIT
GAPS = ROAD - NHIT
R_PROJ = [R_GAP + GAPS + a * NHIT - a * (a - 1) // 2 for a in range(NLOC)]
ROWS = 2 * PART


def derivative_row(hit):
    return hit * NPAR if hit < 10 else PART + (hit - 10) * NPAR


LARGE = 60
PER_ITEM = 8
UNROLL = 16
GROUPS = 16
SUM_ROW = NLOC + 1
EDGE = 8
NEXT_ROADS = 2
PREV_ROADS = 4
F32 = jnp.float32
BF16 = jnp.bfloat16


def iota(shape, dim):
    return lax.broadcasted_iota(jnp.int32, shape, dim)


def dot(lhs, rhs, lhs_dim, rhs_dim):
    return lax.dot_general(
        lhs, rhs, (((lhs_dim,), (rhs_dim,)), ((), ())), preferred_element_type=F32
    )


def split_three(value):
    high = value.astype(BF16)
    rest = value - high.astype(F32)
    middle = rest.astype(BF16)
    low = (rest - middle.astype(F32)).astype(BF16)
    return high, middle, low


def householder(rows, first, column):
    vector = [row[column : column + 1] for row in rows[first:]]
    norm = jnp.sqrt(sum(part * part for part in vector))
    vector[0] = vector[0] + jnp.where(vector[0] >= 0.0, norm, -norm)
    square = sum(part * part for part in vector)
    scale = jnp.where(square > 1e-30, 2.0 / jnp.maximum(square, 1e-30), 0.0)
    along = sum(part * row for part, row in zip(vector, rows[first:])) * scale
    return rows[:first] + [row - part * along for part, row in zip(vector, rows[first:])]


def place_tracks(cap, road_dev, track_road, hot_ref):
    tracks = track_road.shape[1]
    owner = track_road // road_dev
    owner_col = jnp.concatenate(
        [
            jnp.broadcast_to(owner[:, at : at + LANES], (LANES, LANES)).astype(F32).T[:, :1]
            for at in range(0, tracks, LANES)
        ],
        axis=0,
    ).astype(jnp.int32)
    earlier = iota((tracks, tracks), 0) < iota((tracks, tracks), 1)
    same = jnp.where(jnp.logical_and(owner_col == owner, earlier), 1.0, 0.0)
    rank = jnp.sum(same, axis=0, keepdims=True).astype(jnp.int32)
    target = owner * cap + rank
    step = 2 * LANES
    for at in range(0, hot_ref.shape[0], step):
        hot = jnp.where(target == iota((step, tracks), 0) + at, 1.0, 0.0)
        hot_ref[at : at + step, :] = hot.astype(BF16)


def pack_kernel(
    cap, road_dev, module_count, ld_hbm, gd_hbm, me_hbm, hw_hbm, hm_hbm, hc_hbm, tr_hbm,
    out_ref, words_ref, parts_ref, mixed_ref, sorted_ref, hot_ref,
    ld_ref, gd_ref, me_ref, hw_ref, hm_ref, hc_ref, tr_ref, sems,
):
    sources = (tr_hbm, hc_hbm, hw_hbm, ld_hbm, me_hbm, hm_hbm, gd_hbm)
    targets = (tr_ref, hc_ref, hw_ref, ld_ref, me_ref, hm_ref, gd_ref)
    copies = [
        pltpu.make_async_copy(source, target, sems.at[num])
        for num, (source, target) in enumerate(zip(sources, targets))
    ]
    for copy in copies:
        copy.start()
    copies[0].wait()
    place_tracks(cap, road_dev, tr_ref[...], hot_ref)
    for copy in copies[1:]:
        copy.wait()
    tracks = tr_ref.shape[1]
    weight = jnp.where(iota((NHIT, tracks), 0) < hc_ref[...], hw_ref[...], 0.0)
    root = jnp.sqrt(weight)
    ahead = hm_ref[...] - tr_ref[...] * (ROAD // 2)
    ahead = jnp.where(ahead < 0, ahead + module_count, ahead).astype(F32)
    order = jnp.zeros((NHIT, tracks), F32)
    for i in range(NHIT):
        order = order + jnp.where(ahead[i : i + 1] < ahead, 1.0, 0.0)
    for a in range(NLOC):
        mixed_ref[:, a, :] = ld_ref[a] * root
    mixed_ref[:, NLOC, :] = me_ref[...] * root
    mixed_ref[:, NLOC + 1, :] = ahead
    mixed_ref[:, NLOC + 2, :] = order
    for at in range(0, tracks, LANES):
        lanes = slice(at, at + LANES)
        tiles = [mixed_ref[i, :, lanes] for i in range(NHIT)]
        places = [jnp.broadcast_to(tile[NLOC + 2 : NLOC + 3], (8, LANES)) for tile in tiles]
        derivs = [gd_ref[i, :, lanes] * root[i : i + 1, lanes] for i in range(NHIT)]
        for k in range(NHIT):
            tile, deriv = tiles[0], derivs[0]
            for i in range(1, NHIT):
                here = places[i] == float(k)
                tile = jnp.where(here, tiles[i], tile)
                deriv = jnp.where(here, derivs[i], deriv)
            sorted_ref[k, :, lanes] = tile
            row = derivative_row(k)
            words_ref[row : row + NPAR, lanes] = deriv
    scaled = [sorted_ref[:, a, :] for a in range(NLOC)]
    factor = {}
    for a in range(NLOC):
        for b in range(a + 1):
            running = jnp.sum(scaled[a] * scaled[b], axis=0, keepdims=True)
            if a == b:
                running = running + 1.0
            for c in range(b):
                running = running - factor[a, c] * factor[b, c]
            factor[a, b] = jnp.sqrt(running) if a == b else running / factor[b, b]
    proj = []
    for a in range(NLOC):
        running = scaled[a]
        for b in range(a):
            running = running - factor[a, b] * proj[b]
        proj.append(running / factor[a, a])
    residual = sorted_ref[:, NLOC, :]
    solved = residual
    for a in range(NLOC):
        solved = solved - proj[a] * jnp.sum(proj[a] * residual, axis=0, keepdims=True)
    for a in range(NLOC - 1):
        proj = householder(proj, a, a)
    ahead = sorted_ref[:, NLOC + 1, :]
    skipped = ahead - ahead[0:1] - iota((NHIT, tracks), 0).astype(F32)
    words_ref[R_ROAD:R_FIRST, :] = (tr_ref[...] % road_dev + 1).astype(F32)
    words_ref[R_FIRST:USED, :] = ahead[0:1]
    words_ref[USED:PART, :] = jnp.zeros((PART - USED, tracks), F32)
    words_ref[R_SOLVED:R_GAP, :] = solved
    for gap in range(GAPS):
        words_ref[R_GAP + gap : R_GAP + gap + 1, :] = jnp.sum(
            jnp.where(skipped < gap + 0.5, 1.0, 0.0), axis=0, keepdims=True
        )
    for a in range(NLOC):
        words_ref[R_PROJ[a] : R_PROJ[a] + NHIT - a, :] = proj[a][a:]
    words_ref[PART + USED :, :] = jnp.zeros((PART - USED, tracks), F32)
    for num, part in enumerate(split_three(words_ref[...])):
        parts_ref[num * ROWS : (num + 1) * ROWS, :] = part
    lower_half = iota((USED, LANES), 1) < LANES // 2
    step = 2 * LANES
    for at in range(0, hot_ref.shape[0], step):
        moved = dot(parts_ref[...], hot_ref[at : at + step, :], 1, 1)
        moved = moved[:ROWS] + moved[ROWS : 2 * ROWS] + moved[2 * ROWS :]
        if not folded(cap):
            out_ref[:, at : at + step] = moved
            continue
        for sub in range(2):
            lanes = slice(sub * LANES, (sub + 1) * LANES)
            one = moved[:USED, lanes]
            two = moved[PART : PART + USED, lanes]
            row = (at // LANES + sub) * 2 * USED
            out_ref[row : row + USED] = jnp.where(lower_half, one, pltpu.roll(two, LANES // 2, 1))
            out_ref[row + USED : row + 2 * USED] = jnp.where(
                lower_half, pltpu.roll(one, LANES // 2, 1), two
            )


def folded(cap):
    return 2 * cap == LANES


def sort_kernel(cap, recv_ref, off_ref, list_ref, item_ref, bound_ref, off_out_ref, road_ref):
    roads = off_ref.shape[0]
    blocks = road_ref.shape[0]
    if folded(cap):
        even = recv_ref[pl.ds(R_ROAD, blocks, stride=2 * USED), :]
        odd = recv_ref[pl.ds(R_ROAD + USED, blocks, stride=2 * USED), :]
        lower_half = iota((blocks, LANES), 1) < LANES // 2
        road_ref[...] = jnp.where(lower_half, even, pltpu.roll(odd, LANES // 2, 1))
    else:
        for e in range(blocks):
            road_ref[e : e + 1, :] = recv_ref[R_ROAD : R_ROAD + 1, e * LANES : (e + 1) * LANES]
    road_num = (iota((roads, LANES), 0) + 1).astype(F32)
    upper = jnp.where(iota((LANES, LANES), 0) < iota((LANES, LANES), 1), 1.0, 0.0).astype(BF16)
    offset = off_ref[...]
    counts = jnp.zeros((roads, 1), F32)
    ranks = []
    for e in range(blocks):
        hot = jnp.where(road_ref[e : e + 1, :] == road_num, 1.0, 0.0)
        before = dot(hot.astype(BF16), upper, 1, 0) + counts
        ranks.append(jnp.sum(hot * before, axis=0, keepdims=True))
        off_out_ref[e : e + 1, :] = jnp.sum(hot * offset, axis=0, keepdims=True)
        counts = counts + jnp.sum(hot, axis=1, keepdims=True)
    items = jnp.maximum(jnp.floor((counts + (PER_ITEM - 1)) * (1.0 / PER_ITEM)), 1.0)
    items = jnp.broadcast_to(items, (roads, LANES))
    lower = jnp.where(iota((roads, roads), 1) < iota((roads, roads), 0), 1.0, 0.0).astype(BF16)
    begin = dot(lower, items.astype(BF16), 1, 0)
    rows = list_ref.shape[0]
    total = jnp.zeros((rows, 2 * LANES), F32)
    row_num = iota((rows, LANES), 0).astype(F32)
    lane_num = iota((LANES, LANES), 0).astype(F32)
    track_lane = iota((1, LANES), 1).astype(F32)
    for e in range(blocks):
        road = road_ref[e : e + 1, :]
        hot = jnp.where(road == road_num, 1.0, 0.0)
        place = PER_ITEM * jnp.sum(hot * begin, axis=0, keepdims=True) + ranks[e]
        place = jnp.where(road > 0.5, place, -1.0)
        high = jnp.floor(place * (1.0 / LANES))
        low = place - high * LANES
        pick = jnp.where(high == row_num, 1.0, 0.0).astype(BF16)
        match = low == lane_num
        values = jnp.concatenate(
            [jnp.where(match, float(e + 1), 0.0), jnp.where(match, track_lane, 0.0)], axis=0
        )
        total = total + dot(pick, values.astype(BF16), 1, 1)
    found = total[:, :LANES]
    track = jnp.where(found > 0.5, (found - 1.0) * LANES + total[:, LANES:], float(blocks * LANES))
    list_ref[...] = track.astype(jnp.int32)
    item_rows = item_ref.shape[0]
    for row in range(item_rows):
        item = (iota((1, LANES), 1) + row * LANES).astype(F32)
        road = jnp.sum(jnp.where(begin <= item, 1.0, 0.0), axis=0, keepdims=True) - 1.0
        first = jnp.sum(jnp.where(begin == item, 1.0, 0.0), axis=0, keepdims=True)
        item_ref[row : row + 1, :] = (2.0 * road + first).astype(jnp.int32)
    each = roads // GROUPS
    begins = jnp.where(iota((roads, LANES), 0) == iota((roads, LANES), 1) * each, begin, 0.0)
    bound = jnp.sum(begins, axis=0, keepdims=True)
    last = jnp.sum(items, axis=0, keepdims=True)
    bound = jnp.where(iota((1, LANES), 1) < GROUPS, bound, last)
    bound_ref[...] = jnp.broadcast_to(bound, bound_ref.shape).astype(jnp.int32)


def lay_tiles(cap, recv_ref, off_ref, tiles_ref, words_ref, shift_ref):
    blocks = off_ref.shape[0]
    width = ROAD * NPAR
    lower_half = iota((USED, LANES), 1) < LANES // 2
    slot_num = iota((ROAD, LANES), 0)
    tiles_ref[blocks * LANES] = jnp.zeros((8, width), F32)
    shift_ref[:, :8, :] = jnp.full((2, 8, LANES), -1.0, F32)

    def lay(num, held):
        words = words_ref.at[held]
        shifts = shift_ref.at[held]
        e = 2 * num + held
        if folded(cap):
            both = recv_ref.at[pl.ds(pl.multiple_of(num * 4 * USED, 8), 4 * USED)]
            one = both[held * 2 * USED : held * 2 * USED + USED, :]
            two = both[held * 2 * USED + USED : held * 2 * USED + 2 * USED, :]
            words[:USED] = jnp.where(lower_half, one, pltpu.roll(two, LANES // 2, 1))
            words[PART : PART + USED] = jnp.where(lower_half, pltpu.roll(one, LANES // 2, 1), two)
        else:
            words[...] = recv_ref[:, pl.ds(pl.multiple_of(e * LANES, LANES), LANES)]
        shift = words[R_FIRST : R_FIRST + 1, :] - off_ref[pl.ds(e, 1), :]
        for gap in range(GAPS):
            reached = slot_num.astype(F32) >= words[R_GAP + gap : R_GAP + gap + 1, :]
            shift = shift + jnp.where(reached, 1.0, 0.0)
        shifts[8 : 8 + ROAD] = jnp.where(slot_num < NHIT, shift, -1.0)
        laid = [jnp.zeros((NPAR, LANES), F32) for s in range(ROAD)]
        for i in range(NHIT):
            row = derivative_row(i)
            value = words[row : row + NPAR, :]
            wide = jnp.broadcast_to(shifts[8 + i : 9 + i, :], (NPAR, LANES))
            for move in range(GAPS + 1):
                laid[i + move] = jnp.where(wide == float(move), value, laid[i + move])
        placed = [jnp.zeros((ROAD, LANES), F32) for a in range(NLOC + 1)]
        for move in range(GAPS + 1):
            match = shifts[8 - move : 8 - move + ROAD, :] == float(move)
            for a in range(NLOC + 1):
                if a == NLOC:
                    row, valid = R_SOLVED - move, match
                else:
                    row = R_PROJ[a] - a - move
                    valid = jnp.logical_and(match, slot_num >= a + move) if a else match
                placed[a] = jnp.where(valid, words[row : row + ROAD, :], placed[a])
        start = pl.multiple_of(e * LANES, LANES)
        for a in range(NLOC + 1):
            mixed = jnp.concatenate([laid[s] * placed[a][s : s + 1] for s in range(ROAD)], axis=0)
            tiles_ref[pl.ds(start, LANES), a if a < NLOC else SUM_ROW, :] = mixed.T
        tiles_ref[pl.ds(start, LANES), NLOC, :] = jnp.concatenate(laid, axis=0).T
        tiles_ref[pl.ds(start, LANES), SUM_ROW + 1, :] = jnp.zeros((LANES, width), F32)

    def lay_two(num, carry):
        lay(num, 0)
        lay(num, 1)
        return carry

    lax.fori_loop(0, blocks // 2, lay_two, 0)


def item_steps(list_ref, item_ref, tiles_ref, out_ref, held_ref):
    width = ROAD * NPAR
    row_kind = iota((PER_ITEM * 8, width), 0) % 8
    is_proj = row_kind < NLOC
    is_own = row_kind == NLOC
    same_slot = iota((width, width), 0) // NPAR == iota((width, width), 1) // NPAR
    spare = list_ref.shape[0] // PER_ITEM - 1

    def step(begin, end, num):
        for u in range(UNROLL):
            item = begin + num * UNROLL + u
            live = item < end
            item = jnp.where(live, item, spare)
            info = item_ref[item]
            first = (info & 1) == 1
            road = jnp.where(live, info >> 1, 0)
            at = item * PER_ITEM
            parts = [tiles_ref[list_ref[at + j]] for j in range(PER_ITEM)]
            tall = jnp.concatenate(parts, axis=0)
            high = tall.astype(BF16)
            high32 = high.astype(F32)
            low32 = tall - high32
            low = low32.astype(BF16)
            left = jnp.concatenate([high, high, low], axis=0)
            high_p = jnp.where(is_proj, high32, 0.0).astype(BF16)
            high_o = jnp.where(is_own, high32, 0.0).astype(BF16)
            low_p = jnp.where(is_proj, low32, 0.0).astype(BF16)
            low_o = jnp.where(is_own, low32, 0.0).astype(BF16)
            right = jnp.concatenate(
                [
                    jnp.concatenate([high_p, low_p, high_p], axis=0),
                    jnp.concatenate([high_o, low_o, high_o], axis=0),
                ],
                axis=1,
            )
            both = dot(left, right, 0, 0)
            value = jnp.where(same_slot, both[:, width:], 0.0) - both[:, :width]
            out_ref[road] = value + jnp.where(first, 0.0, out_ref[road])
            added = parts[0]
            for part in parts[1:]:
                added = added + part
            held_ref[road] = added + jnp.where(first, 0.0, held_ref[road])

    return step


def edge_kernel(
    cap, bound_ref, list_ref, item_ref, recv_ref, off_ref, off_rows_ref, prior_ref,
    tiles_ref, out_ref, sums_ref, to_next_ref, to_prev_ref, words_ref, shift_ref, held_ref,
):
    roads, width = sums_ref.shape
    edge = roads // GROUPS
    lay_tiles(cap, recv_ref, off_ref, tiles_ref, words_ref, shift_ref)
    step = item_steps(list_ref, item_ref, tiles_ref, out_ref, held_ref)
    for group in (0, GROUPS - 1):
        begin, end = bound_ref[group], bound_ref[group + 1]

        def body(num, carry, begin=begin, end=end):
            step(begin, end, num)
            return carry

        lax.fori_loop(0, (end - begin + UNROLL - 1) // UNROLL, body, 0)
    sums_ref[:edge] = held_ref[:edge, SUM_ROW, :]
    sums_ref[roads - edge :] = held_ref[roads - edge :, SUM_ROW, :]
    two = 2 * EDGE
    for ref, first_block, count, first_road, first_row in (
        (to_next_ref, roads - PREV_ROADS, PREV_ROADS, roads - two, prior_ref.shape[0] - EDGE),
        (to_prev_ref, 0, NEXT_ROADS, 0, 0),
    ):
        for num in range(count):
            ref[num * width : (num + 1) * width] = out_ref[first_block + num]
        at = count * width
        ref[at : at + two] = sums_ref[first_road : first_road + two]
        ref[at + two : at + 2 * two] = off_rows_ref[first_road : first_road + two]
        ref[at + 2 * two :] = prior_ref[first_row : first_row + EDGE]


def inner_kernel(
    bound_ref, list_ref, item_ref, tiles_ref, edge_ref, edge_sums_ref,
    blocks_hbm, out_ref, sums_ref, held_ref, sems,
):
    roads, width = sums_ref.shape
    edge = roads // GROUPS
    step = item_steps(list_ref, item_ref, tiles_ref, out_ref, held_ref)
    outer = [
        pltpu.make_async_copy(
            out_ref.at[pl.ds(at, edge)], blocks_hbm.at[pl.ds(at, edge)], sems.at[num]
        )
        for num, at in enumerate((0, roads - edge))
    ]
    begin, end = bound_ref[1], bound_ref[GROUPS - 1]
    done = 0
    copies = []
    pieces = (GROUPS - 2) // 2
    for piece in range(pieces):
        group = 1 + 2 * piece
        until = (bound_ref[group + 2] - begin + UNROLL - 1) // UNROLL

        def body(num, carry):
            step(begin, end, num)
            return carry

        lax.fori_loop(done, until, body, 0)
        done = until
        where = pl.ds(group * edge, 2 * edge)
        copies.append(
            pltpu.make_async_copy(out_ref.at[where], blocks_hbm.at[where], sems.at[2 + piece])
        )
        copies[-1].start()
    for copy in outer:
        copy.start()
    sums_ref[edge : roads - edge] = held_ref[edge : roads - edge, SUM_ROW, :]
    for copy in outer + copies:
        copy.wait()
    del edge_ref, edge_sums_ref


def lane_bits(offset, bit):
    return (offset // (1 << bit)) % 2 == 1


def gathered(rows, offset, odd):
    lane = iota(rows.shape, 1)
    here = rows
    there = jnp.concatenate([rows[1:], jnp.zeros((1, LANES), F32)], axis=0)
    if odd:
        half = LANES // 2
        turned_here, turned_there = pltpu.roll(here, half, 1), pltpu.roll(there, half, 1)
        here = jnp.where(lane < LANES - half, turned_here, turned_there)
        there = turned_there
    for bit in range(3):
        step = NPAR << bit
        take = lane_bits(offset, bit)
        turned_here, turned_there = (
            pltpu.roll(here, LANES - step, 1),
            pltpu.roll(there, LANES - step, 1),
        )
        moved = jnp.where(lane < LANES - step, turned_here, turned_there)
        here = jnp.where(take, moved, here)
        there = jnp.where(take, turned_there, there)
    return here


def scattered(rows, offset, odd):
    lane = iota(rows.shape, 1)
    here, there = rows, jnp.zeros_like(rows)
    steps = [(NPAR << bit, bit) for bit in range(3)] + ([(LANES // 2, None)] if odd else [])
    for step, bit in steps:
        turned_here, turned_there = pltpu.roll(here, step, 1), pltpu.roll(there, step, 1)
        new_here = jnp.where(lane < step, 0.0, turned_here)
        new_there = jnp.where(lane < step, turned_here, turned_there)
        if bit is None:
            here, there = new_here, new_there
        else:
            take = lane_bits(offset, bit)
            here = jnp.where(take, new_here, here)
            there = jnp.where(take, new_there, there)
    return here, there


def krylov_kernel(
    held, sums_ref, off_ref, prior_ref, from_prev_ref, from_next_ref,
    first_ref, second_ref, dots_ref,
    even_sum, odd_sum, even_off, odd_off, prior, even_part, odd_part, turned_even,
    turned_odd,
):
    roads, width = sums_ref.shape
    half = roads // 2
    each = min(roads, 64)
    chunks = roads // each
    own = slice(EDGE, EDGE + half)
    two = 2 * EDGE
    at_prev = PREV_ROADS * width
    at_next = NEXT_ROADS * width
    for parity, total_sum, total_off in ((0, even_sum, even_off), (1, odd_sum, odd_off)):
        pick = lambda ref, start, count: ref[pl.ds(start + parity, count, stride=2), :]
        total_sum[0:EDGE] = pick(from_prev_ref, at_prev, EDGE)
        total_sum[own] = pick(sums_ref, 0, half)
        total_sum[EDGE + half :] = pick(from_next_ref, at_next, EDGE)
        total_off[0:EDGE] = pick(from_prev_ref, at_prev + two, EDGE).astype(jnp.int32)
        total_off[own] = pick(off_ref, 0, half).astype(jnp.int32)
        total_off[EDGE + half :] = pick(from_next_ref, at_next + two, EDGE).astype(jnp.int32)
    prior[0:EDGE] = from_prev_ref[at_prev + 2 * two : at_prev + 2 * two + EDGE]
    prior[own] = prior_ref[...]
    prior[EDGE + half :] = from_next_ref[at_next + 2 * two : at_next + 2 * two + EDGE]

    def spread(even, odd):
        even_here, even_there = scattered(even, even_off[...], False)
        odd_here, odd_there = scattered(odd, odd_off[...], True)
        over = even_there + odd_there
        return (
            even_here
            + odd_here
            + jnp.concatenate([jnp.zeros((1, LANES), F32), over[:-1]], axis=0)
        )

    def column_product(tile_at, column):
        acc = None
        for s in range(width // 8):
            term = tile_at(s) * column[s * 8 : (s + 1) * 8]
            acc = term if acc is None else acc + term
        return acc

    def apply(vector):
        even = gathered(vector, even_off[...], False)
        odd = gathered(vector, odd_off[...], True)
        even_part[...] = jnp.zeros_like(even_part)
        odd_part[...] = jnp.zeros_like(odd_part)
        edge_even = jnp.concatenate(
            [even[:EDGE], even[EDGE + half :], jnp.zeros((LANES - 2 * EDGE, LANES), F32)], axis=0
        ).T
        edge_odd = jnp.concatenate(
            [odd[:EDGE], odd[EDGE + half :], jnp.zeros((LANES - 2 * EDGE, LANES), F32)], axis=0
        ).T
        for num in range(PREV_ROADS):
            row = EDGE - PREV_ROADS // 2 + num // 2
            column = (edge_even if num % 2 == 0 else edge_odd)[:, row : row + 1]
            part = even_part if num % 2 == 0 else odd_part
            part[row] = column_product(
                lambda s, num=num: from_prev_ref[num * width + s * 8 : num * width + s * 8 + 8],
                column,
            )
        for num in range(NEXT_ROADS):
            column = (edge_even if num % 2 == 0 else edge_odd)[:, EDGE : EDGE + 1]
            part = even_part if num % 2 == 0 else odd_part
            part[EDGE + half] = column_product(
                lambda s, num=num: from_next_ref[num * width + s * 8 : num * width + s * 8 + 8],
                column,
            )
        turned_even[:, :half] = even[own].T
        turned_odd[:, :half] = odd[own].T
        per = each // 2

        copies_of = iota((3 * per, per * width), 0) % per == iota((3 * per, per * width), 1) // width
        copies_of = jnp.where(copies_of, 1.0, 0.0).astype(BF16)

        def chunk(c, carry):
            columns_even = turned_even[...]
            columns_odd = turned_odd[...]
            spread_odd = dot(
                jnp.concatenate(split_three(columns_odd[:, :per]), axis=1), copies_of, 1, 0
            )
            for j in range(per):
                road = c * each + 2 * j
                even_part[EDGE + c * per + j] = column_product(
                    lambda s, road=road: held[road, s * 8 : s * 8 + 8, :],
                    columns_even[:, j : j + 1],
                )
                odd_part[EDGE + c * per + j] = column_product(
                    lambda s, road=road: held[road + 1, s * 8 : s * 8 + 8, :],
                    spread_odd[:, j * width : (j + 1) * width],
                )
            turned_even[...] = pltpu.roll(columns_even, columns_even.shape[1] - per, 1)
            turned_odd[...] = pltpu.roll(columns_odd, columns_odd.shape[1] - per, 1)
            return carry

        lax.fori_loop(0, chunks, chunk, 0)
        even = even_part[:, 0, :]
        odd = odd_part[:, 0, :]
        for k in range(1, 8):
            even = even + even_part[:, k, :]
            odd = odd + odd_part[:, k, :]
        return prior[...] * vector + spread(even, odd)

    first = spread(even_sum[...], odd_sum[...])
    second = apply(first)
    third = apply(second)
    first, second, third = first[own], second[own], third[own]
    first_ref[...] = first
    second_ref[...] = second
    lane = iota(dots_ref.shape, 2)
    dots = jnp.zeros(dots_ref.shape, F32)
    pairs = ((first, first), (first, second), (second, second), (second, third), (third, third))
    for num, (one, other) in enumerate(pairs):
        dots = dots + jnp.where(lane == num, jnp.sum(one * other), 0.0)
    dots_ref[...] = dots


def finish_kernel(dots_ref, first_ref, second_ref, out_hbm, out_ref, sem):
    sums = jnp.sum(dots_ref[...], axis=0, keepdims=True)
    s00, s01, s11, s12, s22 = (sums[:, num : num + 1] for num in range(5))
    square_one = s00 + EPS
    beta_one = jnp.sqrt(square_one)
    alpha_one = s01 / square_one
    square_two = (s11 - 2.0 * alpha_one * s01 + alpha_one * alpha_one * s00) / square_one + EPS
    beta_two = jnp.sqrt(square_two)
    scale = 1.0 / (beta_one * beta_two)
    s02 = s11
    cross = s12 - alpha_one * s11 - square_two * s01
    cross = cross - alpha_one * (s02 - alpha_one * s01 - square_two * s00)
    alpha_two = cross * scale * scale
    near = alpha_one + alpha_two
    far = alpha_one * alpha_two - square_two
    square_three = s22 - 2.0 * near * s12 + near * near * s11
    square_three = square_three + 2.0 * far * s02 - 2.0 * near * far * s01 + far * far * s00
    square_three = square_three * scale * scale + EPS
    entry_first = alpha_one * alpha_one + square_two
    entry_cross = beta_two * near
    entry_second = square_two + alpha_two * alpha_two + square_three
    determinant = entry_first * entry_second - entry_cross * entry_cross
    coef_one = beta_one * (entry_second * alpha_one - entry_cross * beta_two) / determinant
    coef_two = beta_one * (entry_first * beta_two - entry_cross * alpha_one) / determinant
    on_second = coef_two * scale
    on_first = coef_one / beta_one - alpha_one * on_second
    out_ref[...] = on_first * first_ref[...] + on_second * second_ref[...]
    copy = pltpu.make_async_copy(out_ref, out_hbm, sem)
    copy.start()
    copy.wait()


def neighbour(value, steps):
    count = lax.axis_size(AXES)
    return lax.ppermute(value, AXES, [(s, (s + steps) % count) for s in range(count)])


def shape(*dims, dtype=F32):
    return jax.ShapeDtypeStruct(dims, dtype)


def on_device(
    local_deriv, global_deriv, measured, hit_weight, hit_module, hit_count, track_road, road_start,
    prior_weight,
):
    devices = lax.axis_size(AXES)
    roads = road_start.shape[0]
    tracks = hit_count.shape[0]
    modules = prior_weight.shape[0]
    cap = 4 * tracks // devices
    slots = devices * cap
    width = ROAD * NPAR
    half = modules // ROAD
    vmem = pl.BlockSpec(memory_space=pltpu.VMEM)
    smem = pl.BlockSpec(memory_space=pltpu.SMEM)
    limit = pltpu.CompilerParams(vmem_limit_bytes=32 * 1024 * 1024)
    large = pltpu.CompilerParams(vmem_limit_bytes=LARGE * 1024 * 1024)
    small = pltpu.CompilerParams(vmem_limit_bytes=12 * 1024 * 1024)

    sent = (
        local_deriv, jnp.transpose(global_deriv, (1, 0, 2)), measured, hit_weight, hit_module,
        hit_count[None, :], track_road[None, :],
    )
    message = (devices * USED, LANES) if folded(cap) else (ROWS, slots)
    send = pl.pallas_call(
        functools.partial(pack_kernel, cap, roads, modules * devices),
        out_shape=shape(*message),
        in_specs=[pl.BlockSpec(memory_space=pltpu.HBM)] * len(sent),
        out_specs=vmem,
        scratch_shapes=[
            pltpu.VMEM((ROWS, tracks), F32),
            pltpu.VMEM((3 * ROWS, tracks), BF16),
            pltpu.VMEM((NHIT, 8, tracks), F32),
            pltpu.VMEM((NHIT, 8, tracks), F32),
            pltpu.VMEM((slots, tracks), BF16),
            *(pltpu.VMEM(x.shape, x.dtype) for x in sent),
            pltpu.SemaphoreType.DMA((len(sent),)),
        ],
        compiler_params=large,
        name="fit_and_pack",
    )(*sent)
    if folded(cap):
        send = send.reshape(devices, USED, 1, LANES)
    else:
        send = jnp.transpose(send.reshape(ROWS, devices, cap), (1, 0, 2))
    recv = lax.all_to_all(send, AXES, split_axis=0, concat_axis=0, tiled=True)
    if folded(cap):
        recv = recv.reshape(message)
    else:
        recv = jnp.transpose(recv, (1, 0, 2)).reshape(message)

    offset = road_start % (ROAD // 2)
    list_rows = ((PER_ITEM * roads + slots) // (8 * LANES) + 1) * 8
    item_rows = -(-(list_rows * LANES // PER_ITEM) // (8 * LANES)) * 8
    track_list, items, bounds, track_off = pl.pallas_call(
        functools.partial(sort_kernel, cap),
        out_shape=(
            shape(list_rows, LANES, dtype=jnp.int32),
            shape(item_rows, LANES, dtype=jnp.int32),
            shape(8, LANES, dtype=jnp.int32),
            shape(slots // LANES, LANES),
        ),
        in_specs=[vmem] * 2,
        out_specs=(vmem,) * 4,
        scratch_shapes=[pltpu.VMEM((slots // LANES, LANES), F32)],
        compiler_params=limit,
        name="sort_by_road",
    )(recv, offset.astype(F32)[:, None])

    edge = roads // GROUPS
    prior = prior_weight.reshape(half, width)
    off_rows = jnp.broadcast_to(offset.astype(F32)[:, None], (roads, LANES))
    lists = (bounds.reshape(-1), track_list.reshape(-1), items.reshape(-1))
    halo = 4 * EDGE + EDGE
    tiles, edge_blocks, edge_sums, to_next, to_prev = pl.pallas_call(
        functools.partial(edge_kernel, cap),
        out_shape=(
            shape(slots + 8, 8, width), shape(roads, width, width), shape(roads, width),
            shape(PREV_ROADS * width + halo, width), shape(NEXT_ROADS * width + halo, width),
        ),
        in_specs=[smem] * 3 + [vmem] * 4,
        out_specs=(vmem,) * 5,
        scratch_shapes=[
            pltpu.VMEM((2, ROWS, LANES), F32),
            pltpu.VMEM((2, 8 + ROAD, LANES), F32),
            pltpu.VMEM((roads, 8, width), F32),
        ],
        compiler_params=small,
        name="lay_and_assemble_edges",
    )(*lists, recv, track_off, off_rows, prior)
    from_prev = neighbour(to_next, 1)
    from_next = neighbour(to_prev, -1)
    normal_blocks, held_blocks, sums = pl.pallas_call(
        inner_kernel,
        out_shape=(
            shape(roads, width, width), shape(roads, width, width), shape(roads, width),
        ),
        in_specs=[smem] * 3 + [vmem] * 3,
        out_specs=(pl.BlockSpec(memory_space=pltpu.HBM), vmem, vmem),
        scratch_shapes=[
            pltpu.VMEM((roads, 8, width), F32),
            pltpu.SemaphoreType.DMA((2 + (GROUPS - 2) // 2,)),
        ],
        input_output_aliases={4: 1, 5: 2},
        compiler_params=small,
        name="assemble_blocks",
    )(*lists, tiles, edge_blocks, edge_sums)

    total = half + 2 * EDGE
    rows = pltpu.VMEM((total, LANES), F32)
    int_rows = pltpu.VMEM((total, LANES), jnp.int32)
    parts = pltpu.VMEM((total, 8, LANES), F32)
    turned = pltpu.VMEM((LANES, LANES), F32)
    first, second, dots = pl.pallas_call(
        krylov_kernel,
        out_shape=(shape(half, width), shape(half, width), shape(devices, 1, LANES)),
        in_specs=[vmem] * 6,
        out_specs=(vmem,) * 3,
        scratch_shapes=[rows, rows, int_rows, int_rows, rows, parts, parts, turned, turned],
        compiler_params=small,
        name="two_products",
    )(held_blocks, sums, off_rows, prior, from_prev, from_next)
    everyone = lax.all_to_all(dots, AXES, split_axis=0, concat_axis=0, tiled=True)
    rhs = first.reshape(modules, NPAR)
    summed = (everyone.reshape(devices, LANES), rhs.T, second.reshape(modules, NPAR).T)
    corrections = pl.pallas_call(
        finish_kernel,
        out_shape=shape(NPAR, modules),
        in_specs=[vmem] * 3,
        out_specs=pl.BlockSpec(memory_space=pltpu.HBM),
        scratch_shapes=[pltpu.VMEM((NPAR, modules), F32), pltpu.SemaphoreType.DMA],
        compiler_params=pltpu.CompilerParams(vmem_limit_bytes=4 * 1024 * 1024),
        name="combine",
    )(*summed)
    return (normal_blocks, rhs, corrections.T)


def solution(mesh):
    track = P(None, None, AXES)
    in_specs = (
        track, track, P(None, AXES), P(None, AXES), P(None, AXES), P(AXES), P(AXES), P(AXES),
        P(AXES, None),
    )
    out_specs = (P(AXES, None, None), P(AXES, None), P(AXES, None))
    return jax.shard_map(
        on_device, mesh=mesh, in_specs=in_specs, out_specs=out_specs, check_vma=False
    )
```

```python
import functools

import jax
import jax.numpy as jnp
from jax import lax
from jax.experimental import pallas as pl
from jax.experimental.pallas import tpu as pltpu
from jax.sharding import PartitionSpec as P

NPAR = 8
NHIT = 12
NLOC = 5
ROAD = 16
LANES = 128
EPS = 1e-06
AXES = ("trk", "mod")

PART = 88
USED = 82
R_ROAD = 10 * NPAR
R_FIRST = R_ROAD + 1
R_SOLVED = PART + 2 * NPAR
R_GAP = R_SOLVED + NHIT
GAPS = ROAD - NHIT
R_PROJ = [R_GAP + GAPS + a * NHIT - a * (a - 1) // 2 for a in range(NLOC)]
ROWS = 2 * PART


def derivative_row(hit):
    return hit * NPAR if hit < 10 else PART + (hit - 10) * NPAR


LARGE = 60
PER_ITEM = 8
UNROLL = 16
GROUPS = 16
SUM_ROW = NLOC + 1
EDGE = 8
NEXT_ROADS = 2
PREV_ROADS = 4
F32 = jnp.float32
BF16 = jnp.bfloat16


def iota(shape, dim):
    return lax.broadcasted_iota(jnp.int32, shape, dim)


def dot(lhs, rhs, lhs_dim, rhs_dim):
    return lax.dot_general(
        lhs, rhs, (((lhs_dim,), (rhs_dim,)), ((), ())), preferred_element_type=F32
    )


def split_two(value):
    high = value.astype(BF16)
    return high, (value - high.astype(F32)).astype(BF16)


def householder(rows, first, column):
    vector = [row[column : column + 1] for row in rows[first:]]
    norm = jnp.sqrt(sum(part * part for part in vector))
    vector[0] = vector[0] + jnp.where(vector[0] >= 0.0, norm, -norm)
    square = sum(part * part for part in vector)
    scale = jnp.where(square > 1e-30, 2.0 / jnp.maximum(square, 1e-30), 0.0)
    along = sum(part * row for part, row in zip(vector, rows[first:])) * scale
    return rows[:first] + [row - part * along for part, row in zip(vector, rows[first:])]


def place_tracks(cap, road_dev, track_road, hot_ref):
    tracks = track_road.shape[1]
    owner = track_road // road_dev
    owner_col = jnp.concatenate(
        [
            jnp.broadcast_to(owner[:, at : at + LANES], (LANES, LANES)).astype(F32).T[:, :1]
            for at in range(0, tracks, LANES)
        ],
        axis=0,
    ).astype(jnp.int32)
    earlier = iota((tracks, tracks), 0) < iota((tracks, tracks), 1)
    same = jnp.where(jnp.logical_and(owner_col == owner, earlier), 1.0, 0.0)
    rank = jnp.sum(same, axis=0, keepdims=True).astype(jnp.int32)
    target = owner * cap + rank
    step = 2 * LANES
    for at in range(0, hot_ref.shape[0], step):
        hot = jnp.where(target == iota((step, tracks), 0) + at, 1.0, 0.0)
        hot_ref[at : at + step, :] = hot.astype(BF16)


def pack_kernel(
    cap, road_dev, module_count, ld_hbm, gd_hbm, me_hbm, hw_hbm, hm_hbm, hc_hbm, tr_hbm,
    out_ref, words_ref, parts_ref, mixed_ref, sorted_ref, hot_ref,
    ld_ref, gd_ref, me_ref, hw_ref, hm_ref, hc_ref, tr_ref, sems,
):
    sources = (tr_hbm, hc_hbm, hw_hbm, ld_hbm, me_hbm, hm_hbm, gd_hbm)
    targets = (tr_ref, hc_ref, hw_ref, ld_ref, me_ref, hm_ref, gd_ref)
    copies = [
        pltpu.make_async_copy(source, target, sems.at[num])
        for num, (source, target) in enumerate(zip(sources, targets))
    ]
    for copy in copies:
        copy.start()
    copies[0].wait()
    place_tracks(cap, road_dev, tr_ref[...], hot_ref)
    for copy in copies[1:]:
        copy.wait()
    tracks = tr_ref.shape[1]
    weight = jnp.where(iota((NHIT, tracks), 0) < hc_ref[...], hw_ref[...], 0.0)
    root = jnp.sqrt(weight)
    ahead = hm_ref[...] - tr_ref[...] * (ROAD // 2)
    ahead = jnp.where(ahead < 0, ahead + module_count, ahead).astype(F32)
    order = jnp.zeros((NHIT, tracks), F32)
    for i in range(NHIT):
        order = order + jnp.where(ahead[i : i + 1] < ahead, 1.0, 0.0)
    for a in range(NLOC):
        mixed_ref[:, a, :] = ld_ref[a] * root
    mixed_ref[:, NLOC, :] = me_ref[...] * root
    mixed_ref[:, NLOC + 1, :] = ahead
    mixed_ref[:, NLOC + 2, :] = order
    for at in range(0, tracks, LANES):
        lanes = slice(at, at + LANES)
        tiles = [mixed_ref[i, :, lanes] for i in range(NHIT)]
        places = [jnp.broadcast_to(tile[NLOC + 2 : NLOC + 3], (8, LANES)) for tile in tiles]
        derivs = [gd_ref[i, :, lanes] * root[i : i + 1, lanes] for i in range(NHIT)]
        for k in range(NHIT):
            tile, deriv = tiles[0], derivs[0]
            for i in range(1, NHIT):
                here = places[i] == float(k)
                tile = jnp.where(here, tiles[i], tile)
                deriv = jnp.where(here, derivs[i], deriv)
            sorted_ref[k, :, lanes] = tile
            row = derivative_row(k)
            words_ref[row : row + NPAR, lanes] = deriv
    scaled = [sorted_ref[:, a, :] for a in range(NLOC)]
    factor = {}
    for a in range(NLOC):
        for b in range(a + 1):
            running = jnp.sum(scaled[a] * scaled[b], axis=0, keepdims=True)
            if a == b:
                running = running + 1.0
            for c in range(b):
                running = running - factor[a, c] * factor[b, c]
            factor[a, b] = jnp.sqrt(running) if a == b else running / factor[b, b]
    proj = []
    for a in range(NLOC):
        running = scaled[a]
        for b in range(a):
            running = running - factor[a, b] * proj[b]
        proj.append(running / factor[a, a])
    residual = sorted_ref[:, NLOC, :]
    solved = residual
    for a in range(NLOC):
        solved = solved - proj[a] * jnp.sum(proj[a] * residual, axis=0, keepdims=True)
    for a in range(NLOC - 1):
        proj = householder(proj, a, a)
    ahead = sorted_ref[:, NLOC + 1, :]
    skipped = ahead - ahead[0:1] - iota((NHIT, tracks), 0).astype(F32)
    words_ref[R_ROAD:R_FIRST, :] = (tr_ref[...] % road_dev + 1).astype(F32)
    words_ref[R_FIRST:USED, :] = ahead[0:1]
    words_ref[USED:PART, :] = jnp.zeros((PART - USED, tracks), F32)
    words_ref[R_SOLVED:R_GAP, :] = solved
    for gap in range(GAPS):
        words_ref[R_GAP + gap : R_GAP + gap + 1, :] = jnp.sum(
            jnp.where(skipped < gap + 0.5, 1.0, 0.0), axis=0, keepdims=True
        )
    for a in range(NLOC):
        words_ref[R_PROJ[a] : R_PROJ[a] + NHIT - a, :] = proj[a][a:]
    words_ref[PART + USED :, :] = jnp.zeros((PART - USED, tracks), F32)
    for num, part in enumerate(split_two(words_ref[...])):
        parts_ref[num * ROWS : (num + 1) * ROWS, :] = part
    lower_half = iota((USED, LANES), 1) < LANES // 2
    step = 2 * LANES
    for at in range(0, hot_ref.shape[0], step):
        moved = dot(parts_ref[...], hot_ref[at : at + step, :], 1, 1)
        moved = moved[:ROWS] + moved[ROWS:]
        if not folded(cap):
            out_ref[:, at : at + step] = moved
            continue
        for sub in range(2):
            lanes = slice(sub * LANES, (sub + 1) * LANES)
            one = moved[:USED, lanes]
            two = moved[PART : PART + USED, lanes]
            row = (at // LANES + sub) * 2 * USED
            out_ref[row : row + USED] = jnp.where(lower_half, one, pltpu.roll(two, LANES // 2, 1))
            out_ref[row + USED : row + 2 * USED] = jnp.where(
                lower_half, pltpu.roll(one, LANES // 2, 1), two
            )


def folded(cap):
    return 2 * cap == LANES


def sort_kernel(cap, recv_ref, off_ref, list_ref, item_ref, bound_ref, off_out_ref, road_ref):
    roads = off_ref.shape[0]
    blocks = road_ref.shape[0]
    if folded(cap):
        even = recv_ref[pl.ds(R_ROAD, blocks, stride=2 * USED), :]
        odd = recv_ref[pl.ds(R_ROAD + USED, blocks, stride=2 * USED), :]
        lower_half = iota((blocks, LANES), 1) < LANES // 2
        road_ref[...] = jnp.where(lower_half, even, pltpu.roll(odd, LANES // 2, 1))
    else:
        for e in range(blocks):
            road_ref[e : e + 1, :] = recv_ref[R_ROAD : R_ROAD + 1, e * LANES : (e + 1) * LANES]
    road_num = (iota((roads, LANES), 0) + 1).astype(F32)
    upper = jnp.where(iota((LANES, LANES), 0) < iota((LANES, LANES), 1), 1.0, 0.0).astype(BF16)
    offset = off_ref[...]
    counts = jnp.zeros((roads, 1), F32)
    ranks = []
    for e in range(blocks):
        hot = jnp.where(road_ref[e : e + 1, :] == road_num, 1.0, 0.0)
        before = dot(hot.astype(BF16), upper, 1, 0) + counts
        ranks.append(jnp.sum(hot * before, axis=0, keepdims=True))
        off_out_ref[e : e + 1, :] = jnp.sum(hot * offset, axis=0, keepdims=True)
        counts = counts + jnp.sum(hot, axis=1, keepdims=True)
    items = jnp.maximum(jnp.floor((counts + (PER_ITEM - 1)) * (1.0 / PER_ITEM)), 1.0)
    items = jnp.broadcast_to(items, (roads, LANES))
    lower = jnp.where(iota((roads, roads), 1) < iota((roads, roads), 0), 1.0, 0.0).astype(BF16)
    begin = dot(lower, items.astype(BF16), 1, 0)
    rows = list_ref.shape[0]
    total = jnp.zeros((rows, 2 * LANES), F32)
    row_num = iota((rows, LANES), 0).astype(F32)
    lane_num = iota((LANES, LANES), 0).astype(F32)
    track_lane = iota((1, LANES), 1).astype(F32)
    for e in range(blocks):
        road = road_ref[e : e + 1, :]
        hot = jnp.where(road == road_num, 1.0, 0.0)
        place = PER_ITEM * jnp.sum(hot * begin, axis=0, keepdims=True) + ranks[e]
        place = jnp.where(road > 0.5, place, -1.0)
        high = jnp.floor(place * (1.0 / LANES))
        low = place - high * LANES
        pick = jnp.where(high == row_num, 1.0, 0.0).astype(BF16)
        match = low == lane_num
        values = jnp.concatenate(
            [jnp.where(match, float(e + 1), 0.0), jnp.where(match, track_lane, 0.0)], axis=0
        )
        total = total + dot(pick, values.astype(BF16), 1, 1)
    found = total[:, :LANES]
    track = jnp.where(found > 0.5, (found - 1.0) * LANES + total[:, LANES:], float(blocks * LANES))
    list_ref[...] = track.astype(jnp.int32)
    item_rows = item_ref.shape[0]
    for row in range(item_rows):
        item = (iota((1, LANES), 1) + row * LANES).astype(F32)
        road = jnp.sum(jnp.where(begin <= item, 1.0, 0.0), axis=0, keepdims=True) - 1.0
        first = jnp.sum(jnp.where(begin == item, 1.0, 0.0), axis=0, keepdims=True)
        item_ref[row : row + 1, :] = (2.0 * road + first).astype(jnp.int32)
    each = roads // GROUPS
    begins = jnp.where(iota((roads, LANES), 0) == iota((roads, LANES), 1) * each, begin, 0.0)
    bound = jnp.sum(begins, axis=0, keepdims=True)
    last = jnp.sum(items, axis=0, keepdims=True)
    bound = jnp.where(iota((1, LANES), 1) < GROUPS, bound, last)
    bound_ref[...] = jnp.broadcast_to(bound, bound_ref.shape).astype(jnp.int32)


def lay_tiles(cap, recv_ref, off_ref, tiles_ref, words_ref, shift_ref):
    blocks = off_ref.shape[0]
    width = ROAD * NPAR
    lower_half = iota((USED, LANES), 1) < LANES // 2
    slot_num = iota((ROAD, LANES), 0)
    tiles_ref[blocks * LANES] = jnp.zeros((8, width), F32)
    shift_ref[:, :8, :] = jnp.full((2, 8, LANES), -1.0, F32)

    def lay(num, held):
        words = words_ref.at[held]
        shifts = shift_ref.at[held]
        e = 2 * num + held
        if folded(cap):
            both = recv_ref.at[pl.ds(pl.multiple_of(num * 4 * USED, 8), 4 * USED)]
            one = both[held * 2 * USED : held * 2 * USED + USED, :]
            two = both[held * 2 * USED + USED : held * 2 * USED + 2 * USED, :]
            words[:USED] = jnp.where(lower_half, one, pltpu.roll(two, LANES // 2, 1))
            words[PART : PART + USED] = jnp.where(lower_half, pltpu.roll(one, LANES // 2, 1), two)
        else:
            words[...] = recv_ref[:, pl.ds(pl.multiple_of(e * LANES, LANES), LANES)]
        shift = words[R_FIRST : R_FIRST + 1, :] - off_ref[pl.ds(e, 1), :]
        for gap in range(GAPS):
            reached = slot_num.astype(F32) >= words[R_GAP + gap : R_GAP + gap + 1, :]
            shift = shift + jnp.where(reached, 1.0, 0.0)
        shifts[8 : 8 + ROAD] = jnp.where(slot_num < NHIT, shift, -1.0)
        laid = [jnp.zeros((NPAR, LANES), F32) for s in range(ROAD)]
        for i in range(NHIT):
            row = derivative_row(i)
            value = words[row : row + NPAR, :]
            wide = jnp.broadcast_to(shifts[8 + i : 9 + i, :], (NPAR, LANES))
            for move in range(GAPS + 1):
                laid[i + move] = jnp.where(wide == float(move), value, laid[i + move])
        placed = [jnp.zeros((ROAD, LANES), F32) for a in range(NLOC + 1)]
        for move in range(GAPS + 1):
            match = shifts[8 - move : 8 - move + ROAD, :] == float(move)
            for a in range(NLOC + 1):
                if a == NLOC:
                    row, valid = R_SOLVED - move, match
                else:
                    row = R_PROJ[a] - a - move
                    valid = jnp.logical_and(match, slot_num >= a + move) if a else match
                placed[a] = jnp.where(valid, words[row : row + ROAD, :], placed[a])
        start = pl.multiple_of(e * LANES, LANES)
        for a in range(NLOC + 1):
            mixed = jnp.concatenate([laid[s] * placed[a][s : s + 1] for s in range(ROAD)], axis=0)
            tiles_ref[pl.ds(start, LANES), a if a < NLOC else SUM_ROW, :] = mixed.T
        tiles_ref[pl.ds(start, LANES), NLOC, :] = jnp.concatenate(laid, axis=0).T
        tiles_ref[pl.ds(start, LANES), SUM_ROW + 1, :] = jnp.zeros((LANES, width), F32)

    def lay_two(num, carry):
        lay(num, 0)
        lay(num, 1)
        return carry

    lax.fori_loop(0, blocks // 2, lay_two, 0)


def item_steps(list_ref, item_ref, tiles_ref, out_ref, held_ref):
    width = ROAD * NPAR
    row_kind = iota((PER_ITEM * 8, width), 0) % 8
    proj = jnp.where(row_kind < NLOC, 1.0, 0.0).astype(BF16)
    own = jnp.where(row_kind == NLOC, 1.0, 0.0).astype(BF16)
    same_slot = iota((width, width), 0) // NPAR == iota((width, width), 1) // NPAR
    spare = list_ref.shape[0] // PER_ITEM - 1

    def step(item_at, count, num):
        for u in range(UNROLL):
            item = num * UNROLL + u
            live = item < count
            item = jnp.where(live, item_at(item), spare)
            info = item_ref[item]
            first = (info & 1) == 1
            road = jnp.where(live, info >> 1, 0)
            at = item * PER_ITEM
            parts = [tiles_ref[list_ref[at + j]] for j in range(PER_ITEM)]
            tall = jnp.concatenate(parts, axis=0)
            high, low = split_two(tall)
            left = jnp.concatenate([high, high, low], axis=0)
            high_p, low_p, high_o, low_o = high * proj, low * proj, high * own, low * own
            right = jnp.concatenate(
                [
                    jnp.concatenate([high_p, low_p, high_p], axis=0),
                    jnp.concatenate([high_o, low_o, high_o], axis=0),
                ],
                axis=1,
            )
            both = dot(left, right, 0, 0)
            value = jnp.where(same_slot, both[:, width:], 0.0) - both[:, :width]
            out_ref[road] = value + jnp.where(first, 0.0, out_ref[road])
            added = parts[0]
            for part in parts[1:]:
                added = added + part
            held_ref[road] = added + jnp.where(first, 0.0, held_ref[road])

    return step


def edge_kernel(
    cap, bound_ref, list_ref, item_ref, recv_ref, off_ref, off_rows_ref, prior_ref,
    tiles_ref, out_ref, sums_ref, to_next_ref, to_prev_ref, words_ref, shift_ref, held_ref,
):
    roads, width = sums_ref.shape
    edge = roads // GROUPS
    lay_tiles(cap, recv_ref, off_ref, tiles_ref, words_ref, shift_ref)
    step = item_steps(list_ref, item_ref, tiles_ref, out_ref, held_ref)
    low = bound_ref[1]
    high = bound_ref[GROUPS - 1]
    count = low + bound_ref[GROUPS] - high

    def body(num, carry):
        step(lambda item: jnp.where(item < low, item, item - low + high), count, num)
        return carry

    lax.fori_loop(0, (count + UNROLL - 1) // UNROLL, body, 0)
    sums_ref[:edge] = held_ref[:edge, SUM_ROW, :]
    sums_ref[roads - edge :] = held_ref[roads - edge :, SUM_ROW, :]
    two = 2 * EDGE
    for ref, first_block, count, first_road, first_row in (
        (to_next_ref, roads - PREV_ROADS, PREV_ROADS, roads - two, prior_ref.shape[0] - EDGE),
        (to_prev_ref, 0, NEXT_ROADS, 0, 0),
    ):
        for num in range(count):
            ref[num * width : (num + 1) * width] = out_ref[first_block + num]
        at = count * width
        ref[at : at + two] = sums_ref[first_road : first_road + two]
        ref[at + two : at + 2 * two] = off_rows_ref[first_road : first_road + two]
        ref[at + 2 * two :] = prior_ref[first_row : first_row + EDGE]


def inner_kernel(
    bound_ref, list_ref, item_ref, tiles_ref, edge_ref, edge_sums_ref,
    blocks_hbm, out_ref, sums_ref, held_ref, sems,
):
    roads, width = sums_ref.shape
    edge = roads // GROUPS
    step = item_steps(list_ref, item_ref, tiles_ref, out_ref, held_ref)
    outer = [
        pltpu.make_async_copy(
            out_ref.at[pl.ds(at, edge)], blocks_hbm.at[pl.ds(at, edge)], sems.at[num]
        )
        for num, at in enumerate((0, roads - edge))
    ]
    begin, end = bound_ref[1], bound_ref[GROUPS - 1]
    done = 0
    copies = []
    pieces = (GROUPS - 2) // 2
    for piece in range(pieces):
        group = 1 + 2 * piece
        until = (bound_ref[group + 2] - begin + UNROLL - 1) // UNROLL

        def body(num, carry):
            step(lambda item: item + begin, end - begin, num)
            return carry

        lax.fori_loop(done, until, body, 0)
        done = until
        where = pl.ds(group * edge, 2 * edge)
        copies.append(
            pltpu.make_async_copy(out_ref.at[where], blocks_hbm.at[where], sems.at[2 + piece])
        )
        copies[-1].start()
    for copy in outer:
        copy.start()
    sums_ref[edge : roads - edge] = held_ref[edge : roads - edge, SUM_ROW, :]
    for copy in outer + copies:
        copy.wait()
    del edge_ref, edge_sums_ref


def lane_bits(offset, bit):
    return (offset // (1 << bit)) % 2 == 1


def gathered(rows, offset, odd):
    lane = iota(rows.shape, 1)
    here = rows
    there = jnp.concatenate([rows[1:], jnp.zeros((1, LANES), F32)], axis=0)
    if odd:
        half = LANES // 2
        turned_here, turned_there = pltpu.roll(here, half, 1), pltpu.roll(there, half, 1)
        here = jnp.where(lane < LANES - half, turned_here, turned_there)
        there = turned_there
    for bit in range(3):
        step = NPAR << bit
        take = lane_bits(offset, bit)
        turned_here, turned_there = (
            pltpu.roll(here, LANES - step, 1),
            pltpu.roll(there, LANES - step, 1),
        )
        moved = jnp.where(lane < LANES - step, turned_here, turned_there)
        here = jnp.where(take, moved, here)
        there = jnp.where(take, turned_there, there)
    return here


def scattered(rows, offset, odd):
    lane = iota(rows.shape, 1)
    here, there = rows, jnp.zeros_like(rows)
    steps = [(NPAR << bit, bit) for bit in range(3)] + ([(LANES // 2, None)] if odd else [])
    for step, bit in steps:
        turned_here, turned_there = pltpu.roll(here, step, 1), pltpu.roll(there, step, 1)
        new_here = jnp.where(lane < step, 0.0, turned_here)
        new_there = jnp.where(lane < step, turned_here, turned_there)
        if bit is None:
            here, there = new_here, new_there
        else:
            take = lane_bits(offset, bit)
            here = jnp.where(take, new_here, here)
            there = jnp.where(take, new_there, there)
    return here, there


def krylov_kernel(
    held, sums_ref, off_ref, prior_ref, from_prev_ref, from_next_ref,
    first_ref, second_ref, dots_ref,
    even_sum, odd_sum, even_off, odd_off, prior, even_part, odd_part, held_halves, edge_halves,
):
    roads, width = sums_ref.shape
    half = roads // 2
    own = slice(EDGE, EDGE + half)
    two = 2 * EDGE
    at_prev = PREV_ROADS * width
    at_next = NEXT_ROADS * width
    for parity, total_sum, total_off in ((0, even_sum, even_off), (1, odd_sum, odd_off)):
        pick = lambda ref, start, count: ref[pl.ds(start + parity, count, stride=2), :]
        total_sum[0:EDGE] = pick(from_prev_ref, at_prev, EDGE)
        total_sum[own] = pick(sums_ref, 0, half)
        total_sum[EDGE + half :] = pick(from_next_ref, at_next, EDGE)
        total_off[0:EDGE] = pick(from_prev_ref, at_prev + two, EDGE).astype(jnp.int32)
        total_off[own] = pick(off_ref, 0, half).astype(jnp.int32)
        total_off[EDGE + half :] = pick(from_next_ref, at_next + two, EDGE).astype(jnp.int32)
    prior[0:EDGE] = from_prev_ref[at_prev + 2 * two : at_prev + 2 * two + EDGE]
    prior[own] = prior_ref[...]
    prior[EDGE + half :] = from_next_ref[at_next + 2 * two : at_next + 2 * two + EDGE]

    def spread(even, odd):
        even_here, even_there = scattered(even, even_off[...], False)
        odd_here, odd_there = scattered(odd, odd_off[...], True)
        over = even_there + odd_there
        return (
            even_here
            + odd_here
            + jnp.concatenate([jnp.zeros((1, LANES), F32), over[:-1]], axis=0)
        )

    def row_products(rows, tiles_at):
        lane_block = iota((8, 8 * width), 1) // width
        diagonal = lane_block == iota((8, 8 * width), 0)
        left = jnp.concatenate(
            [jnp.where(diagonal, jnp.concatenate([part.astype(F32)] * 8, axis=1), 0.0)
             for part in split_two(rows)],
            axis=0,
        ).astype(BF16)
        right = jnp.concatenate([tiles_at(k) for k in range(8)], axis=0)
        both = dot(left, right, 1, 0)
        both = both[:, :width] + both[:, width:]
        return both[:8] + both[8:]

    def halves(block):
        return jnp.concatenate(split_two(block), axis=1)

    edge_blocks = [(from_prev_ref, num) for num in range(PREV_ROADS)]
    edge_blocks += [(from_next_ref, num) for num in range(NEXT_ROADS)]
    edge_blocks += edge_blocks[:2]
    edge_rows = [(EDGE - PREV_ROADS // 2 + num // 2, num % 2) for num in range(PREV_ROADS)]
    edge_rows += [(EDGE + half, num) for num in range(NEXT_ROADS)]

    def apply(vector, again):
        even_part[...] = gathered(vector, even_off[...], False)
        odd_part[...] = gathered(vector, odd_off[...], True)
        outer = [(odd_part if odd else even_part)[row : row + 1, :] for row, odd in edge_rows]
        outer = jnp.concatenate(outer + [jnp.zeros((2, LANES), F32)], axis=0)

        def edge_tile(k):
            if again:
                return edge_halves[k]
            ref, num = edge_blocks[k]
            edge_halves[k] = halves(ref[num * width : (num + 1) * width, :])
            return edge_halves[k]

        outer = row_products(outer, edge_tile)
        for part, parity in ((even_part, 0), (odd_part, 1)):
            part[EDGE + half :, :] = jnp.zeros((EDGE, LANES), F32)
            part[:EDGE, :] = jnp.zeros((EDGE, LANES), F32)
        for num, (row, odd) in enumerate(edge_rows):
            (odd_part if odd else even_part)[row : row + 1, :] = outer[num : num + 1]

        def chunk(c, carry):
            for part, parity in ((even_part, 0), (odd_part, 1)):
                where = pl.ds(pl.multiple_of(EDGE + c * 8, 8), 8)

                def tile(k, parity=parity):
                    road = c * 16 + 2 * k + parity
                    if not again:
                        held_halves[road] = halves(held[road])
                    return held_halves[road]

                part[where, :] = row_products(part[where, :], tile)
            return carry

        lax.fori_loop(0, half // 8, chunk, 0, unroll=min(8, half // 8))
        return prior[...] * vector + spread(even_part[...], odd_part[...])

    first = spread(even_sum[...], odd_sum[...])
    second = apply(first, False)
    third = apply(second, True)
    first, second, third = first[own], second[own], third[own]
    first_ref[...] = first
    second_ref[...] = second
    lane = iota(dots_ref.shape, 2)
    dots = jnp.zeros(dots_ref.shape, F32)
    pairs = ((first, first), (first, second), (second, second), (second, third), (third, third))
    for num, (one, other) in enumerate(pairs):
        dots = dots + jnp.where(lane == num, jnp.sum(one * other), 0.0)
    dots_ref[...] = dots


def finish_kernel(dots_ref, first_ref, second_ref, out_hbm, out_ref, sem):
    sums = jnp.sum(dots_ref[...], axis=0, keepdims=True)
    s00, s01, s11, s12, s22 = (sums[:, num : num + 1] for num in range(5))
    square_one = s00 + EPS
    beta_one = jnp.sqrt(square_one)
    alpha_one = s01 / square_one
    square_two = (s11 - 2.0 * alpha_one * s01 + alpha_one * alpha_one * s00) / square_one + EPS
    beta_two = jnp.sqrt(square_two)
    scale = 1.0 / (beta_one * beta_two)
    s02 = s11
    cross = s12 - alpha_one * s11 - square_two * s01
    cross = cross - alpha_one * (s02 - alpha_one * s01 - square_two * s00)
    alpha_two = cross * scale * scale
    near = alpha_one + alpha_two
    far = alpha_one * alpha_two - square_two
    square_three = s22 - 2.0 * near * s12 + near * near * s11
    square_three = square_three + 2.0 * far * s02 - 2.0 * near * far * s01 + far * far * s00
    square_three = square_three * scale * scale + EPS
    entry_first = alpha_one * alpha_one + square_two
    entry_cross = beta_two * near
    entry_second = square_two + alpha_two * alpha_two + square_three
    determinant = entry_first * entry_second - entry_cross * entry_cross
    coef_one = beta_one * (entry_second * alpha_one - entry_cross * beta_two) / determinant
    coef_two = beta_one * (entry_first * beta_two - entry_cross * alpha_one) / determinant
    on_second = coef_two * scale
    on_first = coef_one / beta_one - alpha_one * on_second
    out_ref[...] = on_first * first_ref[...] + on_second * second_ref[...]
    copy = pltpu.make_async_copy(out_ref, out_hbm, sem)
    copy.start()
    copy.wait()


def neighbour(value, steps):
    count = lax.axis_size(AXES)
    return lax.ppermute(value, AXES, [(s, (s + steps) % count) for s in range(count)])


def shape(*dims, dtype=F32):
    return jax.ShapeDtypeStruct(dims, dtype)


def on_device(
    local_deriv, global_deriv, measured, hit_weight, hit_module, hit_count, track_road, road_start,
    prior_weight,
):
    devices = lax.axis_size(AXES)
    roads = road_start.shape[0]
    tracks = hit_count.shape[0]
    modules = prior_weight.shape[0]
    cap = 4 * tracks // devices
    slots = devices * cap
    width = ROAD * NPAR
    half = modules // ROAD
    vmem = pl.BlockSpec(memory_space=pltpu.VMEM)
    smem = pl.BlockSpec(memory_space=pltpu.SMEM)
    limit = pltpu.CompilerParams(vmem_limit_bytes=32 * 1024 * 1024)
    large = pltpu.CompilerParams(vmem_limit_bytes=LARGE * 1024 * 1024)
    small = pltpu.CompilerParams(vmem_limit_bytes=20 * 1024 * 1024)

    sent = (
        local_deriv, jnp.transpose(global_deriv, (1, 0, 2)), measured, hit_weight, hit_module,
        hit_count[None, :], track_road[None, :],
    )
    message = (devices * USED, LANES) if folded(cap) else (ROWS, slots)
    send = pl.pallas_call(
        functools.partial(pack_kernel, cap, roads, modules * devices),
        out_shape=shape(*message),
        in_specs=[pl.BlockSpec(memory_space=pltpu.HBM)] * len(sent),
        out_specs=vmem,
        scratch_shapes=[
            pltpu.VMEM((ROWS, tracks), F32),
            pltpu.VMEM((2 * ROWS, tracks), BF16),
            pltpu.VMEM((NHIT, 8, tracks), F32),
            pltpu.VMEM((NHIT, 8, tracks), F32),
            pltpu.VMEM((slots, tracks), BF16),
            *(pltpu.VMEM(x.shape, x.dtype) for x in sent),
            pltpu.SemaphoreType.DMA((len(sent),)),
        ],
        compiler_params=large,
        name="fit_and_pack",
    )(*sent)
    if folded(cap):
        send = send.reshape(devices, USED, 1, LANES)
    else:
        send = jnp.transpose(send.reshape(ROWS, devices, cap), (1, 0, 2))
    recv = lax.all_to_all(send, AXES, split_axis=0, concat_axis=0, tiled=True)
    if folded(cap):
        recv = recv.reshape(message)
    else:
        recv = jnp.transpose(recv, (1, 0, 2)).reshape(message)

    offset = road_start % (ROAD // 2)
    list_rows = ((PER_ITEM * roads + slots) // (8 * LANES) + 1) * 8
    item_rows = -(-(list_rows * LANES // PER_ITEM) // (8 * LANES)) * 8
    track_list, items, bounds, track_off = pl.pallas_call(
        functools.partial(sort_kernel, cap),
        out_shape=(
            shape(list_rows, LANES, dtype=jnp.int32),
            shape(item_rows, LANES, dtype=jnp.int32),
            shape(8, LANES, dtype=jnp.int32),
            shape(slots // LANES, LANES),
        ),
        in_specs=[vmem] * 2,
        out_specs=(vmem,) * 4,
        scratch_shapes=[pltpu.VMEM((slots // LANES, LANES), F32)],
        compiler_params=limit,
        name="sort_by_road",
    )(recv, offset.astype(F32)[:, None])

    edge = roads // GROUPS
    prior = prior_weight.reshape(half, width)
    off_rows = jnp.broadcast_to(offset.astype(F32)[:, None], (roads, LANES))
    lists = (bounds.reshape(-1), track_list.reshape(-1), items.reshape(-1))
    halo = 4 * EDGE + EDGE
    tiles, edge_blocks, edge_sums, to_next, to_prev = pl.pallas_call(
        functools.partial(edge_kernel, cap),
        out_shape=(
            shape(slots + 8, 8, width), shape(roads, width, width), shape(roads, width),
            shape(PREV_ROADS * width + halo, width), shape(NEXT_ROADS * width + halo, width),
        ),
        in_specs=[smem] * 3 + [vmem] * 4,
        out_specs=(vmem,) * 5,
        scratch_shapes=[
            pltpu.VMEM((2, ROWS, LANES), F32),
            pltpu.VMEM((2, 8 + ROAD, LANES), F32),
            pltpu.VMEM((roads, 8, width), F32),
        ],
        compiler_params=small,
        name="lay_and_assemble_edges",
    )(*lists, recv, track_off, off_rows, prior)
    from_prev = neighbour(to_next, 1)
    from_next = neighbour(to_prev, -1)
    normal_blocks, held_blocks, sums = pl.pallas_call(
        inner_kernel,
        out_shape=(
            shape(roads, width, width), shape(roads, width, width), shape(roads, width),
        ),
        in_specs=[smem] * 3 + [vmem] * 3,
        out_specs=(pl.BlockSpec(memory_space=pltpu.HBM), vmem, vmem),
        scratch_shapes=[
            pltpu.VMEM((roads, 8, width), F32),
            pltpu.SemaphoreType.DMA((2 + (GROUPS - 2) // 2,)),
        ],
        input_output_aliases={4: 1, 5: 2},
        compiler_params=small,
        name="assemble_blocks",
    )(*lists, tiles, edge_blocks, edge_sums)

    total = half + 2 * EDGE
    rows = pltpu.VMEM((total, LANES), F32)
    int_rows = pltpu.VMEM((total, LANES), jnp.int32)
    halves = pltpu.VMEM((roads, width, 2 * width), BF16)
    edge_halves = pltpu.VMEM((8, width, 2 * width), BF16)
    first, second, dots = pl.pallas_call(
        krylov_kernel,
        out_shape=(shape(half, width), shape(half, width), shape(devices, 1, LANES)),
        in_specs=[vmem] * 6,
        out_specs=(vmem,) * 3,
        scratch_shapes=[
            rows, rows, int_rows, int_rows, rows, rows, rows, halves, edge_halves,
        ],
        compiler_params=small,
        name="two_products",
    )(held_blocks, sums, off_rows, prior, from_prev, from_next)
    everyone = lax.all_to_all(dots, AXES, split_axis=0, concat_axis=0, tiled=True)
    rhs = first.reshape(modules, NPAR)
    summed = (everyone.reshape(devices, LANES), rhs.T, second.reshape(modules, NPAR).T)
    corrections = pl.pallas_call(
        finish_kernel,
        out_shape=shape(NPAR, modules),
        in_specs=[vmem] * 3,
        out_specs=pl.BlockSpec(memory_space=pltpu.HBM),
        scratch_shapes=[pltpu.VMEM((NPAR, modules), F32), pltpu.SemaphoreType.DMA],
        compiler_params=pltpu.CompilerParams(vmem_limit_bytes=4 * 1024 * 1024),
        name="combine",
    )(*summed)
    return (normal_blocks, rhs, corrections.T)


def solution(mesh):
    track = P(None, None, AXES)
    in_specs = (
        track, track, P(None, AXES), P(None, AXES), P(None, AXES), P(AXES), P(AXES), P(AXES),
        P(AXES, None),
    )
    out_specs = (P(AXES, None, None), P(AXES, None), P(AXES, None))
    return jax.shard_map(
        on_device, mesh=mesh, in_specs=in_specs, out_specs=out_specs, check_vma=False
    )
```

```python
import functools

import jax
import jax.numpy as jnp
from jax import lax
from jax.experimental import pallas as pl
from jax.experimental.pallas import tpu as pltpu
from jax.sharding import PartitionSpec as P

NPAR = 8
NHIT = 12
NLOC = 5
ROAD = 16
LANES = 128
EPS = 1e-06
AXES = ("trk", "mod")

PART = 88
USED = 82
R_ROAD = 10 * NPAR
R_FIRST = R_ROAD + 1
R_SOLVED = PART + 2 * NPAR
R_GAP = R_SOLVED + NHIT
GAPS = ROAD - NHIT
R_PROJ = [R_GAP + GAPS + a * NHIT - a * (a - 1) // 2 for a in range(NLOC)]
ROWS = 2 * PART


def derivative_row(hit):
    return hit * NPAR if hit < 10 else PART + (hit - 10) * NPAR


LARGE = 60
PER_ITEM = 8
UNROLL = 16
GROUPS = 16
SUM_ROW = NLOC + 1
EDGE = 8
NEXT_ROADS = 2
PREV_ROADS = 4
F32 = jnp.float32
BF16 = jnp.bfloat16


def iota(shape, dim):
    return lax.broadcasted_iota(jnp.int32, shape, dim)


def dot(lhs, rhs, lhs_dim, rhs_dim):
    return lax.dot_general(
        lhs, rhs, (((lhs_dim,), (rhs_dim,)), ((), ())), preferred_element_type=F32
    )


def split_two(value):
    high = value.astype(BF16)
    return high, (value - high.astype(F32)).astype(BF16)


def householder(rows, first, column):
    vector = [row[column : column + 1] for row in rows[first:]]
    norm = jnp.sqrt(sum(part * part for part in vector))
    vector[0] = vector[0] + jnp.where(vector[0] >= 0.0, norm, -norm)
    square = sum(part * part for part in vector)
    scale = jnp.where(square > 1e-30, 2.0 / jnp.maximum(square, 1e-30), 0.0)
    along = sum(part * row for part, row in zip(vector, rows[first:])) * scale
    return rows[:first] + [row - part * along for part, row in zip(vector, rows[first:])]


def place_tracks(cap, road_dev, track_road, hot_ref):
    tracks = track_road.shape[1]
    owner = track_road // road_dev
    owner_col = jnp.concatenate(
        [
            jnp.broadcast_to(owner[:, at : at + LANES], (LANES, LANES)).astype(F32).T[:, :1]
            for at in range(0, tracks, LANES)
        ],
        axis=0,
    ).astype(jnp.int32)
    earlier = iota((tracks, tracks), 0) < iota((tracks, tracks), 1)
    same = jnp.where(jnp.logical_and(owner_col == owner, earlier), 1.0, 0.0)
    rank = jnp.sum(same, axis=0, keepdims=True).astype(jnp.int32)
    target = owner * cap + rank
    step = 2 * LANES
    for at in range(0, hot_ref.shape[0], step):
        hot = jnp.where(target == iota((step, tracks), 0) + at, 1.0, 0.0)
        hot_ref[at : at + step, :] = hot.astype(BF16)


def pack_kernel(
    cap, road_dev, module_count, ld_hbm, gd_hbm, me_hbm, hw_hbm, hm_hbm, hc_hbm, tr_hbm,
    out_ref, words_ref, parts_ref, mixed_ref, sorted_ref, hot_ref,
    ld_ref, gd_ref, me_ref, hw_ref, hm_ref, hc_ref, tr_ref, sems,
):
    sources = (tr_hbm, hc_hbm, hw_hbm, ld_hbm, me_hbm, hm_hbm, gd_hbm)
    targets = (tr_ref, hc_ref, hw_ref, ld_ref, me_ref, hm_ref, gd_ref)
    copies = [
        pltpu.make_async_copy(source, target, sems.at[num])
        for num, (source, target) in enumerate(zip(sources, targets))
    ]
    for copy in copies:
        copy.start()
    copies[0].wait()
    place_tracks(cap, road_dev, tr_ref[...], hot_ref)
    for copy in copies[1:]:
        copy.wait()
    tracks = tr_ref.shape[1]
    weight = jnp.where(iota((NHIT, tracks), 0) < hc_ref[...], hw_ref[...], 0.0)
    root = jnp.sqrt(weight)
    ahead = hm_ref[...] - tr_ref[...] * (ROAD // 2)
    ahead = jnp.where(ahead < 0, ahead + module_count, ahead).astype(F32)
    order = jnp.zeros((NHIT, tracks), F32)
    for i in range(NHIT):
        order = order + jnp.where(ahead[i : i + 1] < ahead, 1.0, 0.0)
    rows = [ld_ref[a] * root for a in range(NLOC)] + [me_ref[...] * root, ahead, order]
    for at in range(0, tracks, LANES):
        lanes = slice(at, at + LANES)
        mixed, ordered = mixed_ref.at[at // LANES], sorted_ref.at[at // LANES]
        for num, row in enumerate(rows):
            mixed[pl.ds(num, NHIT, stride=8), :] = row[:, lanes]
        tiles = [mixed[i * 8 : i * 8 + 8, :] for i in range(NHIT)]
        places = [jnp.broadcast_to(tile[NLOC + 2 : NLOC + 3], (8, LANES)) for tile in tiles]
        derivs = [gd_ref[i, :, lanes] * root[i : i + 1, lanes] for i in range(NHIT)]
        for k in range(NHIT):
            tile, deriv = tiles[0], derivs[0]
            for i in range(1, NHIT):
                here = places[i] == float(k)
                tile = jnp.where(here, tiles[i], tile)
                deriv = jnp.where(here, derivs[i], deriv)
            ordered[k * 8 : k * 8 + 8, :] = tile
            row = derivative_row(k)
            words_ref[row : row + NPAR, lanes] = deriv

    def in_order(num):
        parts = [
            sorted_ref[at, pl.ds(num, NHIT, stride=8), :] for at in range(tracks // LANES)
        ]
        return jnp.concatenate(parts, axis=1)

    scaled = [in_order(a) for a in range(NLOC)]
    factor = {}
    for a in range(NLOC):
        for b in range(a + 1):
            running = jnp.sum(scaled[a] * scaled[b], axis=0, keepdims=True)
            if a == b:
                running = running + 1.0
            for c in range(b):
                running = running - factor[a, c] * factor[b, c]
            factor[a, b] = jnp.sqrt(running) if a == b else running / factor[b, b]
    proj = []
    for a in range(NLOC):
        running = scaled[a]
        for b in range(a):
            running = running - factor[a, b] * proj[b]
        proj.append(running / factor[a, a])
    residual = in_order(NLOC)
    solved = residual
    for a in range(NLOC):
        solved = solved - proj[a] * jnp.sum(proj[a] * residual, axis=0, keepdims=True)
    for a in range(NLOC - 1):
        proj = householder(proj, a, a)
    ahead = in_order(NLOC + 1)
    skipped = ahead - ahead[0:1] - iota((NHIT, tracks), 0).astype(F32)
    words_ref[R_ROAD:R_FIRST, :] = (tr_ref[...] % road_dev + 1).astype(F32)
    words_ref[R_FIRST:USED, :] = ahead[0:1]
    words_ref[USED:PART, :] = jnp.zeros((PART - USED, tracks), F32)
    words_ref[R_SOLVED:R_GAP, :] = solved
    for gap in range(GAPS):
        words_ref[R_GAP + gap : R_GAP + gap + 1, :] = jnp.sum(
            jnp.where(skipped < gap + 0.5, 1.0, 0.0), axis=0, keepdims=True
        )
    for a in range(NLOC):
        words_ref[R_PROJ[a] : R_PROJ[a] + NHIT - a, :] = proj[a][a:]
    words_ref[PART + USED :, :] = jnp.zeros((PART - USED, tracks), F32)
    for num, part in enumerate(split_two(words_ref[...])):
        parts_ref[num * ROWS : (num + 1) * ROWS, :] = part
    lower_half = iota((USED, LANES), 1) < LANES // 2
    step = 2 * LANES
    for at in range(0, hot_ref.shape[0], step):
        moved = dot(parts_ref[...], hot_ref[at : at + step, :], 1, 1)
        moved = moved[:ROWS] + moved[ROWS:]
        if not folded(cap):
            out_ref[:, at : at + step] = moved
            continue
        for sub in range(2):
            lanes = slice(sub * LANES, (sub + 1) * LANES)
            one = moved[:USED, lanes]
            two = moved[PART : PART + USED, lanes]
            row = (at // LANES + sub) * 2 * USED
            out_ref[row : row + USED] = jnp.where(lower_half, one, pltpu.roll(two, LANES // 2, 1))
            out_ref[row + USED : row + 2 * USED] = jnp.where(
                lower_half, pltpu.roll(one, LANES // 2, 1), two
            )


def folded(cap):
    return 2 * cap == LANES


def sort_kernel(cap, recv_ref, off_ref, list_ref, item_ref, bound_ref, off_out_ref, road_ref):
    roads = off_ref.shape[0]
    blocks = road_ref.shape[0]
    if folded(cap):
        even = recv_ref[pl.ds(R_ROAD, blocks, stride=2 * USED), :]
        odd = recv_ref[pl.ds(R_ROAD + USED, blocks, stride=2 * USED), :]
        lower_half = iota((blocks, LANES), 1) < LANES // 2
        road_ref[...] = jnp.where(lower_half, even, pltpu.roll(odd, LANES // 2, 1))
    else:
        for e in range(blocks):
            road_ref[e : e + 1, :] = recv_ref[R_ROAD : R_ROAD + 1, e * LANES : (e + 1) * LANES]
    road_num = (iota((roads, LANES), 0) + 1).astype(F32)
    upper = jnp.where(iota((LANES, LANES), 0) < iota((LANES, LANES), 1), 1.0, 0.0).astype(BF16)
    offset = off_ref[...]
    counts = jnp.zeros((roads, 1), F32)
    ranks = []
    for e in range(blocks):
        hot = jnp.where(road_ref[e : e + 1, :] == road_num, 1.0, 0.0)
        before = dot(hot.astype(BF16), upper, 1, 0) + counts
        ranks.append(jnp.sum(hot * before, axis=0, keepdims=True))
        off_out_ref[e : e + 1, :] = jnp.sum(hot * offset, axis=0, keepdims=True)
        counts = counts + jnp.sum(hot, axis=1, keepdims=True)
    items = jnp.maximum(jnp.floor((counts + (PER_ITEM - 1)) * (1.0 / PER_ITEM)), 1.0)
    items = jnp.broadcast_to(items, (roads, LANES))
    lower = jnp.where(iota((roads, roads), 1) < iota((roads, roads), 0), 1.0, 0.0).astype(BF16)
    begin = dot(lower, items.astype(BF16), 1, 0)
    rows = list_ref.shape[0]
    total = jnp.zeros((rows, 2 * LANES), F32)
    row_num = iota((rows, LANES), 0).astype(F32)
    lane_num = iota((LANES, LANES), 0).astype(F32)
    track_lane = iota((1, LANES), 1).astype(F32)
    for e in range(blocks):
        road = road_ref[e : e + 1, :]
        hot = jnp.where(road == road_num, 1.0, 0.0)
        place = PER_ITEM * jnp.sum(hot * begin, axis=0, keepdims=True) + ranks[e]
        place = jnp.where(road > 0.5, place, -1.0)
        high = jnp.floor(place * (1.0 / LANES))
        low = place - high * LANES
        pick = jnp.where(high == row_num, 1.0, 0.0).astype(BF16)
        match = low == lane_num
        values = jnp.concatenate(
            [jnp.where(match, float(e + 1), 0.0), jnp.where(match, track_lane, 0.0)], axis=0
        )
        total = total + dot(pick, values.astype(BF16), 1, 1)
    found = total[:, :LANES]
    track = jnp.where(found > 0.5, (found - 1.0) * LANES + total[:, LANES:], float(blocks * LANES))
    list_ref[...] = (8.0 * track).astype(jnp.int32)
    item_rows = item_ref.shape[0]
    for row in range(item_rows):
        item = (iota((1, LANES), 1) + row * LANES).astype(F32)
        road = jnp.sum(jnp.where(begin <= item, 1.0, 0.0), axis=0, keepdims=True) - 1.0
        first = jnp.sum(jnp.where(begin == item, 1.0, 0.0), axis=0, keepdims=True)
        item_ref[row : row + 1, :] = (2.0 * road + first).astype(jnp.int32)
    each = roads // GROUPS
    begins = jnp.where(iota((roads, LANES), 0) == iota((roads, LANES), 1) * each, begin, 0.0)
    bound = jnp.sum(begins, axis=0, keepdims=True)
    last = jnp.sum(items, axis=0, keepdims=True)
    bound = jnp.where(iota((1, LANES), 1) < GROUPS, bound, last)
    bound_ref[...] = jnp.broadcast_to(bound, bound_ref.shape).astype(jnp.int32)


def lay_tiles(cap, recv_ref, off_ref, tiles_ref, words_ref, shift_ref):
    blocks = off_ref.shape[0]
    width = ROAD * NPAR
    lower_half = iota((USED, LANES), 1) < LANES // 2
    slot_num = iota((ROAD, LANES), 0)
    tiles_ref[blocks * LANES * 8 : (blocks * LANES + 1) * 8] = jnp.zeros((8, width), F32)
    shift_ref[:, :8, :] = jnp.full((2, 8, LANES), -1.0, F32)

    def lay(num, held):
        words = words_ref.at[held]
        shifts = shift_ref.at[held]
        e = 2 * num + held
        if folded(cap):
            both = recv_ref.at[pl.ds(pl.multiple_of(num * 4 * USED, 8), 4 * USED)]
            one = both[held * 2 * USED : held * 2 * USED + USED, :]
            two = both[held * 2 * USED + USED : held * 2 * USED + 2 * USED, :]
            words[:USED] = jnp.where(lower_half, one, pltpu.roll(two, LANES // 2, 1))
            words[PART : PART + USED] = jnp.where(lower_half, pltpu.roll(one, LANES // 2, 1), two)
        else:
            words[...] = recv_ref[:, pl.ds(pl.multiple_of(e * LANES, LANES), LANES)]
        shift = words[R_FIRST : R_FIRST + 1, :] - off_ref[pl.ds(e, 1), :]
        for gap in range(GAPS):
            reached = slot_num.astype(F32) >= words[R_GAP + gap : R_GAP + gap + 1, :]
            shift = shift + jnp.where(reached, 1.0, 0.0)
        shifts[8 : 8 + ROAD] = jnp.where(slot_num < NHIT, shift, -1.0)
        laid = [jnp.zeros((NPAR, LANES), F32) for s in range(ROAD)]
        for i in range(NHIT):
            row = derivative_row(i)
            value = words[row : row + NPAR, :]
            wide = jnp.broadcast_to(shifts[8 + i : 9 + i, :], (NPAR, LANES))
            for move in range(GAPS + 1):
                laid[i + move] = jnp.where(wide == float(move), value, laid[i + move])
        placed = [jnp.zeros((ROAD, LANES), F32) for a in range(NLOC + 1)]
        for move in range(GAPS + 1):
            match = shifts[8 - move : 8 - move + ROAD, :] == float(move)
            for a in range(NLOC + 1):
                if a == NLOC:
                    row, valid = R_SOLVED - move, match
                else:
                    row = R_PROJ[a] - a - move
                    valid = jnp.logical_and(match, slot_num >= a + move) if a else match
                placed[a] = jnp.where(valid, words[row : row + ROAD, :], placed[a])
        start = pl.multiple_of(e * LANES * 8, LANES * 8)
        for a in range(NLOC + 1):
            mixed = jnp.concatenate([laid[s] * placed[a][s : s + 1] for s in range(ROAD)], axis=0)
            row = a if a < NLOC else SUM_ROW
            tiles_ref[pl.ds(start + row, LANES, stride=8), :] = mixed.T
        tiles_ref[pl.ds(start + NLOC, LANES, stride=8), :] = jnp.concatenate(laid, axis=0).T
        empty = jnp.zeros((LANES, width), F32)
        tiles_ref[pl.ds(start + SUM_ROW + 1, LANES, stride=8), :] = empty

    def lay_two(num, carry):
        lay(num, 0)
        lay(num, 1)
        return carry

    lax.fori_loop(0, blocks // 2, lay_two, 0)


def item_steps(list_ref, item_ref, tiles_ref, out_ref, held_ref):
    width = ROAD * NPAR
    row_kind = iota((PER_ITEM * 8, width), 0) % 8
    proj = jnp.where(row_kind < NLOC, 1.0, 0.0).astype(BF16)
    own = jnp.where(row_kind == NLOC, 1.0, 0.0).astype(BF16)
    same_slot = iota((width, width), 0) // NPAR == iota((width, width), 1) // NPAR
    spare = list_ref.shape[0] // PER_ITEM - 1

    def step(item_at, count, num):
        for u in range(UNROLL):
            item = num * UNROLL + u
            live = item < count
            item = jnp.where(live, item_at(item), spare)
            info = item_ref[item]
            first = (info & 1) == 1
            road = jnp.where(live, info >> 1, 0)
            at = item * PER_ITEM
            parts = [
                tiles_ref[pl.ds(pl.multiple_of(list_ref[at + j], 8), 8), :] for j in range(PER_ITEM)
            ]
            tall = jnp.concatenate(parts, axis=0)
            high, low = split_two(tall)
            left = jnp.concatenate([high, high, low], axis=0)
            high_p, low_p, high_o, low_o = high * proj, low * proj, high * own, low * own
            right = jnp.concatenate(
                [
                    jnp.concatenate([high_p, low_p, high_p], axis=0),
                    jnp.concatenate([high_o, low_o, high_o], axis=0),
                ],
                axis=1,
            )
            both = dot(left, right, 0, 0)
            value = jnp.where(same_slot, both[:, width:], 0.0) - both[:, :width]
            out_ref[road] = value + jnp.where(first, 0.0, out_ref[road])
            added = parts[0]
            for part in parts[1:]:
                added = added + part
            where = pl.ds(pl.multiple_of(road * 8, 8), 8)
            held_ref[where, :] = added + jnp.where(first, 0.0, held_ref[where, :])

    return step


def edge_kernel(
    cap, bound_ref, list_ref, item_ref, recv_ref, off_ref, off_rows_ref, prior_ref,
    tiles_ref, out_ref, sums_ref, to_next_ref, to_prev_ref, words_ref, shift_ref, held_ref,
):
    roads, width = sums_ref.shape
    edge = roads // GROUPS
    lay_tiles(cap, recv_ref, off_ref, tiles_ref, words_ref, shift_ref)
    step = item_steps(list_ref, item_ref, tiles_ref, out_ref, held_ref)
    low = bound_ref[1]
    high = bound_ref[GROUPS - 1]
    count = low + bound_ref[GROUPS] - high

    def body(num, carry):
        step(lambda item: jnp.where(item < low, item, item - low + high), count, num)
        return carry

    lax.fori_loop(0, (count + UNROLL - 1) // UNROLL, body, 0)
    for start in (0, roads - edge):
        sums_ref[start : start + edge] = held_ref[pl.ds(start * 8 + SUM_ROW, edge, stride=8), :]
    two = 2 * EDGE
    for ref, first_block, count, first_road, first_row in (
        (to_next_ref, roads - PREV_ROADS, PREV_ROADS, roads - two, prior_ref.shape[0] - EDGE),
        (to_prev_ref, 0, NEXT_ROADS, 0, 0),
    ):
        for num in range(count):
            ref[num * width : (num + 1) * width] = out_ref[first_block + num]
        at = count * width
        ref[at : at + two] = sums_ref[first_road : first_road + two]
        ref[at + two : at + 2 * two] = off_rows_ref[first_road : first_road + two]
        ref[at + 2 * two :] = prior_ref[first_row : first_row + EDGE]


def inner_kernel(
    bound_ref, list_ref, item_ref, tiles_ref, edge_ref, edge_sums_ref,
    blocks_hbm, out_ref, sums_ref, held_ref, sems,
):
    roads, width = sums_ref.shape
    edge = roads // GROUPS
    step = item_steps(list_ref, item_ref, tiles_ref, out_ref, held_ref)
    outer = [
        pltpu.make_async_copy(
            out_ref.at[pl.ds(at, edge)], blocks_hbm.at[pl.ds(at, edge)], sems.at[num]
        )
        for num, at in enumerate((0, roads - edge))
    ]
    begin, end = bound_ref[1], bound_ref[GROUPS - 1]
    done = 0
    copies = []
    pieces = (GROUPS - 2) // 2
    for piece in range(pieces):
        group = 1 + 2 * piece
        until = (bound_ref[group + 2] - begin + UNROLL - 1) // UNROLL

        def body(num, carry):
            step(lambda item: item + begin, end - begin, num)
            return carry

        lax.fori_loop(done, until, body, 0)
        done = until
        where = pl.ds(group * edge, 2 * edge)
        copies.append(
            pltpu.make_async_copy(out_ref.at[where], blocks_hbm.at[where], sems.at[2 + piece])
        )
        copies[-1].start()
    for copy in outer:
        copy.start()
    sums_ref[edge : roads - edge] = held_ref[
        pl.ds(edge * 8 + SUM_ROW, roads - 2 * edge, stride=8), :
    ]
    for copy in outer + copies:
        copy.wait()
    del edge_ref, edge_sums_ref


def lane_bits(offset, bit):
    return (offset // (1 << bit)) % 2 == 1


def gathered(rows, offset, odd):
    lane = iota(rows.shape, 1)
    here = rows
    there = jnp.concatenate([rows[1:], jnp.zeros((1, LANES), F32)], axis=0)
    if odd:
        half = LANES // 2
        turned_here, turned_there = pltpu.roll(here, half, 1), pltpu.roll(there, half, 1)
        here = jnp.where(lane < LANES - half, turned_here, turned_there)
        there = turned_there
    for bit in range(3):
        step = NPAR << bit
        take = lane_bits(offset, bit)
        turned_here, turned_there = (
            pltpu.roll(here, LANES - step, 1),
            pltpu.roll(there, LANES - step, 1),
        )
        moved = jnp.where(lane < LANES - step, turned_here, turned_there)
        here = jnp.where(take, moved, here)
        there = jnp.where(take, turned_there, there)
    return here


def scattered(rows, offset, odd):
    lane = iota(rows.shape, 1)
    here, there = rows, jnp.zeros_like(rows)
    steps = [(NPAR << bit, bit) for bit in range(3)] + ([(LANES // 2, None)] if odd else [])
    for step, bit in steps:
        turned_here, turned_there = pltpu.roll(here, step, 1), pltpu.roll(there, step, 1)
        new_here = jnp.where(lane < step, 0.0, turned_here)
        new_there = jnp.where(lane < step, turned_here, turned_there)
        if bit is None:
            here, there = new_here, new_there
        else:
            take = lane_bits(offset, bit)
            here = jnp.where(take, new_here, here)
            there = jnp.where(take, new_there, there)
    return here, there


def krylov_kernel(
    held, sums_ref, off_ref, prior_ref, from_prev_ref, from_next_ref,
    first_ref, second_ref, dots_ref,
    even_sum, odd_sum, even_off, odd_off, prior, even_part, odd_part, held_halves, edge_halves,
):
    roads, width = sums_ref.shape
    half = roads // 2
    own = slice(EDGE, EDGE + half)
    two = 2 * EDGE
    at_prev = PREV_ROADS * width
    at_next = NEXT_ROADS * width
    for parity, total_sum, total_off in ((0, even_sum, even_off), (1, odd_sum, odd_off)):
        pick = lambda ref, start, count: ref[pl.ds(start + parity, count, stride=2), :]
        total_sum[0:EDGE] = pick(from_prev_ref, at_prev, EDGE)
        total_sum[own] = pick(sums_ref, 0, half)
        total_sum[EDGE + half :] = pick(from_next_ref, at_next, EDGE)
        total_off[0:EDGE] = pick(from_prev_ref, at_prev + two, EDGE).astype(jnp.int32)
        total_off[own] = pick(off_ref, 0, half).astype(jnp.int32)
        total_off[EDGE + half :] = pick(from_next_ref, at_next + two, EDGE).astype(jnp.int32)
    prior[0:EDGE] = from_prev_ref[at_prev + 2 * two : at_prev + 2 * two + EDGE]
    prior[own] = prior_ref[...]
    prior[EDGE + half :] = from_next_ref[at_next + 2 * two : at_next + 2 * two + EDGE]

    def spread(even, odd):
        even_here, even_there = scattered(even, even_off[...], False)
        odd_here, odd_there = scattered(odd, odd_off[...], True)
        over = even_there + odd_there
        return (
            even_here
            + odd_here
            + jnp.concatenate([jnp.zeros((1, LANES), F32), over[:-1]], axis=0)
        )

    def row_products(rows, tiles_at):
        lane_block = iota((8, 8 * width), 1) // width
        diagonal = lane_block == iota((8, 8 * width), 0)
        left = jnp.concatenate(
            [jnp.where(diagonal, jnp.concatenate([part.astype(F32)] * 8, axis=1), 0.0)
             for part in split_two(rows)],
            axis=0,
        ).astype(BF16)
        right = jnp.concatenate([tiles_at(k) for k in range(8)], axis=0)
        both = dot(left, right, 1, 0)
        both = both[:, :width] + both[:, width:]
        return both[:8] + both[8:]

    def halves(block):
        return jnp.concatenate(split_two(block), axis=1)

    edge_blocks = [(from_prev_ref, num) for num in range(PREV_ROADS)]
    edge_blocks += [(from_next_ref, num) for num in range(NEXT_ROADS)]
    edge_blocks += edge_blocks[:2]
    edge_rows = [(EDGE - PREV_ROADS // 2 + num // 2, num % 2) for num in range(PREV_ROADS)]
    edge_rows += [(EDGE + half, num) for num in range(NEXT_ROADS)]

    def apply(vector, again):
        even_part[...] = gathered(vector, even_off[...], False)
        odd_part[...] = gathered(vector, odd_off[...], True)
        outer = [(odd_part if odd else even_part)[row : row + 1, :] for row, odd in edge_rows]
        outer = jnp.concatenate(outer + [jnp.zeros((2, LANES), F32)], axis=0)

        def edge_tile(k):
            if again:
                return edge_halves[k]
            ref, num = edge_blocks[k]
            edge_halves[k] = halves(ref[num * width : (num + 1) * width, :])
            return edge_halves[k]

        outer = row_products(outer, edge_tile)
        for part, parity in ((even_part, 0), (odd_part, 1)):
            part[EDGE + half :, :] = jnp.zeros((EDGE, LANES), F32)
            part[:EDGE, :] = jnp.zeros((EDGE, LANES), F32)
        for num, (row, odd) in enumerate(edge_rows):
            (odd_part if odd else even_part)[row : row + 1, :] = outer[num : num + 1]

        def chunk(c, carry):
            for part, parity in ((even_part, 0), (odd_part, 1)):
                where = pl.ds(pl.multiple_of(EDGE + c * 8, 8), 8)

                def tile(k, parity=parity):
                    road = c * 16 + 2 * k + parity
                    if not again:
                        held_halves[road] = halves(held[road])
                    return held_halves[road]

                part[where, :] = row_products(part[where, :], tile)
            return carry

        lax.fori_loop(0, half // 8, chunk, 0, unroll=min(8, half // 8))
        return prior[...] * vector + spread(even_part[...], odd_part[...])

    first = spread(even_sum[...], odd_sum[...])
    second = apply(first, False)
    third = apply(second, True)
    first, second, third = first[own], second[own], third[own]
    first_ref[...] = first
    second_ref[...] = second
    lane = iota(dots_ref.shape, 2)
    dots = jnp.zeros(dots_ref.shape, F32)
    pairs = ((first, first), (first, second), (second, second), (second, third), (third, third))
    for num, (one, other) in enumerate(pairs):
        dots = dots + jnp.where(lane == num, jnp.sum(one * other), 0.0)
    dots_ref[...] = dots


def finish_kernel(dots_ref, first_ref, second_ref, out_hbm, out_ref, sem):
    sums = jnp.sum(dots_ref[...], axis=0, keepdims=True)
    s00, s01, s11, s12, s22 = (sums[:, num : num + 1] for num in range(5))
    square_one = s00 + EPS
    beta_one = jnp.sqrt(square_one)
    alpha_one = s01 / square_one
    square_two = (s11 - 2.0 * alpha_one * s01 + alpha_one * alpha_one * s00) / square_one + EPS
    beta_two = jnp.sqrt(square_two)
    scale = 1.0 / (beta_one * beta_two)
    s02 = s11
    cross = s12 - alpha_one * s11 - square_two * s01
    cross = cross - alpha_one * (s02 - alpha_one * s01 - square_two * s00)
    alpha_two = cross * scale * scale
    near = alpha_one + alpha_two
    far = alpha_one * alpha_two - square_two
    square_three = s22 - 2.0 * near * s12 + near * near * s11
    square_three = square_three + 2.0 * far * s02 - 2.0 * near * far * s01 + far * far * s00
    square_three = square_three * scale * scale + EPS
    entry_first = alpha_one * alpha_one + square_two
    entry_cross = beta_two * near
    entry_second = square_two + alpha_two * alpha_two + square_three
    determinant = entry_first * entry_second - entry_cross * entry_cross
    coef_one = beta_one * (entry_second * alpha_one - entry_cross * beta_two) / determinant
    coef_two = beta_one * (entry_first * beta_two - entry_cross * alpha_one) / determinant
    on_second = coef_two * scale
    on_first = coef_one / beta_one - alpha_one * on_second
    out_ref[...] = on_first * first_ref[...] + on_second * second_ref[...]
    copy = pltpu.make_async_copy(out_ref, out_hbm, sem)
    copy.start()
    copy.wait()


def neighbour(value, steps):
    count = lax.axis_size(AXES)
    return lax.ppermute(value, AXES, [(s, (s + steps) % count) for s in range(count)])


def shape(*dims, dtype=F32):
    return jax.ShapeDtypeStruct(dims, dtype)


def on_device(
    local_deriv, global_deriv, measured, hit_weight, hit_module, hit_count, track_road, road_start,
    prior_weight,
):
    devices = lax.axis_size(AXES)
    roads = road_start.shape[0]
    tracks = hit_count.shape[0]
    modules = prior_weight.shape[0]
    cap = 4 * tracks // devices
    slots = devices * cap
    width = ROAD * NPAR
    half = modules // ROAD
    vmem = pl.BlockSpec(memory_space=pltpu.VMEM)
    smem = pl.BlockSpec(memory_space=pltpu.SMEM)
    limit = pltpu.CompilerParams(vmem_limit_bytes=32 * 1024 * 1024)
    large = pltpu.CompilerParams(vmem_limit_bytes=LARGE * 1024 * 1024)
    small = pltpu.CompilerParams(vmem_limit_bytes=20 * 1024 * 1024)

    sent = (
        local_deriv, jnp.transpose(global_deriv, (1, 0, 2)), measured, hit_weight, hit_module,
        hit_count[None, :], track_road[None, :],
    )
    message = (devices * USED, LANES) if folded(cap) else (ROWS, slots)
    send = pl.pallas_call(
        functools.partial(pack_kernel, cap, roads, modules * devices),
        out_shape=shape(*message),
        in_specs=[pl.BlockSpec(memory_space=pltpu.HBM)] * len(sent),
        out_specs=vmem,
        scratch_shapes=[
            pltpu.VMEM((ROWS, tracks), F32),
            pltpu.VMEM((2 * ROWS, tracks), BF16),
            pltpu.VMEM((tracks // LANES, NHIT * 8, LANES), F32),
            pltpu.VMEM((tracks // LANES, NHIT * 8, LANES), F32),
            pltpu.VMEM((slots, tracks), BF16),
            *(pltpu.VMEM(x.shape, x.dtype) for x in sent),
            pltpu.SemaphoreType.DMA((len(sent),)),
        ],
        compiler_params=large,
        name="fit_and_pack",
    )(*sent)
    if folded(cap):
        send = send.reshape(devices, USED, 1, LANES)
    else:
        send = jnp.transpose(send.reshape(ROWS, devices, cap), (1, 0, 2))
    recv = lax.all_to_all(send, AXES, split_axis=0, concat_axis=0, tiled=True)
    if folded(cap):
        recv = recv.reshape(message)
    else:
        recv = jnp.transpose(recv, (1, 0, 2)).reshape(message)

    offset = road_start % (ROAD // 2)
    list_rows = ((PER_ITEM * roads + slots) // (8 * LANES) + 1) * 8
    item_rows = -(-(list_rows * LANES // PER_ITEM) // (8 * LANES)) * 8
    track_list, items, bounds, track_off = pl.pallas_call(
        functools.partial(sort_kernel, cap),
        out_shape=(
            shape(list_rows, LANES, dtype=jnp.int32),
            shape(item_rows, LANES, dtype=jnp.int32),
            shape(8, LANES, dtype=jnp.int32),
            shape(slots // LANES, LANES),
        ),
        in_specs=[vmem] * 2,
        out_specs=(vmem,) * 4,
        scratch_shapes=[pltpu.VMEM((slots // LANES, LANES), F32)],
        compiler_params=limit,
        name="sort_by_road",
    )(recv, offset.astype(F32)[:, None])

    edge = roads // GROUPS
    prior = prior_weight.reshape(half, width)
    off_rows = jnp.broadcast_to(offset.astype(F32)[:, None], (roads, LANES))
    lists = (bounds.reshape(-1), track_list.reshape(-1), items.reshape(-1))
    halo = 4 * EDGE + EDGE
    tiles, edge_blocks, edge_sums, to_next, to_prev = pl.pallas_call(
        functools.partial(edge_kernel, cap),
        out_shape=(
            shape((slots + 8) * 8, width), shape(roads, width, width), shape(roads, width),
            shape(PREV_ROADS * width + halo, width), shape(NEXT_ROADS * width + halo, width),
        ),
        in_specs=[smem] * 3 + [vmem] * 4,
        out_specs=(vmem,) * 5,
        scratch_shapes=[
            pltpu.VMEM((2, ROWS, LANES), F32),
            pltpu.VMEM((2, 8 + ROAD, LANES), F32),
            pltpu.VMEM((roads * 8, width), F32),
        ],
        compiler_params=small,
        name="lay_and_assemble_edges",
    )(*lists, recv, track_off, off_rows, prior)
    from_prev = neighbour(to_next, 1)
    from_next = neighbour(to_prev, -1)
    normal_blocks, held_blocks, sums = pl.pallas_call(
        inner_kernel,
        out_shape=(
            shape(roads, width, width), shape(roads, width, width), shape(roads, width),
        ),
        in_specs=[smem] * 3 + [vmem] * 3,
        out_specs=(pl.BlockSpec(memory_space=pltpu.HBM), vmem, vmem),
        scratch_shapes=[
            pltpu.VMEM((roads * 8, width), F32),
            pltpu.SemaphoreType.DMA((2 + (GROUPS - 2) // 2,)),
        ],
        input_output_aliases={4: 1, 5: 2},
        compiler_params=small,
        name="assemble_blocks",
    )(*lists, tiles, edge_blocks, edge_sums)

    total = half + 2 * EDGE
    rows = pltpu.VMEM((total, LANES), F32)
    int_rows = pltpu.VMEM((total, LANES), jnp.int32)
    halves = pltpu.VMEM((roads, width, 2 * width), BF16)
    edge_halves = pltpu.VMEM((8, width, 2 * width), BF16)
    first, second, dots = pl.pallas_call(
        krylov_kernel,
        out_shape=(shape(half, width), shape(half, width), shape(devices, 1, LANES)),
        in_specs=[vmem] * 6,
        out_specs=(vmem,) * 3,
        scratch_shapes=[
            rows, rows, int_rows, int_rows, rows, rows, rows, halves, edge_halves,
        ],
        compiler_params=small,
        name="two_products",
    )(held_blocks, sums, off_rows, prior, from_prev, from_next)
    everyone = lax.all_to_all(dots, AXES, split_axis=0, concat_axis=0, tiled=True)
    rhs = first.reshape(modules, NPAR)
    summed = (everyone.reshape(devices, LANES), rhs.T, second.reshape(modules, NPAR).T)
    corrections = pl.pallas_call(
        finish_kernel,
        out_shape=shape(NPAR, modules),
        in_specs=[vmem] * 3,
        out_specs=pl.BlockSpec(memory_space=pltpu.HBM),
        scratch_shapes=[pltpu.VMEM((NPAR, modules), F32), pltpu.SemaphoreType.DMA],
        compiler_params=pltpu.CompilerParams(vmem_limit_bytes=4 * 1024 * 1024),
        name="combine",
    )(*summed)
    return (normal_blocks, rhs, corrections.T)


def solution(mesh):
    track = P(None, None, AXES)
    in_specs = (
        track, track, P(None, AXES), P(None, AXES), P(None, AXES), P(AXES), P(AXES), P(AXES),
        P(AXES, None),
    )
    out_specs = (P(AXES, None, None), P(AXES, None), P(AXES, None))
    return jax.shard_map(
        on_device, mesh=mesh, in_specs=in_specs, out_specs=out_specs, check_vma=False
    )
```

```python
import functools

import jax
import jax.numpy as jnp
from jax import lax
from jax.experimental import pallas as pl
from jax.experimental.pallas import tpu as pltpu
from jax.sharding import PartitionSpec as P

NPAR = 8
NHIT = 12
NLOC = 5
ROAD = 16
LANES = 128
EPS = 1e-06
AXES = ("trk", "mod")

PART = 88
USED = 82
R_ROAD = 10 * NPAR
R_FIRST = R_ROAD + 1
R_SOLVED = PART + 2 * NPAR
R_GAP = R_SOLVED + NHIT
GAPS = ROAD - NHIT
R_PROJ = [R_GAP + GAPS + a * NHIT - a * (a - 1) // 2 for a in range(NLOC)]
ROWS = 2 * PART


def derivative_row(hit):
    return hit * NPAR if hit < 10 else PART + (hit - 10) * NPAR


LARGE = 60
PER_ITEM = 8
UNROLL = 24
GROUPS = 16
SUM_ROW = NLOC + 1
EDGE = 8
NEXT_ROADS = 2
PREV_ROADS = 4
F32 = jnp.float32
BF16 = jnp.bfloat16


def iota(shape, dim):
    return lax.broadcasted_iota(jnp.int32, shape, dim)


def dot(lhs, rhs, lhs_dim, rhs_dim):
    return lax.dot_general(
        lhs, rhs, (((lhs_dim,), (rhs_dim,)), ((), ())), preferred_element_type=F32
    )


def split_two(value):
    high = value.astype(BF16)
    return high, (value - high.astype(F32)).astype(BF16)


def householder(rows, first, column):
    vector = [row[column : column + 1] for row in rows[first:]]
    norm = jnp.sqrt(sum(part * part for part in vector))
    vector[0] = vector[0] + jnp.where(vector[0] >= 0.0, norm, -norm)
    square = sum(part * part for part in vector)
    scale = jnp.where(square > 1e-30, 2.0 / jnp.maximum(square, 1e-30), 0.0)
    along = sum(part * row for part, row in zip(vector, rows[first:])) * scale
    return rows[:first] + [row - part * along for part, row in zip(vector, rows[first:])]


def place_tracks(cap, road_dev, track_road, hot_ref):
    tracks = track_road.shape[1]
    owner = track_road // road_dev
    owner_col = jnp.concatenate(
        [
            jnp.broadcast_to(owner[:, at : at + LANES], (LANES, LANES)).astype(F32).T[:, :1]
            for at in range(0, tracks, LANES)
        ],
        axis=0,
    ).astype(jnp.int32)
    earlier = iota((tracks, tracks), 0) < iota((tracks, tracks), 1)
    same = jnp.where(jnp.logical_and(owner_col == owner, earlier), 1.0, 0.0)
    rank = jnp.sum(same, axis=0, keepdims=True).astype(jnp.int32)
    target = owner * cap + rank
    step = 2 * LANES
    for at in range(0, hot_ref.shape[0], step):
        hot = jnp.where(target == iota((step, tracks), 0) + at, 1.0, 0.0)
        hot_ref[at : at + step, :] = hot.astype(BF16)


def pack_kernel(
    cap, road_dev, module_count, ld_hbm, gd_hbm, me_hbm, hw_hbm, hm_hbm, hc_hbm, tr_hbm,
    out_ref, words_ref, parts_ref, mixed_ref, sorted_ref, hot_ref,
    ld_ref, gd_ref, me_ref, hw_ref, hm_ref, hc_ref, tr_ref, sems,
):
    sources = (tr_hbm, hc_hbm, hw_hbm, ld_hbm, me_hbm, hm_hbm, gd_hbm)
    targets = (tr_ref, hc_ref, hw_ref, ld_ref, me_ref, hm_ref, gd_ref)
    copies = [
        pltpu.make_async_copy(source, target, sems.at[num])
        for num, (source, target) in enumerate(zip(sources, targets))
    ]
    for copy in copies:
        copy.start()
    copies[0].wait()
    place_tracks(cap, road_dev, tr_ref[...], hot_ref)
    for copy in copies[1:]:
        copy.wait()
    tracks = tr_ref.shape[1]
    weight = jnp.where(iota((NHIT, tracks), 0) < hc_ref[...], hw_ref[...], 0.0)
    root = jnp.sqrt(weight)
    ahead = hm_ref[...] - tr_ref[...] * (ROAD // 2)
    ahead = jnp.where(ahead < 0, ahead + module_count, ahead).astype(F32)
    order = jnp.zeros((NHIT, tracks), F32)
    for i in range(NHIT):
        order = order + jnp.where(ahead[i : i + 1] < ahead, 1.0, 0.0)
    rows = [ld_ref[a] * root for a in range(NLOC)] + [me_ref[...] * root, ahead, order]
    for at in range(0, tracks, LANES):
        lanes = slice(at, at + LANES)
        mixed, ordered = mixed_ref.at[at // LANES], sorted_ref.at[at // LANES]
        for num, row in enumerate(rows):
            mixed[pl.ds(num, NHIT, stride=8), :] = row[:, lanes]
        tiles = [mixed[i * 8 : i * 8 + 8, :] for i in range(NHIT)]
        places = [jnp.broadcast_to(tile[NLOC + 2 : NLOC + 3], (8, LANES)) for tile in tiles]
        derivs = [gd_ref[i, :, lanes] * root[i : i + 1, lanes] for i in range(NHIT)]
        for k in range(NHIT):
            tile, deriv = tiles[0], derivs[0]
            for i in range(1, NHIT):
                here = places[i] == float(k)
                tile = jnp.where(here, tiles[i], tile)
                deriv = jnp.where(here, derivs[i], deriv)
            ordered[k * 8 : k * 8 + 8, :] = tile
            row = derivative_row(k)
            words_ref[row : row + NPAR, lanes] = deriv

    def in_order(num):
        parts = [
            sorted_ref[at, pl.ds(num, NHIT, stride=8), :] for at in range(tracks // LANES)
        ]
        return jnp.concatenate(parts, axis=1)

    scaled = [in_order(a) for a in range(NLOC)]
    factor = {}
    for a in range(NLOC):
        for b in range(a + 1):
            running = jnp.sum(scaled[a] * scaled[b], axis=0, keepdims=True)
            if a == b:
                running = running + 1.0
            for c in range(b):
                running = running - factor[a, c] * factor[b, c]
            factor[a, b] = jnp.sqrt(running) if a == b else running / factor[b, b]
    proj = []
    for a in range(NLOC):
        running = scaled[a]
        for b in range(a):
            running = running - factor[a, b] * proj[b]
        proj.append(running / factor[a, a])
    residual = in_order(NLOC)
    solved = residual
    for a in range(NLOC):
        solved = solved - proj[a] * jnp.sum(proj[a] * residual, axis=0, keepdims=True)
    for a in range(NLOC - 1):
        proj = householder(proj, a, a)
    ahead = in_order(NLOC + 1)
    skipped = ahead - ahead[0:1] - iota((NHIT, tracks), 0).astype(F32)
    words_ref[R_ROAD:R_FIRST, :] = (tr_ref[...] % road_dev + 1).astype(F32)
    words_ref[R_FIRST:USED, :] = ahead[0:1]
    words_ref[USED:PART, :] = jnp.zeros((PART - USED, tracks), F32)
    words_ref[R_SOLVED:R_GAP, :] = solved
    for gap in range(GAPS):
        words_ref[R_GAP + gap : R_GAP + gap + 1, :] = jnp.sum(
            jnp.where(skipped < gap + 0.5, 1.0, 0.0), axis=0, keepdims=True
        )
    for a in range(NLOC):
        words_ref[R_PROJ[a] : R_PROJ[a] + NHIT - a, :] = proj[a][a:]
    words_ref[PART + USED :, :] = jnp.zeros((PART - USED, tracks), F32)
    for num, part in enumerate(split_two(words_ref[...])):
        parts_ref[num * ROWS : (num + 1) * ROWS, :] = part
    lower_half = iota((USED, LANES), 1) < LANES // 2
    step = 2 * LANES
    for at in range(0, hot_ref.shape[0], step):
        moved = dot(parts_ref[...], hot_ref[at : at + step, :], 1, 1)
        moved = moved[:ROWS] + moved[ROWS:]
        if not folded(cap):
            out_ref[:, at : at + step] = moved
            continue
        for sub in range(2):
            lanes = slice(sub * LANES, (sub + 1) * LANES)
            one = moved[:USED, lanes]
            two = moved[PART : PART + USED, lanes]
            row = (at // LANES + sub) * 2 * USED
            out_ref[row : row + USED] = jnp.where(lower_half, one, pltpu.roll(two, LANES // 2, 1))
            out_ref[row + USED : row + 2 * USED] = jnp.where(
                lower_half, pltpu.roll(one, LANES // 2, 1), two
            )


def folded(cap):
    return 2 * cap == LANES


def sort_kernel(cap, recv_ref, off_ref, list_ref, item_ref, bound_ref, off_out_ref, road_ref):
    roads = off_ref.shape[0]
    blocks = road_ref.shape[0]
    if folded(cap):
        even = recv_ref[pl.ds(R_ROAD, blocks, stride=2 * USED), :]
        odd = recv_ref[pl.ds(R_ROAD + USED, blocks, stride=2 * USED), :]
        lower_half = iota((blocks, LANES), 1) < LANES // 2
        road_ref[...] = jnp.where(lower_half, even, pltpu.roll(odd, LANES // 2, 1))
    else:
        for e in range(blocks):
            road_ref[e : e + 1, :] = recv_ref[R_ROAD : R_ROAD + 1, e * LANES : (e + 1) * LANES]
    road_num = (iota((roads, LANES), 0) + 1).astype(F32)
    upper = jnp.where(iota((LANES, LANES), 0) < iota((LANES, LANES), 1), 1.0, 0.0).astype(BF16)
    offset = off_ref[...]
    counts = jnp.zeros((roads, 1), F32)
    ranks = []
    for e in range(blocks):
        hot = jnp.where(road_ref[e : e + 1, :] == road_num, 1.0, 0.0)
        before = dot(hot.astype(BF16), upper, 1, 0) + counts
        ranks.append(jnp.sum(hot * before, axis=0, keepdims=True))
        off_out_ref[e : e + 1, :] = jnp.sum(hot * offset, axis=0, keepdims=True)
        counts = counts + jnp.sum(hot, axis=1, keepdims=True)
    items = jnp.maximum(jnp.floor((counts + (PER_ITEM - 1)) * (1.0 / PER_ITEM)), 1.0)
    items = jnp.broadcast_to(items, (roads, LANES))
    lower = jnp.where(iota((roads, roads), 1) < iota((roads, roads), 0), 1.0, 0.0).astype(BF16)
    begin = dot(lower, items.astype(BF16), 1, 0)
    rows = list_ref.shape[0]
    total = jnp.zeros((rows, 2 * LANES), F32)
    row_num = iota((rows, LANES), 0).astype(F32)
    lane_num = iota((LANES, LANES), 0).astype(F32)
    track_lane = iota((1, LANES), 1).astype(F32)
    for e in range(blocks):
        road = road_ref[e : e + 1, :]
        hot = jnp.where(road == road_num, 1.0, 0.0)
        place = PER_ITEM * jnp.sum(hot * begin, axis=0, keepdims=True) + ranks[e]
        place = jnp.where(road > 0.5, place, -1.0)
        high = jnp.floor(place * (1.0 / LANES))
        low = place - high * LANES
        pick = jnp.where(high == row_num, 1.0, 0.0).astype(BF16)
        match = low == lane_num
        values = jnp.concatenate(
            [jnp.where(match, float(e + 1), 0.0), jnp.where(match, track_lane, 0.0)], axis=0
        )
        total = total + dot(pick, values.astype(BF16), 1, 1)
    found = total[:, :LANES]
    track = jnp.where(found > 0.5, (found - 1.0) * LANES + total[:, LANES:], float(blocks * LANES))
    list_ref[...] = (8.0 * track).astype(jnp.int32)
    item_rows = item_ref.shape[0]
    for row in range(item_rows):
        item = (iota((1, LANES), 1) + row * LANES).astype(F32)
        road = jnp.sum(jnp.where(begin <= item, 1.0, 0.0), axis=0, keepdims=True) - 1.0
        first = jnp.sum(jnp.where(begin == item, 1.0, 0.0), axis=0, keepdims=True)
        item_ref[row : row + 1, :] = (2.0 * road + first).astype(jnp.int32)
    each = roads // GROUPS
    begins = jnp.where(iota((roads, LANES), 0) == iota((roads, LANES), 1) * each, begin, 0.0)
    bound = jnp.sum(begins, axis=0, keepdims=True)
    last = jnp.sum(items, axis=0, keepdims=True)
    bound = jnp.where(iota((1, LANES), 1) < GROUPS, bound, last)
    bound_ref[...] = jnp.broadcast_to(bound, bound_ref.shape).astype(jnp.int32)


def lay_tiles(cap, recv_ref, off_ref, tiles_ref, words_ref, shift_ref):
    blocks = off_ref.shape[0]
    width = ROAD * NPAR
    lower_half = iota((USED, LANES), 1) < LANES // 2
    slot_num = iota((ROAD, LANES), 0)
    tiles_ref[blocks * LANES * 8 : (blocks * LANES + 1) * 8] = jnp.zeros((8, width), F32)
    shift_ref[:, :8, :] = jnp.full((2, 8, LANES), -1.0, F32)

    def lay(num, held):
        words = words_ref.at[held]
        shifts = shift_ref.at[held]
        e = 2 * num + held
        if folded(cap):
            both = recv_ref.at[pl.ds(pl.multiple_of(num * 4 * USED, 8), 4 * USED)]
            one = both[held * 2 * USED : held * 2 * USED + USED, :]
            two = both[held * 2 * USED + USED : held * 2 * USED + 2 * USED, :]
            words[:USED] = jnp.where(lower_half, one, pltpu.roll(two, LANES // 2, 1))
            words[PART : PART + USED] = jnp.where(lower_half, pltpu.roll(one, LANES // 2, 1), two)
        else:
            words[...] = recv_ref[:, pl.ds(pl.multiple_of(e * LANES, LANES), LANES)]
        shift = words[R_FIRST : R_FIRST + 1, :] - off_ref[pl.ds(e, 1), :]
        for gap in range(GAPS):
            reached = slot_num.astype(F32) >= words[R_GAP + gap : R_GAP + gap + 1, :]
            shift = shift + jnp.where(reached, 1.0, 0.0)
        shifts[8 : 8 + ROAD] = jnp.where(slot_num < NHIT, shift, -1.0)
        laid = [jnp.zeros((NPAR, LANES), F32) for s in range(ROAD)]
        for i in range(NHIT):
            row = derivative_row(i)
            value = words[row : row + NPAR, :]
            wide = jnp.broadcast_to(shifts[8 + i : 9 + i, :], (NPAR, LANES))
            for move in range(GAPS + 1):
                laid[i + move] = jnp.where(wide == float(move), value, laid[i + move])
        placed = [jnp.zeros((ROAD, LANES), F32) for a in range(NLOC + 1)]
        for move in range(GAPS + 1):
            match = shifts[8 - move : 8 - move + ROAD, :] == float(move)
            for a in range(NLOC + 1):
                if a == NLOC:
                    row, valid = R_SOLVED - move, match
                else:
                    row = R_PROJ[a] - a - move
                    valid = jnp.logical_and(match, slot_num >= a + move) if a else match
                placed[a] = jnp.where(valid, words[row : row + ROAD, :], placed[a])
        start = pl.multiple_of(e * LANES * 8, LANES * 8)
        for a in range(NLOC + 1):
            mixed = jnp.concatenate([laid[s] * placed[a][s : s + 1] for s in range(ROAD)], axis=0)
            row = a if a < NLOC else SUM_ROW
            tiles_ref[pl.ds(start + row, LANES, stride=8), :] = mixed.T
        tiles_ref[pl.ds(start + NLOC, LANES, stride=8), :] = jnp.concatenate(laid, axis=0).T
        empty = jnp.zeros((LANES, width), F32)
        tiles_ref[pl.ds(start + SUM_ROW + 1, LANES, stride=8), :] = empty

    def lay_two(num, carry):
        lay(num, 0)
        lay(num, 1)
        return carry

    lax.fori_loop(0, blocks // 2, lay_two, 0)


def item_steps(list_ref, item_ref, tiles_ref, out_ref, held_ref):
    width = ROAD * NPAR
    row_kind = iota((PER_ITEM * 8, width), 0) % 8
    proj = jnp.where(row_kind < NLOC, 1.0, 0.0).astype(BF16)
    own = jnp.where(row_kind == NLOC, 1.0, 0.0).astype(BF16)
    same_slot = iota((width, width), 0) // NPAR == iota((width, width), 1) // NPAR
    spare = list_ref.shape[0] // PER_ITEM - 1

    def step(item_at, count, num):
        for u in range(UNROLL):
            item = num * UNROLL + u
            live = item < count
            item = jnp.where(live, item_at(item), spare)
            info = item_ref[item]
            first = (info & 1) == 1
            road = jnp.where(live, info >> 1, 0)
            at = item * PER_ITEM
            parts = [
                tiles_ref[pl.ds(pl.multiple_of(list_ref[at + j], 8), 8), :] for j in range(PER_ITEM)
            ]
            tall = jnp.concatenate(parts, axis=0)
            high, low = split_two(tall)
            left = jnp.concatenate([high, high, low], axis=0)
            high_p, low_p, high_o, low_o = high * proj, low * proj, high * own, low * own
            right = jnp.concatenate(
                [
                    jnp.concatenate([high_p, low_p, high_p], axis=0),
                    jnp.concatenate([high_o, low_o, high_o], axis=0),
                ],
                axis=1,
            )
            both = dot(left, right, 0, 0)
            value = jnp.where(same_slot, both[:, width:], 0.0) - both[:, :width]
            out_ref[road] = value + jnp.where(first, 0.0, out_ref[road])
            added = parts[0]
            for part in parts[1:]:
                added = added + part
            where = pl.ds(pl.multiple_of(road * 8, 8), 8)
            held_ref[where, :] = added + jnp.where(first, 0.0, held_ref[where, :])

    return step


def edge_kernel(
    cap, bound_ref, list_ref, item_ref, recv_ref, off_ref, off_rows_ref, prior_ref,
    tiles_ref, out_ref, sums_ref, to_next_ref, to_prev_ref, words_ref, shift_ref, held_ref,
):
    roads, width = sums_ref.shape
    edge = roads // GROUPS
    lay_tiles(cap, recv_ref, off_ref, tiles_ref, words_ref, shift_ref)
    step = item_steps(list_ref, item_ref, tiles_ref, out_ref, held_ref)
    low = bound_ref[1]
    high = bound_ref[GROUPS - 1]
    count = low + bound_ref[GROUPS] - high

    def body(num, carry):
        step(lambda item: jnp.where(item < low, item, item - low + high), count, num)
        return carry

    lax.fori_loop(0, (count + UNROLL - 1) // UNROLL, body, 0)
    for start in (0, roads - edge):
        sums_ref[start : start + edge] = held_ref[pl.ds(start * 8 + SUM_ROW, edge, stride=8), :]
    two = 2 * EDGE
    for ref, first_block, count, first_road, first_row in (
        (to_next_ref, roads - PREV_ROADS, PREV_ROADS, roads - two, prior_ref.shape[0] - EDGE),
        (to_prev_ref, 0, NEXT_ROADS, 0, 0),
    ):
        for num in range(count):
            ref[num * width : (num + 1) * width] = out_ref[first_block + num]
        at = count * width
        ref[at : at + two] = sums_ref[first_road : first_road + two]
        ref[at + two : at + 2 * two] = off_rows_ref[first_road : first_road + two]
        ref[at + 2 * two :] = prior_ref[first_row : first_row + EDGE]


def inner_kernel(
    bound_ref, list_ref, item_ref, tiles_ref, edge_ref, edge_sums_ref,
    blocks_hbm, out_ref, sums_ref, held_ref, sems,
):
    roads, width = sums_ref.shape
    edge = roads // GROUPS
    step = item_steps(list_ref, item_ref, tiles_ref, out_ref, held_ref)
    outer = [
        pltpu.make_async_copy(
            out_ref.at[pl.ds(at, edge)], blocks_hbm.at[pl.ds(at, edge)], sems.at[num]
        )
        for num, at in enumerate((0, roads - edge))
    ]
    begin, end = bound_ref[1], bound_ref[GROUPS - 1]
    done = 0
    copies = []
    pieces = (GROUPS - 2) // 2
    for piece in range(pieces):
        group = 1 + 2 * piece
        until = (bound_ref[group + 2] - begin + UNROLL - 1) // UNROLL

        def body(num, carry):
            step(lambda item: item + begin, end - begin, num)
            return carry

        lax.fori_loop(done, until, body, 0)
        done = until
        where = pl.ds(group * edge, 2 * edge)
        copies.append(
            pltpu.make_async_copy(out_ref.at[where], blocks_hbm.at[where], sems.at[2 + piece])
        )
        copies[-1].start()
    for copy in outer:
        copy.start()
    sums_ref[edge : roads - edge] = held_ref[
        pl.ds(edge * 8 + SUM_ROW, roads - 2 * edge, stride=8), :
    ]
    for copy in outer + copies:
        copy.wait()
    del edge_ref, edge_sums_ref


def gathered(rows, offset, odd):
    amount = offset * NPAR + (LANES // 2 if odd else 0)
    below = jnp.concatenate([rows[1:], jnp.zeros((1, LANES), F32)], axis=0)
    moved = jnp.where(iota(rows.shape, 1) >= amount, rows, below)
    if odd:
        moved = pltpu.roll(moved, LANES // 2, 1)
    for bit in range(3):
        turned = pltpu.roll(moved, LANES - (NPAR << bit), 1)
        moved = jnp.where((offset & (1 << bit)) != 0, turned, moved)
    return moved


def scattered(rows, offset, odd):
    amount = offset * NPAR + (LANES // 2 if odd else 0)
    moved = pltpu.roll(rows, LANES // 2, 1) if odd else rows
    for bit in range(3):
        turned = pltpu.roll(moved, NPAR << bit, 1)
        moved = jnp.where((offset & (1 << bit)) != 0, turned, moved)
    here = iota(rows.shape, 1) >= amount
    return jnp.where(here, moved, 0.0), jnp.where(here, 0.0, moved)


def krylov_kernel(
    held, sums_ref, off_ref, prior_ref, from_prev_ref, from_next_ref,
    first_ref, second_ref, dots_ref,
    even_sum, odd_sum, even_off, odd_off, prior, even_part, odd_part, held_halves, edge_halves,
):
    roads, width = sums_ref.shape
    half = roads // 2
    own = slice(EDGE, EDGE + half)
    two = 2 * EDGE
    at_prev = PREV_ROADS * width
    at_next = NEXT_ROADS * width
    for parity, total_sum, total_off in ((0, even_sum, even_off), (1, odd_sum, odd_off)):
        pick = lambda ref, start, count: ref[pl.ds(start + parity, count, stride=2), :]
        total_sum[0:EDGE] = pick(from_prev_ref, at_prev, EDGE)
        total_sum[own] = pick(sums_ref, 0, half)
        total_sum[EDGE + half :] = pick(from_next_ref, at_next, EDGE)
        total_off[0:EDGE] = pick(from_prev_ref, at_prev + two, EDGE).astype(jnp.int32)
        total_off[own] = pick(off_ref, 0, half).astype(jnp.int32)
        total_off[EDGE + half :] = pick(from_next_ref, at_next + two, EDGE).astype(jnp.int32)
    prior[0:EDGE] = from_prev_ref[at_prev + 2 * two : at_prev + 2 * two + EDGE]
    prior[own] = prior_ref[...]
    prior[EDGE + half :] = from_next_ref[at_next + 2 * two : at_next + 2 * two + EDGE]

    def spread(even, odd):
        even_here, even_there = scattered(even, even_off[...], False)
        odd_here, odd_there = scattered(odd, odd_off[...], True)
        over = even_there + odd_there
        return (
            even_here
            + odd_here
            + jnp.concatenate([jnp.zeros((1, LANES), F32), over[:-1]], axis=0)
        )

    def row_products(rows, tiles_at):
        lane_block = iota((8, 8 * width), 1) // width
        diagonal = lane_block == iota((8, 8 * width), 0)
        left = jnp.concatenate(
            [jnp.where(diagonal, jnp.concatenate([part.astype(F32)] * 8, axis=1), 0.0)
             for part in split_two(rows)],
            axis=0,
        ).astype(BF16)
        right = jnp.concatenate([tiles_at(k) for k in range(8)], axis=0)
        both = dot(left, right, 1, 0)
        both = both[:, :width] + both[:, width:]
        return both[:8] + both[8:]

    def halves(block):
        return jnp.concatenate(split_two(block), axis=1)

    edge_blocks = [(from_prev_ref, num) for num in range(PREV_ROADS)]
    edge_blocks += [(from_next_ref, num) for num in range(NEXT_ROADS)]
    edge_blocks += edge_blocks[:2]
    edge_rows = [(EDGE - PREV_ROADS // 2 + num // 2, num % 2) for num in range(PREV_ROADS)]
    edge_rows += [(EDGE + half, num) for num in range(NEXT_ROADS)]

    def apply(vector, again):
        even_part[...] = gathered(vector, even_off[...], False)
        odd_part[...] = gathered(vector, odd_off[...], True)
        outer = [(odd_part if odd else even_part)[row : row + 1, :] for row, odd in edge_rows]
        outer = jnp.concatenate(outer + [jnp.zeros((2, LANES), F32)], axis=0)

        def edge_tile(k):
            if again:
                return edge_halves[k]
            ref, num = edge_blocks[k]
            edge_halves[k] = halves(ref[num * width : (num + 1) * width, :])
            return edge_halves[k]

        outer = row_products(outer, edge_tile)
        for part, parity in ((even_part, 0), (odd_part, 1)):
            part[EDGE + half :, :] = jnp.zeros((EDGE, LANES), F32)
            part[:EDGE, :] = jnp.zeros((EDGE, LANES), F32)
        for num, (row, odd) in enumerate(edge_rows):
            (odd_part if odd else even_part)[row : row + 1, :] = outer[num : num + 1]

        def chunk(c, carry):
            for part, parity in ((even_part, 0), (odd_part, 1)):
                where = pl.ds(pl.multiple_of(EDGE + c * 8, 8), 8)

                def tile(k, parity=parity):
                    road = c * 16 + 2 * k + parity
                    if not again:
                        held_halves[road] = halves(held[road])
                    return held_halves[road]

                part[where, :] = row_products(part[where, :], tile)
            return carry

        lax.fori_loop(0, half // 8, chunk, 0, unroll=min(8, half // 8))
        return prior[...] * vector + spread(even_part[...], odd_part[...])

    first = spread(even_sum[...], odd_sum[...])
    second = apply(first, False)
    third = apply(second, True)
    first, second, third = first[own], second[own], third[own]
    first_ref[...] = first
    second_ref[...] = second
    lane = iota(dots_ref.shape, 2)
    dots = jnp.zeros(dots_ref.shape, F32)
    pairs = ((first, first), (first, second), (second, second), (second, third), (third, third))
    for num, (one, other) in enumerate(pairs):
        dots = dots + jnp.where(lane == num, jnp.sum(one * other), 0.0)
    dots_ref[...] = dots


def finish_kernel(dots_ref, first_ref, second_ref, out_hbm, out_ref, sem):
    sums = jnp.sum(dots_ref[...], axis=0, keepdims=True)
    s00, s01, s11, s12, s22 = (sums[:, num : num + 1] for num in range(5))
    square_one = s00 + EPS
    beta_one = jnp.sqrt(square_one)
    alpha_one = s01 / square_one
    square_two = (s11 - 2.0 * alpha_one * s01 + alpha_one * alpha_one * s00) / square_one + EPS
    beta_two = jnp.sqrt(square_two)
    scale = 1.0 / (beta_one * beta_two)
    s02 = s11
    cross = s12 - alpha_one * s11 - square_two * s01
    cross = cross - alpha_one * (s02 - alpha_one * s01 - square_two * s00)
    alpha_two = cross * scale * scale
    near = alpha_one + alpha_two
    far = alpha_one * alpha_two - square_two
    square_three = s22 - 2.0 * near * s12 + near * near * s11
    square_three = square_three + 2.0 * far * s02 - 2.0 * near * far * s01 + far * far * s00
    square_three = square_three * scale * scale + EPS
    entry_first = alpha_one * alpha_one + square_two
    entry_cross = beta_two * near
    entry_second = square_two + alpha_two * alpha_two + square_three
    determinant = entry_first * entry_second - entry_cross * entry_cross
    coef_one = beta_one * (entry_second * alpha_one - entry_cross * beta_two) / determinant
    coef_two = beta_one * (entry_first * beta_two - entry_cross * alpha_one) / determinant
    on_second = coef_two * scale
    on_first = coef_one / beta_one - alpha_one * on_second
    out_ref[...] = on_first * first_ref[...] + on_second * second_ref[...]
    copy = pltpu.make_async_copy(out_ref, out_hbm, sem)
    copy.start()
    copy.wait()


def neighbour(value, steps):
    count = lax.axis_size(AXES)
    return lax.ppermute(value, AXES, [(s, (s + steps) % count) for s in range(count)])


def shape(*dims, dtype=F32):
    return jax.ShapeDtypeStruct(dims, dtype)


def on_device(
    local_deriv, global_deriv, measured, hit_weight, hit_module, hit_count, track_road, road_start,
    prior_weight,
):
    devices = lax.axis_size(AXES)
    roads = road_start.shape[0]
    tracks = hit_count.shape[0]
    modules = prior_weight.shape[0]
    cap = 4 * tracks // devices
    slots = devices * cap
    width = ROAD * NPAR
    half = modules // ROAD
    vmem = pl.BlockSpec(memory_space=pltpu.VMEM)
    smem = pl.BlockSpec(memory_space=pltpu.SMEM)
    limit = pltpu.CompilerParams(vmem_limit_bytes=32 * 1024 * 1024)
    large = pltpu.CompilerParams(vmem_limit_bytes=LARGE * 1024 * 1024)
    small = pltpu.CompilerParams(vmem_limit_bytes=20 * 1024 * 1024)

    sent = (
        local_deriv, jnp.transpose(global_deriv, (1, 0, 2)), measured, hit_weight, hit_module,
        hit_count[None, :], track_road[None, :],
    )
    message = (devices * USED, LANES) if folded(cap) else (ROWS, slots)
    send = pl.pallas_call(
        functools.partial(pack_kernel, cap, roads, modules * devices),
        out_shape=shape(*message),
        in_specs=[pl.BlockSpec(memory_space=pltpu.HBM)] * len(sent),
        out_specs=vmem,
        scratch_shapes=[
            pltpu.VMEM((ROWS, tracks), F32),
            pltpu.VMEM((2 * ROWS, tracks), BF16),
            pltpu.VMEM((tracks // LANES, NHIT * 8, LANES), F32),
            pltpu.VMEM((tracks // LANES, NHIT * 8, LANES), F32),
            pltpu.VMEM((slots, tracks), BF16),
            *(pltpu.VMEM(x.shape, x.dtype) for x in sent),
            pltpu.SemaphoreType.DMA((len(sent),)),
        ],
        compiler_params=large,
        name="fit_and_pack",
    )(*sent)
    if folded(cap):
        send = send.reshape(devices, USED, 1, LANES)
    else:
        send = jnp.transpose(send.reshape(ROWS, devices, cap), (1, 0, 2))
    recv = lax.all_to_all(send, AXES, split_axis=0, concat_axis=0, tiled=True)
    if folded(cap):
        recv = recv.reshape(message)
    else:
        recv = jnp.transpose(recv, (1, 0, 2)).reshape(message)

    offset = road_start % (ROAD // 2)
    list_rows = ((PER_ITEM * roads + slots) // (8 * LANES) + 1) * 8
    item_rows = -(-(list_rows * LANES // PER_ITEM) // (8 * LANES)) * 8
    track_list, items, bounds, track_off = pl.pallas_call(
        functools.partial(sort_kernel, cap),
        out_shape=(
            shape(list_rows, LANES, dtype=jnp.int32),
            shape(item_rows, LANES, dtype=jnp.int32),
            shape(8, LANES, dtype=jnp.int32),
            shape(slots // LANES, LANES),
        ),
        in_specs=[vmem] * 2,
        out_specs=(vmem,) * 4,
        scratch_shapes=[pltpu.VMEM((slots // LANES, LANES), F32)],
        compiler_params=limit,
        name="sort_by_road",
    )(recv, offset.astype(F32)[:, None])

    edge = roads // GROUPS
    prior = prior_weight.reshape(half, width)
    off_rows = jnp.broadcast_to(offset.astype(F32)[:, None], (roads, LANES))
    lists = (bounds.reshape(-1), track_list.reshape(-1), items.reshape(-1))
    halo = 4 * EDGE + EDGE
    tiles, edge_blocks, edge_sums, to_next, to_prev = pl.pallas_call(
        functools.partial(edge_kernel, cap),
        out_shape=(
            shape((slots + 8) * 8, width), shape(roads, width, width), shape(roads, width),
            shape(PREV_ROADS * width + halo, width), shape(NEXT_ROADS * width + halo, width),
        ),
        in_specs=[smem] * 3 + [vmem] * 4,
        out_specs=(vmem,) * 5,
        scratch_shapes=[
            pltpu.VMEM((2, ROWS, LANES), F32),
            pltpu.VMEM((2, 8 + ROAD, LANES), F32),
            pltpu.VMEM((roads * 8, width), F32),
        ],
        compiler_params=small,
        name="lay_and_assemble_edges",
    )(*lists, recv, track_off, off_rows, prior)
    from_prev = neighbour(to_next, 1)
    from_next = neighbour(to_prev, -1)
    normal_blocks, held_blocks, sums = pl.pallas_call(
        inner_kernel,
        out_shape=(
            shape(roads, width, width), shape(roads, width, width), shape(roads, width),
        ),
        in_specs=[smem] * 3 + [vmem] * 3,
        out_specs=(pl.BlockSpec(memory_space=pltpu.HBM), vmem, vmem),
        scratch_shapes=[
            pltpu.VMEM((roads * 8, width), F32),
            pltpu.SemaphoreType.DMA((2 + (GROUPS - 2) // 2,)),
        ],
        input_output_aliases={4: 1, 5: 2},
        compiler_params=small,
        name="assemble_blocks",
    )(*lists, tiles, edge_blocks, edge_sums)

    total = half + 2 * EDGE
    rows = pltpu.VMEM((total, LANES), F32)
    int_rows = pltpu.VMEM((total, LANES), jnp.int32)
    halves = pltpu.VMEM((roads, width, 2 * width), BF16)
    edge_halves = pltpu.VMEM((8, width, 2 * width), BF16)
    first, second, dots = pl.pallas_call(
        krylov_kernel,
        out_shape=(shape(half, width), shape(half, width), shape(devices, 1, LANES)),
        in_specs=[vmem] * 6,
        out_specs=(vmem,) * 3,
        scratch_shapes=[
            rows, rows, int_rows, int_rows, rows, rows, rows, halves, edge_halves,
        ],
        compiler_params=small,
        name="two_products",
    )(held_blocks, sums, off_rows, prior, from_prev, from_next)
    everyone = lax.all_to_all(dots, AXES, split_axis=0, concat_axis=0, tiled=True)
    rhs = first.reshape(modules, NPAR)
    summed = (everyone.reshape(devices, LANES), rhs.T, second.reshape(modules, NPAR).T)
    corrections = pl.pallas_call(
        finish_kernel,
        out_shape=shape(NPAR, modules),
        in_specs=[vmem] * 3,
        out_specs=pl.BlockSpec(memory_space=pltpu.HBM),
        scratch_shapes=[pltpu.VMEM((NPAR, modules), F32), pltpu.SemaphoreType.DMA],
        compiler_params=pltpu.CompilerParams(vmem_limit_bytes=4 * 1024 * 1024),
        name="combine",
    )(*summed)
    return (normal_blocks, rhs, corrections.T)


def solution(mesh):
    track = P(None, None, AXES)
    in_specs = (
        track, track, P(None, AXES), P(None, AXES), P(None, AXES), P(AXES), P(AXES), P(AXES),
        P(AXES, None),
    )
    out_specs = (P(AXES, None, None), P(AXES, None), P(AXES, None))
    return jax.shard_map(
        on_device, mesh=mesh, in_specs=in_specs, out_specs=out_specs, check_vma=False
    )
```
